32 devices in a mesh: dp: 2 (over x), fsdp: 16 (over z, y, core).
Axes of the slice: x: 2, y: 2, z: 4, core: 2. Of those that a mesh axis runs over, the one named last changes fastest.
Arguments:
- hidden_in: bfloat16 [8192, 1536], P(('dp', 'fsdp')), may hold values from -6 to 6
- lengths: int32 [32], P(('dp', 'fsdp')), may hold values from 64 to 256, as said below
- cotangent: bfloat16 [8192, 1536], P(('dp', 'fsdp')), may hold values from -6 to 6
- pre_gain: float32 [1536], replicated, may hold values from 0.1 to 1.9
- in_weight: bfloat16 [1536, 6448], P(('dp', 'fsdp')), may hold values from -0.15625 to 0.15625
- conv_weight: float32 [4, 3328], replicated, may hold values from -3 to 3
- conv_bias: float32 [3328], replicated, may hold values from -3 to 3
- dt_bias: float32 [48], replicated, may hold values from -6.9 to -2.3
- a_log: float32 [48], replicated, may hold values from 0 to 2.77
- skip: float32 [48], replicated, may hold values from 0.5 to 2
- inner_gain: float32 [3072], replicated, may hold values from 0.1 to 1.9
- out_weight: bfloat16 [1536, 3072], P(('dp', 'fsdp')), may hold values from -0.109375 to 0.109375
Outputs:
- output: bfloat16 [8192, 1536], P(('dp', 'fsdp'))
- grad_hidden: bfloat16 [8192, 1536], P(('dp', 'fsdp'))
- grad_pre_gain: float32 [1536], replicated
- grad_in_weight: float32 [1536, 6448], P(('dp', 'fsdp'))
- grad_conv_weight: float32 [4, 3328], replicated
- grad_conv_bias: float32 [3328], replicated
- grad_dt_bias: float32 [48], replicated
- grad_a_log: float32 [48], replicated
- grad_skip: float32 [48], replicated
- grad_inner_gain: float32 [3072], replicated
- grad_out_weight: float32 [1536, 3072], P(('dp', 'fsdp'))
The draws below stay inside these ranges and needn't reach their ends.
Inputs may be any that keep to these rules, and one draw needn't show every extreme that they name: lengths of the slots' sequences; in every draw one slot has exactly 256 and one exactly 64.
All inputs are finite; a program needn't handle non-finite values.
Results may differ from the reference program's by a relative error of at most 0.0075.
Values may be sent and summed in bfloat16 or wider, within the bound.
No kernel may reach another device: no remote copies, remote signals or barrier semaphores. Data moves between devices by JAX's collectives and lax.ppermute only.
A program may use at most 320 MiB of HBM per device.

```python
import jax
import jax.numpy as jnp
from jax import lax

D = 1536
HEADS = 48
CONV = 4
SPAN = 256
SLOT = 256
INNER = 3072
XBC = 3328
PROJ = 6448
MIN_LEN = 64
SLOTS = 32
TOKENS = 8192


def draw_lengths(key, part):
    key = jax.random.fold_in(key, 7)
    first_key, second_key = jax.random.split(key)
    drawn = jax.random.randint(first_key, (SLOTS,), MIN_LEN, SLOT + 1)
    chosen = jax.random.randint(second_key, (), 0, SLOTS)
    places = jnp.arange(SLOTS)
    drawn = jnp.where(places == chosen, SLOT, drawn)
    drawn = jnp.where(places == (chosen + 1) % SLOTS, MIN_LEN, drawn)
    return drawn.astype(jnp.int32)


def levels(own_key, dims, cuts, least, largest):
    level, own = 1.0, jax.random.fold_in(own_key, 6)
    for position, parts in cuts:
        steps = jnp.exp(jax.random.uniform(jax.random.fold_in(own, position), (parts,), jnp.float32, least / len(cuts), largest / len(cuts)))
        level = level * jnp.repeat(steps, dims[position] // parts).reshape([-1 if axis == position else 1 for axis in range(len(dims))])
    return level


def centred(rng, shape, width, reach, shards=(), held_as=jnp.bfloat16):
    array = jax.random.normal(rng, shape, jnp.float32) * width
    if len(shards) > 0:
        array = levels(rng, shape, shards, -0.22, 0.18) * array
    return jnp.clip(array, min=-reach, max=reach).astype(held_as)


def setup_inputs(seed: int = 0) -> dict:
    splits = jax.random.split(jax.random.key(seed), 13)
    return {
        "hidden_in": centred(splits[0], (TOKENS, D), 1.0, 6.0, ((0, 32),)),
        "lengths": draw_lengths(jax.random.fold_in(splits[12], 71), 0),
        "cotangent": centred(splits[2], (TOKENS, D), 1.0, 6.0, ((0, 32),)),
        "pre_gain": jnp.clip(1.0 + 0.18 * jax.random.normal(splits[3], (D,), jnp.float32), 0.1, 1.9),
        "in_weight": centred(splits[4], (D, PROJ), D ** -0.5, 0.15625, ((0, 32),)),
        "conv_weight": centred(splits[5], (CONV, XBC), CONV ** -0.5, 3.0, (), jnp.float32),
        "conv_bias": centred(splits[6], (XBC,), 0.5, 3.0, (), jnp.float32),
        "dt_bias": jnp.clip(jax.random.uniform(splits[7], (HEADS,), jnp.float32, -6.9, -2.3), -6.9, -2.3),
        "a_log": jnp.clip(jax.random.uniform(splits[8], (HEADS,), jnp.float32, 0.0, 2.77), 0.0, 2.77),
        "skip": jnp.clip(jax.random.uniform(splits[9], (HEADS,), jnp.float32, 0.5, 2.0), 0.5, 2.0),
        "inner_gain": jnp.clip(1.0 + 0.18 * jax.random.normal(splits[10], (INNER,), jnp.float32), 0.1, 1.9),
        "out_weight": centred(splits[11], (D, INNER), INNER ** -0.5, 0.109375, ((0, 32),)),
    }


EPSILON = 1e-05
PRECISE = lax.Precision.HIGHEST

@jax.custom_vjp
def low(v):
    return lax.optimization_barrier(v.astype(jnp.bfloat16)).astype(jnp.float32)

@jax.custom_vjp
def low_back(v):
    return v

def low_keep(v):
    return (low(v), None)

def low_pass(kept, grad):
    return (grad,)

def back_keep(v):
    return (v, None)

def back_low(kept, grad):
    return (low(grad),)
low.defvjp(low_keep, low_pass)
low_back.defvjp(back_keep, back_low)

def prenorm(stream, gain):
    return stream * lax.rsqrt(lax.optimization_barrier(jnp.mean(stream * stream, axis=-1, keepdims=True)) + EPSILON) * gain

def causal_conv(conv_input, taps_weight, taps_bias):
    seq_length = conv_input.shape[0]
    kernel_taps = taps_weight.shape[0]
    padded = jnp.concatenate([jnp.zeros((kernel_taps - 1, conv_input.shape[1]), conv_input.dtype), conv_input], axis=0)
    summed = jnp.zeros_like(conv_input) + taps_bias[None, :]
    for tap in range(kernel_taps):
        summed = summed + taps_weight[tap][None, :] * padded[tap:tap + seq_length]
    return jax.nn.silu(summed)

def scan_states(values, b_rows, c_rows, step_size, decay_rate, skip):
    seq_length = values.shape[0]
    block_count = seq_length // SPAN
    head_count = values.shape[1]
    head_width = values.shape[2]
    state_width = b_rows.shape[1]
    causal = jnp.arange(SPAN)[:, None] >= jnp.arange(SPAN)[None, :]

    def step(carried_state, pieces):
        x_block, b_block, c_block, step_block = pieces
        cumulative = jnp.cumsum(step_block * decay_rate[None, :], axis=0)
        spread = jnp.where(causal[:, :, None], cumulative[:, None, :] - cumulative[None, :, :], 0.0)
        decays = jnp.where(causal[:, :, None], jnp.exp(spread), 0.0)
        scores = jnp.dot(c_block, b_block.T, precision=PRECISE)
        mixing = scores[:, :, None] * decays * step_block[None, :, :]
        within = jnp.einsum('tsh,shp->thp', mixing, x_block, precision=PRECISE)
        carried = jnp.einsum('tn,hpn->thp', c_block, carried_state, precision=PRECISE) * jnp.exp(cumulative)[:, :, None]
        tail_decay = jnp.exp(cumulative[-1][None, :] - cumulative) * step_block
        weighted = tail_decay[:, :, None] * x_block
        fresh_state = jnp.einsum('shp,sn->hpn', weighted, b_block, precision=PRECISE)
        carried_state = carried_state * jnp.exp(cumulative[-1])[:, None, None] + fresh_state
        return (carried_state, within + carried + skip[None, :, None] * x_block)
    initial = jnp.zeros((head_count, head_width, state_width), jnp.float32)
    pieces = (values.reshape(block_count, SPAN, head_count, head_width), b_rows.reshape(block_count, SPAN, state_width), c_rows.reshape(block_count, SPAN, state_width), step_size.reshape(block_count, SPAN, head_count))
    final_state, outputs = lax.scan(jax.checkpoint(step), initial, pieces)
    return outputs.reshape(seq_length, head_count * head_width)

def mixer(gate_part, conv_out, step_raw, dt_bias, a_log, skip, inner_gain):
    inner_width = gate_part.shape[1]
    head_count = step_raw.shape[1]
    state_width = (conv_out.shape[1] - inner_width) // 2
    values = conv_out[:, :inner_width].reshape(conv_out.shape[0], head_count, inner_width // head_count)
    b_rows = conv_out[:, inner_width:inner_width + state_width]
    c_rows = conv_out[:, inner_width + state_width:]
    step_size = jax.nn.softplus(step_raw + dt_bias[None, :])
    decay_rate = -jnp.exp(a_log)
    scanned = scan_states(values, b_rows, c_rows, step_size, decay_rate, skip)
    gated_out = scanned * jax.nn.silu(gate_part)
    return gated_out * lax.rsqrt(lax.optimization_barrier(jnp.mean(gated_out * gated_out, axis=-1, keepdims=True)) + EPSILON) * inner_gain

def layer(stream, valid, pre_gain, in_weight, conv_weight, conv_bias, dt_bias, a_log, skip, inner_gain, out_weight):
    normed = low(prenorm(stream, pre_gain))
    projected = low_back(jnp.dot(normed, in_weight, precision=PRECISE))
    inner_width = out_weight.shape[1]
    head_count = dt_bias.shape[0]
    gate_part = projected[:, :inner_width]
    conv_input = projected[:, inner_width:projected.shape[1] - head_count]
    step_raw = projected[:, projected.shape[1] - head_count:]
    conv_out = low(causal_conv(conv_input, conv_weight, conv_bias))
    mixed_out = low(mixer(gate_part, conv_out, step_raw, dt_bias, a_log, skip, inner_gain))
    branch = jnp.dot(mixed_out, out_weight.T, precision=PRECISE)
    return valid[:, None] * (stream + branch)

def reference(hidden_in, lengths, cotangent, pre_gain, in_weight, conv_weight, conv_bias, dt_bias, a_log, skip, inner_gain, out_weight):
    weights = (pre_gain.astype(jnp.float32), in_weight.astype(jnp.float32), conv_weight.astype(jnp.float32), conv_bias.astype(jnp.float32), dt_bias.astype(jnp.float32), a_log.astype(jnp.float32), skip.astype(jnp.float32), inner_gain.astype(jnp.float32), out_weight.astype(jnp.float32))
    streams = hidden_in.astype(jnp.float32).reshape(SLOTS, SLOT, D)
    upstreams = cotangent.astype(jnp.float32).reshape(SLOTS, SLOT, D)
    masks = (jnp.arange(SLOT).astype(jnp.int32)[None, :] < lengths[:, None]).astype(jnp.float32)

    def per_slot(totals, pieces):
        stream, upstream, valid = pieces

        def forward(stream_in, *params):
            return layer(stream_in, valid, *params)
        result, pullback = jax.vjp(forward, stream, *weights)
        gradients = pullback(upstream)
        totals = tuple((total + grad for total, grad in zip(totals, gradients[1:])))
        return (totals, (result.astype(jnp.bfloat16), gradients[0].astype(jnp.bfloat16)))
    initial_sums = tuple((jnp.zeros_like(weight) for weight in weights))
    sums, (outputs, grads_in) = lax.scan(per_slot, initial_sums, (streams, upstreams, masks))
    return (outputs.reshape(TOKENS, D), grads_in.reshape(TOKENS, D), sums[0], sums[1], sums[2], sums[3], sums[4], sums[5], sums[6], sums[7], sums[8])
```

```python
import functools

import jax
import jax.numpy as jnp
from jax import lax
from jax.experimental import pallas as pl
from jax.experimental.pallas import tpu as pltpu
from jax.sharding import Mesh
from jax.sharding import PartitionSpec as P

EPSILON = 1e-05
PRECISE = lax.Precision.HIGHEST
LANES = 128
LOW = jnp.bfloat16

PLANE = ("xi", "yi", "c")
LINE = ("xo", "zo")
EVERY = ("xo", "xi", "zo", "yi", "c")


def swap(value):
    return lax.ppermute(value, "c", [(0, 1), (1, 0)])


def cross(value, axes, distance, count):
    return lax.ppermute(value, axes, [(i, i ^ distance) for i in range(count)])


def shift_down(value, rows):
    if rows == 0:
        return value
    index = lax.broadcasted_iota(jnp.int32, value.shape, 0)
    return jnp.where(index >= rows, pltpu.roll(value, rows, 0), 0.0)


def shift_up(value, rows):
    if rows == 0:
        return value
    length = value.shape[0]
    index = lax.broadcasted_iota(jnp.int32, value.shape, 0)
    return jnp.where(index < length - rows, pltpu.roll(value, length - rows, 0), 0.0)


def softplus(value):
    return jnp.maximum(value, 0.0) + jnp.log1p(jnp.exp(-jnp.abs(value)))


def dot_f32(left, right):
    return jnp.dot(left, right, precision=PRECISE, preferred_element_type=jnp.float32)


def dot_low(left, right):
    return jnp.dot(left, right, preferred_element_type=jnp.float32)


def dot_nt(left, right):
    return lax.dot_general(left, right, (((1,), (1,)), ((), ())), preferred_element_type=jnp.float32)


def convolve(conv_input, taps, bias):
    kernel_taps = taps.shape[0]
    summed = bias
    for tap in range(kernel_taps):
        summed = summed + taps[tap : tap + 1] * shift_down(conv_input, kernel_taps - 1 - tap)
    return summed


def triangle(length, lower):
    row = lax.broadcasted_iota(jnp.int32, (length, length), 0)
    column = lax.broadcasted_iota(jnp.int32, (length, length), 1)
    return row >= column if lower else row <= column


def head_lanes(step, head_count, inner):
    head = lax.broadcasted_iota(jnp.int32, (LANES, inner), 0)
    lane = lax.broadcasted_iota(jnp.int32, (LANES, inner), 1)
    spread = (lane // (inner // head_count) == head).astype(jnp.float32)
    return dot_f32(step, spread)


def lanes_sum(value, head_count):
    inner = value.shape[1]
    lane = lax.broadcasted_iota(jnp.int32, (inner, LANES), 0)
    head = lax.broadcasted_iota(jnp.int32, (inner, LANES), 1)
    return dot_f32(value, (lane // (inner // head_count) == head).astype(jnp.float32))


def scan_forward(heads, part_ref, taps_ref, bias_ref, dt_ref, alog_ref, skip_ref, out_ref):
    inner = out_ref.shape[1]
    length = out_ref.shape[0]
    width = taps_ref.shape[1]
    states = (width - inner) // 2
    conv_low = jax.nn.silu(convolve(part_ref[:, :width], taps_ref[...], bias_ref[...])).astype(LOW)
    step = softplus(part_ref[:, width:] + dt_ref[...])
    lower = triangle(length, True)
    cumulative = dot_f32(lower.astype(jnp.float32), step * -jnp.exp(alog_ref[...]))
    across = cumulative.T
    scores = dot_nt(conv_low[:, inner + states :], conv_low[:, inner : inner + states])
    scores = jnp.where(lower, scores, 0.0)
    values = conv_low[:, :inner].astype(jnp.float32)
    scaled = (values * head_lanes(step, heads, inner)).astype(LOW)
    first = lax.broadcasted_iota(jnp.int32, (length, LANES), 1) < inner // heads
    for pair in range(heads // 2):
        lanes = slice(pair * LANES, (pair + 1) * LANES)
        sums = []
        for head in (2 * pair, 2 * pair + 1):
            spread = cumulative[:, head : head + 1] - across[head : head + 1, :]
            mixing = scores * jnp.exp(jnp.where(lower, spread, 0.0))
            sums.append(dot_low(mixing.astype(LOW), scaled[:, lanes]))
        out_ref[:, lanes] = jnp.where(first, sums[0], sums[1]) + skip_ref[:, lanes] * values[:, lanes]


def scan_backward(
    heads,
    part_ref,
    grad_ref,
    scanned_ref,
    taps_ref,
    bias_ref,
    dt_ref,
    alog_ref,
    skip_ref,
    out_ref,
    small_ref,
):
    inner = grad_ref.shape[1]
    length = grad_ref.shape[0]
    width = taps_ref.shape[1]
    states = (width - inner) // 2
    kernel_taps = taps_ref.shape[0]
    conv_input = part_ref[:, :width]
    summed = convolve(conv_input, taps_ref[...], bias_ref[...])
    gate = jax.nn.sigmoid(summed)
    conv_low = (summed * gate).astype(LOW)
    slope = gate * (1.0 + summed * (1.0 - gate))
    raw = part_ref[:, width:] + dt_ref[...]
    step = softplus(raw)
    decay = -jnp.exp(alog_ref[...])
    lower = triangle(length, True)
    cumulative = dot_f32(lower.astype(jnp.float32), step * decay)
    across = cumulative.T
    b_rows = conv_low[:, inner : inner + states]
    c_rows = conv_low[:, inner + states :]
    scores = jnp.where(lower, dot_nt(c_rows, b_rows), 0.0)
    values = conv_low[:, :inner].astype(jnp.float32)
    steps = head_lanes(step, heads, inner)
    scaled = (values * steps).astype(LOW)
    grad = grad_ref[...]
    grad_low = grad.astype(LOW)
    grad_across = grad.T.astype(LOW)
    half = inner // heads
    first = lax.broadcasted_iota(jnp.int32, (length, LANES), 1) < half
    upper_rows = lax.broadcasted_iota(jnp.int32, (LANES, length), 0) < half
    grad_scores = jnp.zeros((length, length), jnp.float32)
    moved = []
    for pair in range(heads // 2):
        lanes = slice(pair * LANES, (pair + 1) * LANES)
        sums = []
        for head in (2 * pair, 2 * pair + 1):
            spread = cumulative[:, head : head + 1] - across[head : head + 1, :]
            decays = jnp.where(lower, jnp.exp(jnp.where(lower, spread, 0.0)), 0.0)
            mixing = (scores * decays).astype(LOW)
            own = first if head % 2 == 0 else jnp.logical_not(first)
            grad_own = jnp.where(own, grad[:, lanes], 0.0).astype(LOW)
            grad_scores = grad_scores + dot_nt(grad_own, scaled[:, lanes]) * decays
            sums.append(dot_low(grad_across[lanes], mixing))
        moved.append(jnp.where(upper_rows, sums[0], sums[1]).T)
    grad_scaled = jnp.concatenate(moved, axis=1)
    within = scanned_ref[...] - skip_ref[...] * values
    grad_cumulative = lanes_sum(
        grad_low.astype(jnp.float32) * within - scaled.astype(jnp.float32) * grad_scaled, heads
    )
    grad_rate = dot_f32(triangle(length, False).astype(jnp.float32), grad_cumulative)
    grad_step = grad_rate * decay + lanes_sum(values * grad_scaled, heads)
    grad_raw = grad_step * jax.nn.sigmoid(raw)
    grad_values = steps * grad_scaled + skip_ref[...] * grad
    scores_low = grad_scores.astype(LOW)
    grad_c = dot_low(scores_low, b_rows)
    grad_b = dot_low(c_rows.T, scores_low).T
    grad_summed = jnp.concatenate([grad_values, grad_b, grad_c], axis=1) * slope
    grad_input = jnp.zeros_like(grad_summed)
    rows = []
    for tap in range(kernel_taps):
        away = kernel_taps - 1 - tap
        grad_input = grad_input + taps_ref[tap : tap + 1, :] * shift_up(grad_summed, away)
        rows.append(jnp.sum(grad_summed * shift_down(conv_input, away), axis=0, keepdims=True))
    rows.append(jnp.sum(grad_summed, axis=0, keepdims=True))
    out_ref[:, :width] = grad_input.astype(LOW)
    out_ref[:, width:] = grad_raw.astype(LOW)

    @pl.when(pl.program_id(0) == 0)
    def _():
        small_ref[...] = jnp.zeros_like(small_ref)

    for index, row in enumerate(rows):
        small_ref[index : index + 1, :width] += row
    small_ref[5:6, :inner] += jnp.sum(grad * values, axis=0, keepdims=True)
    small_ref[5:6, width:] += jnp.sum(grad_raw, axis=0, keepdims=True)
    small_ref[6:7, width:] += jnp.sum(grad_rate * step, axis=0, keepdims=True) * decay


def row_block(length, width):
    return pl.BlockSpec((length, width), lambda slot: (slot, 0))


def whole_block(array):
    return pl.BlockSpec(array.shape, lambda slot: (0,) * array.ndim)


def run_forward(slots, heads, part, taps, bias, dt_row, alog_row, skip_row):
    length = part.shape[0] // slots
    inner = skip_row.shape[1]
    weights = (taps, bias, dt_row, alog_row, skip_row)
    return pl.pallas_call(
        functools.partial(scan_forward, heads),
        grid=(slots,),
        in_specs=[row_block(length, part.shape[1])] + [whole_block(w) for w in weights],
        out_specs=row_block(length, inner),
        out_shape=jax.ShapeDtypeStruct((part.shape[0], inner), jnp.float32),
        compiler_params=pltpu.CompilerParams(vmem_limit_bytes=32 << 20),
    )(part, *weights)


def run_backward(slots, heads, part, grad, scanned, taps, bias, dt_row, alog_row, skip_row):
    length = part.shape[0] // slots
    weights = (taps, bias, dt_row, alog_row, skip_row)
    return pl.pallas_call(
        functools.partial(scan_backward, heads),
        grid=(slots,),
        in_specs=[
            row_block(length, part.shape[1]),
            row_block(length, grad.shape[1]),
            row_block(length, grad.shape[1]),
        ]
        + [whole_block(w) for w in weights],
        out_specs=[
            row_block(length, part.shape[1]),
            pl.BlockSpec((8, part.shape[1]), lambda slot: (0, 0)),
        ],
        out_shape=[
            jax.ShapeDtypeStruct(part.shape, LOW),
            jax.ShapeDtypeStruct((8, part.shape[1]), jnp.float32),
        ],
        compiler_params=pltpu.CompilerParams(vmem_limit_bytes=32 << 20),
    )(part, grad, scanned, *weights)


def body(
    sizes,
    hidden_in,
    lengths,
    cotangent,
    pre_gain,
    in_weight,
    conv_weight,
    conv_bias,
    dt_bias,
    a_log,
    skip,
    inner_gain,
    out_weight,
):
    length, model = hidden_in.shape
    rows = in_weight.shape[0]
    inner_all = out_weight.shape[1]
    heads_all = dt_bias.shape[0]
    states = (conv_weight.shape[1] - inner_all) // 2
    ranks = sizes["xi"] * sizes["yi"] * sizes["c"]
    lines = sizes["xo"] * sizes["zo"]
    inner = inner_all // ranks
    heads = heads_all // ranks
    head_width = inner // heads
    core = lax.axis_index("c")
    rank = (lax.axis_index("xi") * sizes["yi"] + lax.axis_index("yi")) * sizes["c"] + core
    place = lax.axis_index("xo") * sizes["zo"] + lax.axis_index("zo")
    by_plane = (sizes["xo"], sizes["xi"], sizes["zo"], sizes["yi"] * sizes["c"] * rows)
    from_plane = (sizes["xo"], sizes["zo"], sizes["xi"], sizes["yi"] * sizes["c"] * rows)

    def to_lines(value):
        return value.reshape(-1, *by_plane).transpose(0, 1, 3, 2, 4).reshape(-1, model)

    def from_lines(value):
        return value.reshape(-1, *from_plane).transpose(0, 1, 3, 2, 4).reshape(-1, model)

    def gather_rows(piece):
        if lines != 4:
            return lax.all_gather(piece, LINE, axis=0, tiled=True)
        pieces = [piece] + [cross(piece, LINE, away, lines) for away in range(1, lines)]
        whole = jnp.zeros((lines * piece.shape[0], piece.shape[1]), piece.dtype)
        for away, part in enumerate(pieces):
            whole = lax.dynamic_update_slice(whole, part, ((place ^ away) * piece.shape[0], 0))
        return whole

    def scatter_rows(whole):
        count = whole.shape[0] // lines
        if lines != 4:
            moved = lax.all_to_all(whole.astype(LOW), LINE, split_axis=0, concat_axis=0, tiled=True)
            return jnp.sum(moved.reshape(lines, count, -1).astype(jnp.float32), axis=0)

        def part(away):
            return lax.dynamic_slice(whole, ((place ^ away) * count, 0), (count, whole.shape[1]))

        total = part(0).astype(jnp.float32)
        for away in (2, 3, 1):
            total = total + cross(part(away).astype(LOW), LINE, away, lines).astype(jnp.float32)
        return total

    def exchange(value):
        return lax.all_to_all(value, PLANE, split_axis=0, concat_axis=0, tiled=True)

    def gather_tokens(value):
        near = [value] + [cross(value, ("xi", "yi"), away, 4) for away in range(1, 4)]
        return jnp.concatenate(near + [swap(block) for block in near], axis=0)

    def scatter_tokens(value):
        half = value.shape[0] // 2
        total = value[:half].astype(jnp.float32) + swap(value[half:].astype(LOW)).astype(jnp.float32)
        total = total.reshape(4, length, -1)
        own = total[0]
        for away in range(1, 4):
            own = own + cross(total[away].astype(LOW), ("xi", "yi"), away, 4).astype(jnp.float32)
        return own

    def by_rank(columns):
        return columns.reshape(rows, ranks, -1).transpose(1, 0, 2)

    first_conv = inner_all
    first_state = 2 * inner_all
    first_step = first_state + 2 * states
    state_columns = in_weight[:, first_state:first_step].reshape(rows, 2, states).transpose(1, 0, 2)
    packed_conv = jnp.concatenate(
        [
            by_rank(in_weight[:, first_conv:first_state]),
            jnp.tile(state_columns, (ranks // 2, 1, 1)),
            jnp.pad(by_rank(in_weight[:, first_step:]), ((0, 0), (0, 0), (0, LANES - heads))),
        ],
        axis=2,
    )
    packed_gate = by_rank(in_weight[:, :inner_all])
    packed_out = by_rank(out_weight)
    plane_rows = ranks * rows
    conv_columns = gather_rows(exchange(packed_conv).reshape(plane_rows, -1))
    gate_columns = gather_rows(exchange(packed_gate).reshape(plane_rows, -1))
    out_columns = gather_rows(exchange(packed_out).reshape(plane_rows, -1))
    own_states = conv_columns[:, inner : inner + states]
    other_states = swap(own_states)
    conv_columns = jnp.concatenate(
        [
            conv_columns[:, :inner],
            jnp.where(core == 0, own_states, other_states),
            jnp.where(core == 0, other_states, own_states),
            conv_columns[:, inner + states :],
        ],
        axis=1,
    )

    stream = hidden_in.astype(jnp.float32)
    scale = lax.rsqrt(jnp.mean(stream * stream, axis=-1, keepdims=True) + EPSILON)
    valid = (jnp.arange(length) < lengths[0])[:, None]
    own_upstream = jnp.where(valid, cotangent, jnp.zeros_like(cotangent))
    normed = gather_tokens(to_lines((stream * scale * pre_gain).astype(LOW)))
    upstream = gather_tokens(to_lines(own_upstream))
    slots = normed.shape[0] // length

    def of_rank(value, count):
        return lax.dynamic_slice_in_dim(value, rank * count, count, axis=-1)

    taps = jnp.concatenate(
        [of_rank(conv_weight[:, :inner_all], inner), conv_weight[:, inner_all:]], axis=1
    )
    bias = jnp.concatenate([of_rank(conv_bias[:inner_all], inner), conv_bias[inner_all:]])[None]
    dt_row = jnp.pad(of_rank(dt_bias, heads), (0, LANES - heads))[None]
    alog_row = jnp.pad(of_rank(a_log, heads), (0, LANES - heads))[None]
    skip_row = jnp.repeat(of_rank(skip, heads), head_width)[None]
    gain_row = of_rank(inner_gain, inner)[None]

    conv_part = dot_low(normed, conv_columns)
    scanned = run_forward(slots, heads, conv_part, taps, bias, dt_row, alog_row, skip_row)
    gate_part = dot_low(normed, gate_columns)
    gate_sigmoid = jax.nn.sigmoid(gate_part)
    gate_silu = gate_part * gate_sigmoid
    gated = scanned * gate_silu
    gained_low = (gated * gain_row).astype(LOW)
    branch = dot_nt(gained_low, out_columns)
    grad_mixed = dot_low(upstream, out_columns)
    grad_gained = grad_mixed * gain_row
    stats = jnp.stack([jnp.sum(gated * gated, axis=1), jnp.sum(grad_gained * gated, axis=1)])
    stats = stats.reshape(2, 2, 4, length)
    stats = stats + swap(stats[:, ::-1])
    stats = stats.reshape(2, 2, 2, 2, length)
    far = [
        cross(jnp.flip(stats, axes), ("xi", "yi"), away, 4)
        for axes, away in (((2, 3), 3), ((3,), 1), ((2,), 2))
    ]
    stats = ((stats + far[0]) + (far[1] + far[2])).reshape(2, -1)
    inner_scale = lax.rsqrt(stats[0] / inner_all + EPSILON)[:, None]
    slope = inner_scale**3 * stats[1][:, None] / inner_all
    branch_own = scatter_tokens(branch.astype(LOW))
    branch_own = from_lines(branch_own * inner_scale[:length])
    output = jnp.where(valid, stream + branch_own, 0.0).astype(LOW)

    mixed_low = (gated * inner_scale * gain_row).astype(LOW)
    grad_out_columns = lax.dot_general(
        upstream, mixed_low, (((0,), (0,)), ((), ())), preferred_element_type=jnp.float32
    )
    grad_inner_gain = jnp.sum(grad_mixed * gated * inner_scale, axis=0)
    grad_gated = grad_gained * inner_scale - gated * slope
    grad_gate = (grad_gated * scanned * (gate_sigmoid * (1.0 + gate_part * (1.0 - gate_sigmoid)))).astype(LOW)
    grad_scanned = grad_gated * gate_silu
    grad_gate_columns = lax.dot_general(
        normed, grad_gate, (((0,), (0,)), ((), ())), preferred_element_type=jnp.float32
    )
    grad_conv, small = run_backward(
        slots, heads, conv_part, grad_scanned, scanned, taps, bias, dt_row, alog_row, skip_row
    )
    grad_conv_columns = lax.dot_general(
        normed, grad_conv, (((0,), (0,)), ((), ())), preferred_element_type=jnp.float32
    )
    grad_normed = dot_nt(grad_gate, gate_columns) + dot_nt(grad_conv, conv_columns)
    gain_lines = to_lines(pre_gain[None])
    grad_pre_gain = jnp.sum(grad_normed * normed.astype(jnp.float32), axis=0, keepdims=True) / gain_lines
    grad_pre_gain = from_lines(grad_pre_gain)[0]
    grad_own = from_lines(scatter_tokens(grad_normed.astype(LOW))) * pre_gain
    along = jnp.mean(grad_own * stream, axis=-1, keepdims=True)
    grad_stream = grad_own * scale - stream * (scale**3 * along)
    grad_hidden = (own_upstream.astype(jnp.float32) + grad_stream).astype(LOW)

    def to_owners(value):
        return exchange(value.astype(LOW).reshape(ranks, rows, -1)).astype(jnp.float32)

    grad_b = grad_conv_columns[:, inner : inner + states]
    grad_c = grad_conv_columns[:, inner + states : inner + 2 * states]
    kept = jnp.where(core == 0, grad_b, grad_c)
    given = jnp.where(core == 0, grad_c, grad_b)
    kept = kept + swap(given.astype(LOW)).astype(jnp.float32)
    conv_back = jnp.concatenate(
        [grad_conv_columns[:, :inner], kept, grad_conv_columns[:, inner + 2 * states :]], axis=1
    )
    owned_out = to_owners(scatter_rows(grad_out_columns)).transpose(1, 0, 2).reshape(rows, inner_all)
    owned_gate = to_owners(scatter_rows(grad_gate_columns)).transpose(1, 0, 2).reshape(rows, inner_all)
    owned_conv = to_owners(scatter_rows(conv_back))
    owned_states = jnp.sum(
        owned_conv[:, :, inner : inner + states].reshape(ranks // 2, 2, rows, states), axis=0
    )
    owned_in = jnp.concatenate(
        [
            owned_gate,
            owned_conv[:, :, :inner].transpose(1, 0, 2).reshape(rows, inner_all),
            owned_states.transpose(1, 0, 2).reshape(rows, 2 * states),
            owned_conv[:, :, inner + states : inner + states + heads].transpose(1, 0, 2).reshape(rows, heads_all),
        ],
        axis=1,
    )

    def place_rank(value, total):
        blank = jnp.zeros(value.shape[:-1] + (total,), jnp.float32)
        return lax.dynamic_update_slice_in_dim(blank, value, rank * value.shape[-1], axis=-1)

    taps_count = conv_weight.shape[0]
    width = taps.shape[1]
    conv_small = small[: taps_count + 1, :width]
    conv_small = jnp.concatenate(
        [place_rank(conv_small[:, :inner], inner_all), conv_small[:, inner:]], axis=1
    )
    head_small = jnp.stack(
        [
            small[5, width : width + heads],
            small[6, width : width + heads],
            jnp.sum(small[5, :inner].reshape(heads, head_width), axis=1),
        ]
    )
    head_small = jnp.pad(place_rank(head_small, heads_all), ((0, 0), (0, LANES - heads_all)))
    pieces = (grad_pre_gain, conv_small, place_rank(grad_inner_gain, inner_all), head_small)
    flat = jnp.concatenate([piece.reshape(-1, LANES) for piece in pieces], axis=0)
    flat = flat + swap(flat)
    far = [cross(flat, ("xi", "yi"), away, 4) for away in (3, 1, 2)]
    flat = (flat + far[0]) + (far[1] + far[2])
    if lines == 4:
        far = [cross(flat, LINE, away, 4) for away in (3, 1, 2)]
        flat = (flat + far[0]) + (far[1] + far[2])
    else:
        flat = lax.psum(flat, LINE)
    sums = []
    start = 0
    for piece in pieces:
        count = piece.size // LANES
        sums.append(flat[start : start + count].reshape(piece.shape))
        start += count
    return (
        output,
        grad_hidden,
        sums[0],
        owned_in,
        sums[1][:taps_count],
        sums[1][taps_count],
        sums[3][0, :heads_all],
        sums[3][1, :heads_all],
        sums[3][2, :heads_all],
        sums[2],
        owned_out,
    )


def solution(mesh):
    dp, fsdp = mesh.shape["dp"], mesh.shape["fsdp"]
    shape = (dp // 2, 2, fsdp // 4, 2, 2)
    fine = Mesh(mesh.devices.reshape(shape), EVERY)
    split, kept = P(EVERY, None), P()
    in_specs = (split, P(EVERY), split, kept, split, kept, kept, kept, kept, kept, kept, split)
    out_specs = (split, split, kept, split, kept, kept, kept, kept, kept, kept, split)
    return jax.shard_map(
        functools.partial(body, dict(zip(EVERY, shape))),
        mesh=fine,
        in_specs=in_specs,
        out_specs=out_specs,
        check_vma=False,
    )
```

```python
import functools

import jax
import jax.numpy as jnp
from jax import lax
from jax.experimental import pallas as pl
from jax.experimental.pallas import tpu as pltpu
from jax.sharding import Mesh
from jax.sharding import PartitionSpec as P

EPSILON = 1e-05
LANES = 128
LOW = jnp.bfloat16

PLANE = ("xi", "yi", "c")
LINE = ("xo", "zo")
EVERY = ("xo", "xi", "zo", "yi", "c")


def swap(value):
    return lax.ppermute(value, "c", [(0, 1), (1, 0)])


def cross(value, axes, distance, count):
    return lax.ppermute(value, axes, [(i, i ^ distance) for i in range(count)])


def shift_down(value, rows):
    if rows == 0:
        return value
    index = lax.broadcasted_iota(jnp.int32, value.shape, 0)
    return jnp.where(index >= rows, pltpu.roll(value, rows, 0), 0.0)


def shift_up(value, rows):
    if rows == 0:
        return value
    length = value.shape[0]
    index = lax.broadcasted_iota(jnp.int32, value.shape, 0)
    return jnp.where(index < length - rows, pltpu.roll(value, length - rows, 0), 0.0)


def softplus(value):
    return jnp.maximum(value, 0.0) + jnp.log1p(jnp.exp(-jnp.abs(value)))


def dot_low(left, right):
    return jnp.dot(left, right, preferred_element_type=jnp.float32)


def dot_nt(left, right):
    return lax.dot_general(left, right, (((1,), (1,)), ((), ())), preferred_element_type=jnp.float32)


def dot_tn(left, right):
    return lax.dot_general(left, right, (((0,), (0,)), ((), ())), preferred_element_type=jnp.float32)


def parts_of(value, count):
    terms = []
    for _ in range(count):
        terms.append(value.astype(LOW))
        value = value - terms[-1].astype(jnp.float32)
    return terms


def convolve(conv_input, taps, bias):
    kernel_taps = taps.shape[0]
    summed = bias
    for tap in range(kernel_taps):
        summed = summed + taps[tap : tap + 1] * shift_down(conv_input, kernel_taps - 1 - tap)
    return summed


def triangle(length, lower):
    row = lax.broadcasted_iota(jnp.int32, (length, length), 0)
    column = lax.broadcasted_iota(jnp.int32, (length, length), 1)
    return row >= column if lower else row <= column


def cumulate(mask, value, count):
    mask = mask.astype(LOW)
    return sum(dot_low(mask, term) for term in parts_of(value, count))


def pair_lanes(value, pair, first):
    return jnp.where(first, value[:, 2 * pair : 2 * pair + 1], value[:, 2 * pair + 1 : 2 * pair + 2])


def lanes_sum(value, head_count):
    inner = value.shape[1]
    lane = lax.broadcasted_iota(jnp.int32, (inner, LANES), 0)
    head = lax.broadcasted_iota(jnp.int32, (inner, LANES), 1)
    member = (lane // (inner // head_count) == head).astype(LOW)
    return sum(dot_low(term, member) for term in parts_of(value, 2))


def read(ref):
    if not isinstance(ref, tuple):
        return ref[...]
    near, far = ref
    return jnp.where(pl.program_id(0) < pl.num_programs(0) // 2, near[...], far[...])


def row_spread(row):
    return jnp.broadcast_to(row, (8, row.shape[1])).T[:, :1]


def scan_forward(heads, part, taps_ref, bias_ref, dt_ref, alog_ref, skip_ref, out_ref):
    inner = out_ref.shape[1]
    length = out_ref.shape[0]
    width = taps_ref.shape[1]
    states = (width - inner) // 2
    conv_low = jax.nn.silu(convolve(part[:, :width], taps_ref[...], bias_ref[...])).astype(LOW)
    step = softplus(part[:, width:] + dt_ref[...])
    lower = triangle(length, True)
    cumulative = cumulate(lower, step * -jnp.exp(alog_ref[...]), 3)
    across = cumulative.T
    scores = dot_nt(conv_low[:, inner + states :], conv_low[:, inner : inner + states])
    scores = jnp.where(lower, scores, 0.0)
    first = lax.broadcasted_iota(jnp.int32, (length, LANES), 1) < inner // heads
    for pair in range(heads // 2):
        lanes = slice(pair * LANES, (pair + 1) * LANES)
        values = conv_low[:, lanes].astype(jnp.float32)
        scaled = (values * pair_lanes(step, pair, first)).astype(LOW)
        sums = []
        for head in (2 * pair, 2 * pair + 1):
            spread = cumulative[:, head : head + 1] - across[head : head + 1, :]
            mixing = scores * jnp.exp(jnp.where(lower, spread, 0.0))
            sums.append(dot_low(mixing.astype(LOW), scaled))
        out_ref[:, lanes] = jnp.where(first, sums[0], sums[1]) + skip_ref[:, lanes] * values


def norm_kernel(hidden_ref, gain_ref, *refs):
    stream = hidden_ref[...].astype(jnp.float32)
    scale = lax.rsqrt(jnp.mean(stream * stream, axis=-1, keepdims=True) + EPSILON)
    refs[-1][...] = (stream * scale * gain_ref[...]).astype(LOW)


def mask_kernel(lengths_ref, cotangent_ref, *refs):
    row = lax.broadcasted_iota(jnp.int32, cotangent_ref.shape, 0)
    own = cotangent_ref[...].astype(jnp.float32)
    refs[-1][...] = jnp.where(row < lengths_ref[0], own, 0.0).astype(LOW)


def copy_kernel(value_ref, *refs):
    refs[-1][...] = value_ref[...]


def conv_kernel(
    heads,
    place_ref,
    normed_ref,
    piece_0,
    piece_1,
    piece_2,
    piece_3,
    other_ref,
    taps_ref,
    bias_ref,
    dt_ref,
    alog_ref,
    skip_ref,
    part_ref,
    scanned_ref,
    weight_ref,
):
    inner = scanned_ref.shape[1]
    states = other_ref.shape[1]
    chunk = piece_0.shape[0] // 2

    @pl.when(pl.program_id(0) == 0)
    def _():
        core = place_ref[8]
        for away, piece in enumerate((piece_0, piece_1, piece_2, piece_3)):
            for half in range(2):
                rows = pl.ds(pl.multiple_of(place_ref[2 * away + half], 16), chunk)
                local = slice(half * chunk, (half + 1) * chunk)
                own = piece[local, inner : inner + states]
                other = other_ref[(2 * away + half) * chunk : (2 * away + half + 1) * chunk, :]
                weight_ref[rows, :inner] = piece[local, :inner]
                weight_ref[rows, inner : inner + states] = jnp.where(core == 0, own, other)
                weight_ref[rows, inner + states : inner + 2 * states] = jnp.where(core == 0, other, own)
                weight_ref[rows, inner + 2 * states :] = piece[local, inner + states :]

    part = dot_low(read(normed_ref), weight_ref[...])
    part_ref[...] = part
    scan_forward(heads, part, taps_ref, bias_ref, dt_ref, alog_ref, skip_ref, scanned_ref)


def scan_backward(
    heads,
    part_ref,
    grad_ref,
    scanned_ref,
    taps_ref,
    bias_ref,
    dt_ref,
    alog_ref,
    skip_ref,
    out_ref,
    small_ref,
):
    inner = grad_ref.shape[1]
    length = grad_ref.shape[0]
    width = taps_ref.shape[1]
    states = (width - inner) // 2
    kernel_taps = taps_ref.shape[0]
    conv_input = part_ref[:, :width]
    summed = convolve(conv_input, taps_ref[...], bias_ref[...])
    gate = jax.nn.sigmoid(summed)
    conv_low = (summed * gate).astype(LOW)
    slope = gate * (1.0 + summed * (1.0 - gate))
    raw = part_ref[:, width:] + dt_ref[...]
    step = softplus(raw)
    decay = -jnp.exp(alog_ref[...])
    lower = triangle(length, True)
    cumulative = cumulate(lower, step * decay, 3)
    across = cumulative.T
    b_rows = conv_low[:, inner : inner + states]
    c_rows = conv_low[:, inner + states :]
    scores = jnp.where(lower, dot_nt(c_rows, b_rows), 0.0)
    values = conv_low[:, :inner].astype(jnp.float32)
    half = inner // heads
    first = lax.broadcasted_iota(jnp.int32, (length, LANES), 1) < half
    steps = jnp.concatenate([pair_lanes(step, pair, first) for pair in range(heads // 2)], axis=1)
    scaled = (values * steps).astype(LOW)
    grad = grad_ref[...]
    grad_low = grad.astype(LOW)
    grad_across = grad.T.astype(LOW)
    upper_rows = lax.broadcasted_iota(jnp.int32, (LANES, length), 0) < half
    grad_scores = jnp.zeros((length, length), jnp.float32)
    moved = []
    for pair in range(heads // 2):
        lanes = slice(pair * LANES, (pair + 1) * LANES)
        sums = []
        for head in (2 * pair, 2 * pair + 1):
            spread = cumulative[:, head : head + 1] - across[head : head + 1, :]
            decays = jnp.where(lower, jnp.exp(jnp.where(lower, spread, 0.0)), 0.0)
            mixing = (scores * decays).astype(LOW)
            own = first if head % 2 == 0 else jnp.logical_not(first)
            grad_own = jnp.where(own, grad[:, lanes], 0.0).astype(LOW)
            grad_scores = grad_scores + dot_nt(grad_own, scaled[:, lanes]) * decays
            sums.append(dot_low(grad_across[lanes], mixing))
        moved.append(jnp.where(upper_rows, sums[0], sums[1]).T)
    grad_scaled = jnp.concatenate(moved, axis=1)
    within = scanned_ref[...] - skip_ref[...] * values
    grad_cumulative = lanes_sum(
        grad_low.astype(jnp.float32) * within - scaled.astype(jnp.float32) * grad_scaled, heads
    )
    grad_rate = cumulate(triangle(length, False), grad_cumulative, 3)
    grad_step = grad_rate * decay + lanes_sum(values * grad_scaled, heads)
    grad_raw = grad_step * jax.nn.sigmoid(raw)
    grad_values = steps * grad_scaled + skip_ref[...] * grad
    scores_low = grad_scores.astype(LOW)
    grad_c = dot_low(scores_low, b_rows)
    grad_b = dot_low(c_rows.T, scores_low).T
    grad_summed = jnp.concatenate([grad_values, grad_b, grad_c], axis=1) * slope
    grad_input = jnp.zeros_like(grad_summed)
    rows = []
    for tap in range(kernel_taps):
        away = kernel_taps - 1 - tap
        grad_input = grad_input + taps_ref[tap : tap + 1, :] * shift_up(grad_summed, away)
        rows.append(jnp.sum(grad_summed * shift_down(conv_input, away), axis=0, keepdims=True))
    rows.append(jnp.sum(grad_summed, axis=0, keepdims=True))
    out_ref[:, :width] = grad_input.astype(LOW)
    out_ref[:, width:] = grad_raw.astype(LOW)

    for index, row in enumerate(rows):
        small_ref[index : index + 1, :width] += row
    small_ref[5:6, :inner] += jnp.sum(grad * values, axis=0, keepdims=True)
    small_ref[5:6, width:] += jnp.sum(grad_raw, axis=0, keepdims=True)
    small_ref[6:7, width:] += jnp.sum(grad_rate * step, axis=0, keepdims=True) * decay


def gate_kernel(
    place_ref,
    normed_ref,
    upstream_ref,
    scanned_ref,
    piece_0,
    piece_1,
    piece_2,
    piece_3,
    gain_ref,
    gate_ref,
    mixed_ref,
    gained_ref,
    stats_ref,
    gate_weight,
    out_weight,
):
    inner = gain_ref.shape[1]
    length = gate_ref.shape[0]
    chunk = piece_0.shape[0] // 2
    slot = pl.program_id(0)

    @pl.when(slot == 0)
    def _():
        for away, piece in enumerate((piece_0, piece_1, piece_2, piece_3)):
            for half in range(2):
                rows = pl.ds(pl.multiple_of(place_ref[2 * away + half], 16), chunk)
                local = slice(half * chunk, (half + 1) * chunk)
                gate_weight[rows, :] = piece[local, :inner]
                out_weight[rows, :] = piece[local, inner:]

    gate = dot_low(read(normed_ref), gate_weight[...])
    gated = scanned_ref[...] * jax.nn.silu(gate)
    gained = gated * gain_ref[...]
    grad_mixed = dot_low(read(upstream_ref), out_weight[...])
    gate_ref[...] = gate
    mixed_ref[...] = grad_mixed
    gained_ref[...] = gained.astype(LOW)
    squares = jnp.sum(gated * gated, axis=1, keepdims=True)
    products = jnp.sum(grad_mixed * gained, axis=1, keepdims=True)
    lane = lax.broadcasted_iota(jnp.int32, (length, LANES), 1)
    turned = jnp.where(lane == 0, squares, products).T
    stats_ref[pl.ds(slot, 1), :] = turned[0:1]
    stats_ref[pl.ds(pl.num_programs(0) + slot, 1), :] = turned[1:2]


def branch_kernel(place_ref, gained_ref, weight_ref, out_ref):
    out_ref[...] = dot_nt(gained_ref[...], weight_ref[...]).astype(LOW)


def early_kernel(
    inner_all,
    place_ref,
    normed_ref,
    upstream_ref,
    scanned_ref,
    gate_ref,
    mixed_ref,
    stats_ref,
    gain_ref,
    grad_gate_ref,
    grad_scanned_ref,
    gain_grad_ref,
    piece_0,
    piece_1,
    piece_2,
    piece_3,
    sums_ref,
):
    slot = pl.program_id(0)
    inner = gain_ref.shape[1]
    chunk = piece_0.shape[0] // 2
    count = pl.num_programs(0)
    scale = lax.rsqrt(stats_ref[pl.ds(slot, 1), :] / inner_all + EPSILON)
    slope = scale * scale * scale * stats_ref[pl.ds(count + slot, 1), :] / inner_all
    scale, slope = row_spread(scale), row_spread(slope)
    gate = gate_ref[...]
    scanned = scanned_ref[...]
    sigmoid = jax.nn.sigmoid(gate)
    silu = gate * sigmoid
    gated = scanned * silu
    scaled = gated * scale
    mixed_low = (scaled * gain_ref[...]).astype(LOW)
    grad_mixed = mixed_ref[...]
    grad_gated = grad_mixed * gain_ref[...] * scale - gated * slope
    grad_gate = (grad_gated * scanned * (sigmoid * (1.0 + gate * (1.0 - sigmoid)))).astype(LOW)
    grad_gate_ref[...] = grad_gate
    grad_scanned_ref[...] = grad_gated * silu

    @pl.when(slot == 0)
    def _():
        sums_ref[...] = jnp.zeros_like(sums_ref)
        gain_grad_ref[...] = jnp.zeros_like(gain_grad_ref)

    gain_grad_ref[0:1, :] += jnp.sum(grad_mixed * scaled, axis=0, keepdims=True)
    sums_ref[:, :inner] += dot_tn(read(normed_ref), grad_gate)
    sums_ref[:, inner:] += dot_tn(read(upstream_ref), mixed_low)

    @pl.when(slot == count - 1)
    def _():
        for away, piece in enumerate((piece_0, piece_1, piece_2, piece_3)):
            for half in range(2):
                rows = pl.ds(pl.multiple_of(place_ref[2 * away + half], 16), chunk)
                piece[half * chunk : (half + 1) * chunk, :] = sums_ref[rows, :].astype(LOW)


def back_kernel(
    heads,
    place_ref,
    part_ref,
    grad_ref,
    scanned_ref,
    grad_gate_ref,
    normed_ref,
    weight_ref,
    gate_weight,
    taps_ref,
    bias_ref,
    dt_ref,
    alog_ref,
    skip_ref,
    normed_grad_ref,
    small_ref,
    pre_ref,
    given_ref,
    piece_0,
    piece_1,
    piece_2,
    piece_3,
    sums_ref,
    conv_ref,
):
    slot = pl.program_id(0)
    inner = grad_ref.shape[1]
    width = taps_ref.shape[1]
    states = (width - inner) // 2
    chunk = piece_0.shape[0] // 2

    @pl.when(slot == 0)
    def _():
        small_ref[...] = jnp.zeros_like(small_ref)
        pre_ref[...] = jnp.zeros_like(pre_ref)
        sums_ref[...] = jnp.zeros_like(sums_ref)

    scan_backward(
        heads,
        part_ref,
        grad_ref,
        scanned_ref,
        taps_ref,
        bias_ref,
        dt_ref,
        alog_ref,
        skip_ref,
        conv_ref,
        small_ref,
    )
    normed = read(normed_ref)
    grad_conv = conv_ref[...]
    sums_ref[...] += dot_tn(normed, grad_conv)
    grad_normed = dot_nt(grad_gate_ref[...], gate_weight[...]) + dot_nt(grad_conv, weight_ref[...])
    pre_ref[0:1, :] += jnp.sum(grad_normed * normed.astype(jnp.float32), axis=0, keepdims=True)

    normed_grad_ref[...] = grad_normed.astype(LOW)

    @pl.when(slot == pl.num_programs(0) - 1)
    def _():
        core = place_ref[8]
        for away, piece in enumerate((piece_0, piece_1, piece_2, piece_3)):
            for half in range(2):
                rows = pl.ds(pl.multiple_of(place_ref[2 * away + half], 16), chunk)
                local = slice(half * chunk, (half + 1) * chunk)
                whole = slice((2 * away + half) * chunk, (2 * away + half + 1) * chunk)
                b_sums = sums_ref[rows, inner : inner + states].astype(LOW)
                c_sums = sums_ref[rows, inner + states : width].astype(LOW)
                given_ref[whole, :] = jnp.where(core == 0, c_sums, b_sums)
                piece[local, :inner] = sums_ref[rows, :inner].astype(LOW)
                piece[local, inner : inner + states] = jnp.where(core == 0, b_sums, c_sums)
                piece[local, inner + states :] = sums_ref[rows, width:].astype(LOW)


def row_block(length, width):
    return pl.BlockSpec((length, width), lambda slot, place: (slot, 0))


def core_block(length, width, half):
    def index(slot, place):
        return (2 * (slot % half) + (place[8] ^ (slot // half)), 0)

    return pl.BlockSpec((length, width), index)


def near_block(length, width, half):
    return pl.BlockSpec((length, width), lambda slot, place: (jnp.minimum(slot, half - 1), 0))


def far_block(length, width, half):
    return pl.BlockSpec((length, width), lambda slot, place: (jnp.maximum(slot - half, 0), 0))


def whole_block(shape):
    return pl.BlockSpec(shape, lambda slot, place: (0,) * len(shape))


def run_slots(kernel, slots, place, cut, whole, outs, scratch, micros, waits=(), block=row_block):
    in_specs, arrays, places = [], [], []
    for array in cut:
        places.append(len(arrays))
        if isinstance(array, tuple):
            length = 2 * array[0].shape[0] // slots
            in_specs.append(near_block(length, array[0].shape[1], slots // 2))
            in_specs.append(far_block(length, array[1].shape[1], slots // 2))
            arrays.extend(array)
        else:
            in_specs.append(block(array.shape[0] // slots, array.shape[1]))
            arrays.append(array)
    in_specs += [whole_block(array.shape) for array in whole]
    arrays += whole
    given = len(arrays)

    def run(place_ref, *refs):
        cut_refs = [
            (refs[at], refs[at + 1]) if isinstance(array, tuple) else refs[at]
            for at, array in zip(places, cut)
        ]
        kernel(place_ref, *cut_refs, *refs[given - len(whole) : given], *refs[given + len(waits) :])

    return pl.pallas_call(
        run,
        grid_spec=pltpu.PrefetchScalarGridSpec(
            num_scalar_prefetch=1,
            grid=(slots,),
            in_specs=in_specs + [pl.BlockSpec(memory_space=pl.ANY)] * len(waits),
            out_specs=[spec for _, _, spec in outs],
            scratch_shapes=scratch,
        ),
        out_shape=[jax.ShapeDtypeStruct(shape, dtype) for shape, dtype, _ in outs],
        compiler_params=pltpu.CompilerParams(vmem_limit_bytes=44 << 20),
        cost_estimate=pl.CostEstimate(flops=int(micros * 1e9), bytes_accessed=1 << 20, transcendentals=0),
    )(place, *arrays, *waits)


def copies(kernel, scalars, value, others, count, waits=()):
    shape = value.shape
    return pl.pallas_call(
        kernel,
        grid_spec=pltpu.PrefetchScalarGridSpec(
            num_scalar_prefetch=len(scalars),
            grid=(count,),
            in_specs=[pl.BlockSpec(array.shape, lambda *_: (0, 0)) for array in (value, *others)]
            + [pl.BlockSpec(memory_space=pl.ANY)] * len(waits),
            out_specs=pl.BlockSpec(shape, lambda index, *_: (index, 0)),
        ),
        out_shape=jax.ShapeDtypeStruct((count * shape[0], shape[1]), LOW),
        compiler_params=pltpu.CompilerParams(vmem_limit_bytes=16 << 20),
        cost_estimate=pl.CostEstimate(flops=int(2e9), bytes_accessed=1 << 20, transcendentals=0),
    )(*scalars, value, *others, *waits)


def combine(terms, dtype, waits=()):
    shape = terms[0].shape
    steps = max(1, shape[0] // 384)

    def run(*refs):
        values = [ref[...].astype(jnp.float32) for ref in refs[: len(terms)]]
        if len(values) == 4:
            values = [values[0] + values[1], values[2] + values[3]]
        refs[-1][...] = sum(values[1:], values[0]).astype(dtype)

    block = pl.BlockSpec((shape[0] // steps, shape[1]), lambda index: (index, 0))
    return pl.pallas_call(
        run,
        grid=(steps,),
        in_specs=[block] * len(terms) + [pl.BlockSpec(memory_space=pl.ANY)] * len(waits),
        out_specs=block,
        out_shape=jax.ShapeDtypeStruct(shape, dtype),
        cost_estimate=pl.CostEstimate(flops=int(1e9), bytes_accessed=1 << 20, transcendentals=0),
    )(*terms, *waits)


def hold(values, waits):
    anywhere = pl.BlockSpec(memory_space=pl.ANY)
    return pl.pallas_call(
        lambda *refs: None,
        in_specs=[anywhere] * (len(values) + len(waits)),
        out_specs=[anywhere] * len(values),
        out_shape=[jax.ShapeDtypeStruct(value.shape, value.dtype) for value in values],
        input_output_aliases={index: index for index in range(len(values))},
    )(*values, *waits)


def add_states(pieces, states, start):
    rows, width = states.shape[0] // len(pieces), states.shape[1]
    count = len(pieces)

    def run(*refs):
        for index in range(count):
            own = refs[index][...].astype(jnp.float32)
            other = refs[count][index * rows : (index + 1) * rows, :].astype(jnp.float32)
            refs[count + 1 + index][...] = (own + other).astype(LOW)

    block = pl.BlockSpec((rows, width), lambda _: (0, start // width))
    return pl.pallas_call(
        run,
        grid=(1,),
        in_specs=[block] * count + [pl.BlockSpec(states.shape, lambda _: (0, 0))],
        out_specs=[block] * count,
        out_shape=[jax.ShapeDtypeStruct(piece.shape, piece.dtype) for piece in pieces],
        input_output_aliases={index: index for index in range(count)},
        cost_estimate=pl.CostEstimate(flops=int(1e9), bytes_accessed=1 << 20, transcendentals=0),
    )(*pieces, states)


def columns_of(value, start, width, waits):
    return pl.pallas_call(
        copy_kernel,
        grid=(1,),
        in_specs=[
            pl.BlockSpec((value.shape[0], LANES * (width // LANES)), lambda _: (0, start // width))
        ]
        + [pl.BlockSpec(memory_space=pl.ANY)] * len(waits),
        out_specs=pl.BlockSpec((value.shape[0], width), lambda _: (0, 0)),
        out_shape=jax.ShapeDtypeStruct((value.shape[0], width), LOW),
        cost_estimate=pl.CostEstimate(flops=int(1e9), bytes_accessed=1 << 20, transcendentals=0),
    )(value, *waits)


def body(
    sizes,
    hidden_in,
    lengths,
    cotangent,
    pre_gain,
    in_weight,
    conv_weight,
    conv_bias,
    dt_bias,
    a_log,
    skip,
    inner_gain,
    out_weight,
):
    length, model = hidden_in.shape
    rows = in_weight.shape[0]
    inner_all = out_weight.shape[1]
    heads_all = dt_bias.shape[0]
    states = (conv_weight.shape[1] - inner_all) // 2
    ranks = sizes["xi"] * sizes["yi"] * sizes["c"]
    lines = sizes["xo"] * sizes["zo"]
    slots = ranks
    tokens = slots * length
    inner = inner_all // ranks
    heads = heads_all // ranks
    head_width = inner // heads
    core = lax.axis_index("c")
    rank = (lax.axis_index("xi") * sizes["yi"] + lax.axis_index("yi")) * sizes["c"] + core
    direct = sizes["xo"] == 1 and sizes["zo"] == 4
    piece_rows = model // 4
    chunk = piece_rows // 2
    spread = (sizes["xo"], sizes["zo"], sizes["xi"], sizes["yi"] * sizes["c"] * rows)
    natural = (sizes["xo"], sizes["xi"], sizes["zo"], sizes["yi"] * sizes["c"] * rows)
    if direct:
        planes = [lax.axis_index("zo") ^ away for away in range(4)]
        starts = [half * (model // 2) + plane * chunk for plane in planes for half in range(2)]
    else:
        starts = [chunk * index for index in range(8)]
    place = jnp.stack([jnp.asarray(value, jnp.int32) for value in (*starts, core)])

    def gather_rows(piece):
        if direct:
            return [piece] + [cross(piece, LINE, away, 4) for away in range(1, 4)]
        whole = lax.all_gather(piece, LINE, axis=0, tiled=True).reshape(*spread, -1)
        whole = whole.transpose(0, 2, 1, 3, 4).reshape(model, -1)
        return [whole[index * piece_rows : (index + 1) * piece_rows] for index in range(4)]

    def scatter_rows(pieces, waits=()):
        if direct:
            moved = [cross(pieces[away], LINE, away, 4) for away in (2, 3, 1)]
            return combine([pieces[0], *moved], LOW, waits)
        whole = jnp.concatenate(pieces, axis=0).reshape(*natural, -1)
        whole = whole.transpose(0, 2, 1, 3, 4).reshape(model, -1)
        moved = lax.all_to_all(whole, LINE, split_axis=0, concat_axis=0, tiled=True)
        return jnp.sum(moved.reshape(lines, model // lines, -1).astype(jnp.float32), axis=0).astype(LOW)

    def exchange(value):
        return lax.all_to_all(value, PLANE, split_axis=0, concat_axis=0, tiled=True)

    def gather_tokens(value):
        return lax.all_gather(value, PLANE, axis=0, tiled=True)

    def scatter_far(value):
        return lax.psum_scatter(value, PLANE, scatter_dimension=0, tiled=True)

    def by_rank(columns):
        return columns.reshape(rows, ranks, -1).transpose(1, 0, 2)

    first_state = 2 * inner_all
    first_step = first_state + 2 * states
    state_columns = in_weight[:, first_state:first_step].reshape(rows, 2, states).transpose(1, 0, 2)
    packed = jnp.concatenate(
        [
            by_rank(in_weight[:, :inner_all]),
            by_rank(out_weight),
            by_rank(in_weight[:, inner_all:first_state]),
            jnp.tile(state_columns, (ranks // 2, 1, 1)),
            jnp.pad(by_rank(in_weight[:, first_step:]), ((0, 0), (0, 0), (0, LANES - heads))),
        ],
        axis=2,
    )
    plane_weights = exchange(packed).reshape(ranks * rows, -1)
    conv_pieces = gather_rows(plane_weights[:, 2 * inner :])
    other_states = swap(jnp.concatenate([piece[:, inner : inner + states] for piece in conv_pieces], axis=0))
    late_pieces = gather_rows(columns_of(plane_weights, 0, 2 * inner, conv_pieces[1:]))

    stream = hidden_in.astype(jnp.float32)
    scale = lax.rsqrt(jnp.mean(stream * stream, axis=-1, keepdims=True) + EPSILON)
    valid = (jnp.arange(length) < lengths[0])[:, None]
    own_upstream = jnp.where(valid, cotangent, jnp.zeros_like(cotangent))
    own_normed = copies(norm_kernel, (), hidden_in, (pre_gain[None],), 1)
    normed = gather_tokens(own_normed)
    upstream = gather_tokens(copies(mask_kernel, (lengths,), cotangent, (), 1, (own_normed,)))

    def of_rank(value, count):
        return lax.dynamic_slice_in_dim(value, rank * count, count, axis=-1)

    taps = jnp.concatenate(
        [of_rank(conv_weight[:, :inner_all], inner), conv_weight[:, inner_all:]], axis=1
    )
    bias = jnp.concatenate([of_rank(conv_bias[:inner_all], inner), conv_bias[inner_all:]])[None]
    dt_row = jnp.pad(of_rank(dt_bias, heads), (0, LANES - heads))[None]
    alog_row = jnp.pad(of_rank(a_log, heads), (0, LANES - heads))[None]
    skip_row = jnp.repeat(of_rank(skip, heads), head_width)[None]
    gain_row = of_rank(inner_gain, inner)[None]
    params = (taps, bias, dt_row, alog_row, skip_row)
    part_width = inner + 2 * states + LANES

    part, scanned, conv_weights = run_slots(
        functools.partial(conv_kernel, heads),
        slots,
        place,
        (normed,),
        (*conv_pieces, other_states, *params),
        [
            ((tokens, part_width), jnp.float32, row_block(length, part_width)),
            ((tokens, inner), jnp.float32, row_block(length, inner)),
            ((model, part_width), LOW, whole_block((model, part_width))),
        ],
        [],
        12,
    )
    gate, grad_mixed, gained, stats, gate_weights, out_weights = run_slots(
        gate_kernel,
        slots,
        place,
        (normed, upstream, scanned),
        (*late_pieces, gain_row),
        [
            ((tokens, inner), jnp.float32, row_block(length, inner)),
            ((tokens, inner), jnp.float32, row_block(length, inner)),
            ((tokens, inner), LOW, row_block(length, inner)),
            ((2 * slots, length), jnp.float32, whole_block((2 * slots, length))),
            ((model, inner), LOW, whole_block((model, inner))),
            ((model, inner), LOW, whole_block((model, inner))),
        ],
        [],
        8,
    )
    stats = stats + swap(stats)
    far = [cross(stats, ("xi", "yi"), away, 4) for away in (3, 1, 2)]
    stats = (stats + far[0]) + (far[1] + far[2])
    (branch,) = run_slots(
        branch_kernel,
        slots,
        place,
        (gained,),
        (out_weights,),
        [((tokens, model), LOW, row_block(length, model))],
        [],
        5,
    )
    branch_own = scatter_far(branch)
    squares = lax.dynamic_index_in_dim(stats, rank, axis=0, keepdims=False)
    inner_scale = lax.rsqrt(squares / inner_all + EPSILON)[:, None]
    output = jnp.where(valid, stream + branch_own * inner_scale, 0.0).astype(LOW)

    piece_shape = (piece_rows, 2 * inner)
    grad_gate, grad_scanned, gain_grad, *early = run_slots(
        functools.partial(early_kernel, inner_all),
        slots,
        place,
        (normed, upstream, scanned, gate, grad_mixed),
        (stats, gain_row),
        [
            ((tokens, inner), LOW, row_block(length, inner)),
            ((tokens, inner), jnp.float32, row_block(length, inner)),
            ((8, inner), jnp.float32, whole_block((8, inner))),
        ]
        + [(piece_shape, LOW, whole_block(piece_shape))] * 4,
        [pltpu.VMEM((model, 2 * inner), jnp.float32)],
        16,
        (branch,),
    )
    piece_shape = (piece_rows, inner + states + LANES)
    held = run_slots(
        functools.partial(back_kernel, heads),
        slots,
        place,
        (part, grad_scanned, scanned, grad_gate, normed),
        (conv_weights, gate_weights, *params),
        [
            ((tokens, model), LOW, row_block(length, model)),
            ((8, part_width), jnp.float32, whole_block((8, part_width))),
            ((8, model), jnp.float32, whole_block((8, model))),
            ((model, states), LOW, whole_block((model, states))),
        ]
        + [(piece_shape, LOW, whole_block(piece_shape))] * 4,
        [pltpu.VMEM((model, part_width), jnp.float32), pltpu.VMEM((length, part_width), LOW)],
        40,
    )
    if direct:
        early_moved = [cross(early[away], LINE, away, 4) for away in (2, 3, 1)]
        held = hold(held, [*early_moved, branch_own])
    grad_normed, small, pre_grad, given, *pieces = held
    pieces = add_states(pieces, swap(given), inner)
    grad_own = scatter_far(grad_normed) * pre_gain
    along = jnp.mean(grad_own * stream, axis=-1, keepdims=True)
    grad_stream = grad_own * scale - stream * (scale**3 * along)
    grad_hidden = (own_upstream.astype(jnp.float32) + grad_stream).astype(LOW)

    def to_owners(value):
        return exchange(value.astype(LOW).reshape(ranks, rows, -1)).astype(jnp.float32)

    def all_columns(value):
        return value.transpose(1, 0, 2).reshape(rows, -1)

    early_sum = combine([early[0], *early_moved], LOW) if direct else scatter_rows(early)
    owned_early = to_owners(early_sum)
    conv_sum = scatter_rows(pieces)
    owned_conv = to_owners(conv_sum)
    owned_states = owned_conv[:, :, inner : inner + states].reshape(ranks // 2, 2, rows, states)
    owned_in = jnp.concatenate(
        [
            all_columns(owned_early[:, :, :inner]),
            all_columns(owned_conv[:, :, :inner]),
            all_columns(jnp.sum(owned_states, axis=0)),
            all_columns(owned_conv[:, :, inner + states : inner + states + heads]),
        ],
        axis=1,
    )
    owned_out = all_columns(owned_early[:, :, inner:])

    def place_rank(value, total):
        blank = jnp.zeros(value.shape[:-1] + (total,), jnp.float32)
        return lax.dynamic_update_slice_in_dim(blank, value, rank * value.shape[-1], axis=-1)

    taps_count = conv_weight.shape[0]
    width = taps.shape[1]
    conv_small = small[: taps_count + 1, :width]
    conv_small = jnp.concatenate(
        [place_rank(conv_small[:, :inner], inner_all), conv_small[:, inner:]], axis=1
    )
    head_small = jnp.stack(
        [
            small[5, width : width + heads],
            small[6, width : width + heads],
            jnp.sum(small[5, :inner].reshape(heads, head_width), axis=1),
        ]
    )
    head_small = jnp.pad(place_rank(head_small, heads_all), ((0, 0), (0, LANES - heads_all)))
    grads = (pre_grad[0] / pre_gain, conv_small, place_rank(gain_grad[0], inner_all), head_small)
    flat = jnp.concatenate([grad.reshape(-1, LANES) for grad in grads], axis=0)
    flat = combine([flat, swap(flat)], jnp.float32, (early_sum,))
    flat = combine([flat, *(cross(flat, ("xi", "yi"), away, 4) for away in (3, 1, 2))], jnp.float32, (conv_sum,))
    if direct:
        flat = combine([flat, *(cross(flat, LINE, away, 4) for away in (3, 1, 2))], jnp.float32)
    else:
        flat = lax.psum(flat, LINE)
    sums = []
    start = 0
    for grad in grads:
        count = grad.size // LANES
        sums.append(flat[start : start + count].reshape(grad.shape))
        start += count
    return (
        output,
        grad_hidden,
        sums[0],
        owned_in,
        sums[1][:taps_count],
        sums[1][taps_count],
        sums[3][0, :heads_all],
        sums[3][1, :heads_all],
        sums[3][2, :heads_all],
        sums[2],
        owned_out,
    )


def solution(mesh):
    dp, fsdp = mesh.shape["dp"], mesh.shape["fsdp"]
    shape = (dp // 2, 2, fsdp // 4, 2, 2)
    fine = Mesh(mesh.devices.reshape(shape), EVERY)
    split, kept = P(EVERY, None), P()
    in_specs = (split, P(EVERY), split, kept, split, kept, kept, kept, kept, kept, kept, split)
    out_specs = (split, split, kept, split, kept, kept, kept, kept, kept, kept, split)
    return jax.shard_map(
        functools.partial(body, dict(zip(EVERY, shape))),
        mesh=fine,
        in_specs=in_specs,
        out_specs=out_specs,
        check_vma=False,
    )
```

```python
import functools

import jax
import jax.numpy as jnp
from jax import lax
from jax.experimental import pallas as pl
from jax.experimental.pallas import tpu as pltpu
from jax.sharding import Mesh
from jax.sharding import PartitionSpec as P

EPSILON = 1e-05
LANES = 128
LOW = jnp.bfloat16

PLANE = ("xi", "yi", "c")
LINE = ("xo", "zo")
EVERY = ("xo", "xi", "zo", "yi", "c")


def swap(value):
    return lax.ppermute(value, "c", [(0, 1), (1, 0)])


def cross(value, axes, distance, count):
    return lax.ppermute(value, axes, [(i, i ^ distance) for i in range(count)])


def shift_down(value, rows):
    if rows == 0:
        return value
    index = lax.broadcasted_iota(jnp.int32, value.shape, 0)
    return jnp.where(index >= rows, pltpu.roll(value, rows, 0), 0.0)


def shift_up(value, rows):
    if rows == 0:
        return value
    length = value.shape[0]
    index = lax.broadcasted_iota(jnp.int32, value.shape, 0)
    return jnp.where(index < length - rows, pltpu.roll(value, length - rows, 0), 0.0)


def softplus(value):
    return jnp.maximum(value, 0.0) + jnp.log1p(jnp.exp(-jnp.abs(value)))


def dot_low(left, right):
    return jnp.dot(left, right, preferred_element_type=jnp.float32)


def dot_nt(left, right):
    return lax.dot_general(left, right, (((1,), (1,)), ((), ())), preferred_element_type=jnp.float32)


def dot_tn(left, right):
    return lax.dot_general(left, right, (((0,), (0,)), ((), ())), preferred_element_type=jnp.float32)


def parts_of(value, count):
    terms = []
    for _ in range(count):
        terms.append(value.astype(LOW))
        value = value - terms[-1].astype(jnp.float32)
    return terms


def convolve(conv_input, taps, bias):
    kernel_taps = taps.shape[0]
    summed = bias
    for tap in range(kernel_taps):
        summed = summed + taps[tap : tap + 1] * shift_down(conv_input, kernel_taps - 1 - tap)
    return summed


def triangle(length, lower):
    row = lax.broadcasted_iota(jnp.int32, (length, length), 0)
    column = lax.broadcasted_iota(jnp.int32, (length, length), 1)
    return row >= column if lower else row <= column


def cumulate(mask, value, count):
    mask = mask.astype(LOW)
    return sum(dot_low(mask, term) for term in parts_of(value, count))


def pair_lanes(value, pair, first):
    return jnp.where(first, value[:, 2 * pair : 2 * pair + 1], value[:, 2 * pair + 1 : 2 * pair + 2])


def lanes_sum(value, head_count):
    inner = value.shape[1]
    lane = lax.broadcasted_iota(jnp.int32, (inner, LANES), 0)
    head = lax.broadcasted_iota(jnp.int32, (inner, LANES), 1)
    member = (lane // (inner // head_count) == head).astype(LOW)
    return sum(dot_low(term, member) for term in parts_of(value, 2))


def read(ref):
    if not isinstance(ref, tuple):
        return ref[...]
    near, far = ref
    return jnp.where(pl.program_id(0) < pl.num_programs(0) // 2, near[...], far[...])


def row_spread(row):
    return jnp.broadcast_to(row, (8, row.shape[1])).T[:, :1]


def scan_forward(heads, part, taps_ref, bias_ref, dt_ref, alog_ref, skip_ref, out_ref):
    inner = out_ref.shape[1]
    length = out_ref.shape[0]
    width = taps_ref.shape[1]
    states = (width - inner) // 2
    conv_low = jax.nn.silu(convolve(part[:, :width], taps_ref[...], bias_ref[...])).astype(LOW)
    step = softplus(part[:, width:] + dt_ref[...])
    lower = triangle(length, True)
    cumulative = cumulate(lower, step * -jnp.exp(alog_ref[...]), 3)
    across = cumulative.T
    scores = dot_nt(conv_low[:, inner + states :], conv_low[:, inner : inner + states])
    scores = jnp.where(lower, scores, 0.0)
    first = lax.broadcasted_iota(jnp.int32, (length, LANES), 1) < inner // heads
    for pair in range(heads // 2):
        lanes = slice(pair * LANES, (pair + 1) * LANES)
        values = conv_low[:, lanes].astype(jnp.float32)
        scaled = (values * pair_lanes(step, pair, first)).astype(LOW)
        sums = []
        for head in (2 * pair, 2 * pair + 1):
            spread = cumulative[:, head : head + 1] - across[head : head + 1, :]
            mixing = scores * jnp.exp(jnp.where(lower, spread, 0.0))
            sums.append(dot_low(mixing.astype(LOW), scaled))
        out_ref[:, lanes] = jnp.where(first, sums[0], sums[1]) + skip_ref[:, lanes] * values


def norm_kernel(hidden_ref, gain_ref, *refs):
    stream = hidden_ref[...].astype(jnp.float32)
    scale = lax.rsqrt(jnp.mean(stream * stream, axis=-1, keepdims=True) + EPSILON)
    refs[-1][...] = (stream * scale * gain_ref[...]).astype(LOW)


def mask_kernel(lengths_ref, cotangent_ref, *refs):
    row = lax.broadcasted_iota(jnp.int32, cotangent_ref.shape, 0)
    own = cotangent_ref[...].astype(jnp.float32)
    refs[-1][...] = jnp.where(row < lengths_ref[0], own, 0.0).astype(LOW)


def copy_kernel(value_ref, *refs):
    refs[-1][...] = value_ref[...]


def conv_kernel(
    heads,
    place_ref,
    normed_ref,
    piece_0,
    piece_1,
    piece_2,
    piece_3,
    other_ref,
    taps_ref,
    bias_ref,
    dt_ref,
    alog_ref,
    skip_ref,
    part_ref,
    scanned_ref,
    weight_ref,
):
    inner = scanned_ref.shape[1]
    states = other_ref.shape[1]
    chunk = piece_0.shape[0] // 2

    @pl.when(pl.program_id(0) == 0)
    def _():
        core = place_ref[8]
        for away, piece in enumerate((piece_0, piece_1, piece_2, piece_3)):
            for half in range(2):
                rows = pl.ds(pl.multiple_of(place_ref[2 * away + half], 16), chunk)
                local = slice(half * chunk, (half + 1) * chunk)
                own = piece[local, inner : inner + states]
                other = other_ref[(2 * away + half) * chunk : (2 * away + half + 1) * chunk, :]
                weight_ref[rows, :inner] = piece[local, :inner]
                weight_ref[rows, inner : inner + states] = jnp.where(core == 0, own, other)
                weight_ref[rows, inner + states : inner + 2 * states] = jnp.where(core == 0, other, own)
                weight_ref[rows, inner + 2 * states :] = piece[local, inner + states :]

    part = dot_low(read(normed_ref), weight_ref[...])
    part_ref[...] = part
    scan_forward(heads, part, taps_ref, bias_ref, dt_ref, alog_ref, skip_ref, scanned_ref)


def scan_backward(
    heads,
    part_ref,
    grad_ref,
    scanned_ref,
    taps_ref,
    bias_ref,
    dt_ref,
    alog_ref,
    skip_ref,
    out_ref,
    small_ref,
):
    inner = grad_ref.shape[1]
    length = grad_ref.shape[0]
    width = taps_ref.shape[1]
    states = (width - inner) // 2
    kernel_taps = taps_ref.shape[0]
    conv_input = part_ref[:, :width]
    summed = convolve(conv_input, taps_ref[...], bias_ref[...])
    gate = jax.nn.sigmoid(summed)
    conv_low = (summed * gate).astype(LOW)
    slope = gate * (1.0 + summed * (1.0 - gate))
    raw = part_ref[:, width:] + dt_ref[...]
    step = softplus(raw)
    decay = -jnp.exp(alog_ref[...])
    lower = triangle(length, True)
    cumulative = cumulate(lower, step * decay, 3)
    across = cumulative.T
    b_rows = conv_low[:, inner : inner + states]
    c_rows = conv_low[:, inner + states :]
    scores = jnp.where(lower, dot_nt(c_rows, b_rows), 0.0)
    values = conv_low[:, :inner].astype(jnp.float32)
    half = inner // heads
    first = lax.broadcasted_iota(jnp.int32, (length, LANES), 1) < half
    steps = jnp.concatenate([pair_lanes(step, pair, first) for pair in range(heads // 2)], axis=1)
    scaled = (values * steps).astype(LOW)
    grad = grad_ref[...]
    grad_low = grad.astype(LOW)
    grad_across = grad.T.astype(LOW)
    upper_rows = lax.broadcasted_iota(jnp.int32, (LANES, length), 0) < half
    grad_scores = jnp.zeros((length, length), jnp.float32)
    moved = []
    for pair in range(heads // 2):
        lanes = slice(pair * LANES, (pair + 1) * LANES)
        sums = []
        for head in (2 * pair, 2 * pair + 1):
            spread = cumulative[:, head : head + 1] - across[head : head + 1, :]
            decays = jnp.where(lower, jnp.exp(jnp.where(lower, spread, 0.0)), 0.0)
            mixing = (scores * decays).astype(LOW)
            own = first if head % 2 == 0 else jnp.logical_not(first)
            grad_own = jnp.where(own, grad[:, lanes], 0.0).astype(LOW)
            grad_scores = grad_scores + dot_nt(grad_own, scaled[:, lanes]) * decays
            sums.append(dot_low(grad_across[lanes], mixing))
        moved.append(jnp.where(upper_rows, sums[0], sums[1]).T)
    grad_scaled = jnp.concatenate(moved, axis=1)
    within = scanned_ref[...] - skip_ref[...] * values
    grad_cumulative = lanes_sum(
        grad_low.astype(jnp.float32) * within - scaled.astype(jnp.float32) * grad_scaled, heads
    )
    grad_rate = cumulate(triangle(length, False), grad_cumulative, 3)
    grad_step = grad_rate * decay + lanes_sum(values * grad_scaled, heads)
    grad_raw = grad_step * jax.nn.sigmoid(raw)
    grad_values = steps * grad_scaled + skip_ref[...] * grad
    scores_low = grad_scores.astype(LOW)
    grad_c = dot_low(scores_low, b_rows)
    grad_b = dot_low(c_rows.T, scores_low).T
    grad_summed = jnp.concatenate([grad_values, grad_b, grad_c], axis=1) * slope
    grad_input = jnp.zeros_like(grad_summed)
    rows = []
    for tap in range(kernel_taps):
        away = kernel_taps - 1 - tap
        grad_input = grad_input + taps_ref[tap : tap + 1, :] * shift_up(grad_summed, away)
        rows.append(jnp.sum(grad_summed * shift_down(conv_input, away), axis=0, keepdims=True))
    rows.append(jnp.sum(grad_summed, axis=0, keepdims=True))
    out_ref[:, :width] = grad_input.astype(LOW)
    out_ref[:, width:] = grad_raw.astype(LOW)

    for index, row in enumerate(rows):
        small_ref[index : index + 1, :width] += row
    small_ref[5:6, :inner] += jnp.sum(grad * values, axis=0, keepdims=True)
    small_ref[5:6, width:] += jnp.sum(grad_raw, axis=0, keepdims=True)
    small_ref[6:7, width:] += jnp.sum(grad_rate * step, axis=0, keepdims=True) * decay


def gate_kernel(
    place_ref,
    normed_ref,
    upstream_ref,
    scanned_ref,
    piece_0,
    piece_1,
    piece_2,
    piece_3,
    gain_ref,
    gate_ref,
    mixed_ref,
    branch_ref,
    stats_ref,
    gate_weight,
    out_weight,
):
    inner = gain_ref.shape[1]
    length = gate_ref.shape[0]
    chunk = piece_0.shape[0] // 2
    slot = pl.program_id(0)

    @pl.when(slot == 0)
    def _():
        for away, piece in enumerate((piece_0, piece_1, piece_2, piece_3)):
            for half in range(2):
                rows = pl.ds(pl.multiple_of(place_ref[2 * away + half], 16), chunk)
                local = slice(half * chunk, (half + 1) * chunk)
                gate_weight[rows, :] = piece[local, :inner]
                out_weight[rows, :] = piece[local, inner:]

    gate = dot_low(read(normed_ref), gate_weight[...])
    gated = scanned_ref[...] * jax.nn.silu(gate)
    gained = gated * gain_ref[...]
    grad_mixed = dot_low(read(upstream_ref), out_weight[...])
    gate_ref[...] = gate
    mixed_ref[...] = grad_mixed
    branch_ref[...] = dot_nt(gained.astype(LOW), out_weight[...]).astype(LOW)
    squares = jnp.sum(gated * gated, axis=1, keepdims=True)
    products = jnp.sum(grad_mixed * gained, axis=1, keepdims=True)
    lane = lax.broadcasted_iota(jnp.int32, (length, LANES), 1)
    turned = jnp.where(lane == 0, squares, products).T
    stats_ref[pl.ds(slot, 1), :] = turned[0:1]
    stats_ref[pl.ds(pl.num_programs(0) + slot, 1), :] = turned[1:2]


def early_kernel(
    inner_all,
    place_ref,
    normed_ref,
    upstream_ref,
    scanned_ref,
    gate_ref,
    mixed_ref,
    stats_ref,
    gain_ref,
    grad_gate_ref,
    grad_scanned_ref,
    gain_grad_ref,
    piece_0,
    piece_1,
    piece_2,
    piece_3,
    sums_ref,
):
    slot = pl.program_id(0)
    inner = gain_ref.shape[1]
    chunk = piece_0.shape[0] // 2
    count = pl.num_programs(0)
    scale = lax.rsqrt(stats_ref[pl.ds(slot, 1), :] / inner_all + EPSILON)
    slope = scale * scale * scale * stats_ref[pl.ds(count + slot, 1), :] / inner_all
    scale, slope = row_spread(scale), row_spread(slope)
    gate = gate_ref[...]
    scanned = scanned_ref[...]
    sigmoid = jax.nn.sigmoid(gate)
    silu = gate * sigmoid
    gated = scanned * silu
    scaled = gated * scale
    mixed_low = (scaled * gain_ref[...]).astype(LOW)
    grad_mixed = mixed_ref[...]
    grad_gated = grad_mixed * gain_ref[...] * scale - gated * slope
    grad_gate = (grad_gated * scanned * (sigmoid * (1.0 + gate * (1.0 - sigmoid)))).astype(LOW)
    grad_gate_ref[...] = grad_gate
    grad_scanned_ref[...] = grad_gated * silu

    @pl.when(slot == 0)
    def _():
        sums_ref[...] = jnp.zeros_like(sums_ref)
        gain_grad_ref[...] = jnp.zeros_like(gain_grad_ref)

    gain_grad_ref[0:1, :] += jnp.sum(grad_mixed * scaled, axis=0, keepdims=True)
    sums_ref[:, :inner] += dot_tn(read(normed_ref), grad_gate)
    sums_ref[:, inner:] += dot_tn(read(upstream_ref), mixed_low)

    @pl.when(slot == count - 1)
    def _():
        for away, piece in enumerate((piece_0, piece_1, piece_2, piece_3)):
            for half in range(2):
                rows = pl.ds(pl.multiple_of(place_ref[2 * away + half], 16), chunk)
                piece[half * chunk : (half + 1) * chunk, :] = sums_ref[rows, :].astype(LOW)


def back_kernel(
    heads,
    place_ref,
    part_ref,
    grad_ref,
    scanned_ref,
    grad_gate_ref,
    normed_ref,
    weight_ref,
    gate_weight,
    taps_ref,
    bias_ref,
    dt_ref,
    alog_ref,
    skip_ref,
    gain_grad_ref,
    normed_grad_ref,
    given_ref,
    piece_0,
    piece_1,
    piece_2,
    piece_3,
    sums_ref,
    conv_ref,
    small_ref,
    pre_ref,
    extra_ref,
):
    slot = pl.program_id(0)
    inner = grad_ref.shape[1]
    width = taps_ref.shape[1]
    states = (width - inner) // 2
    chunk = sums_ref.shape[0] // 8

    @pl.when(slot == 0)
    def _():
        small_ref[...] = jnp.zeros_like(small_ref)
        pre_ref[...] = jnp.zeros_like(pre_ref)
        sums_ref[...] = jnp.zeros_like(sums_ref)

    scan_backward(
        heads,
        part_ref,
        grad_ref,
        scanned_ref,
        taps_ref,
        bias_ref,
        dt_ref,
        alog_ref,
        skip_ref,
        conv_ref,
        small_ref,
    )
    normed = read(normed_ref)
    grad_conv = conv_ref[...]
    sums_ref[...] += dot_tn(normed, grad_conv)
    grad_normed = dot_nt(grad_gate_ref[...], gate_weight[...]) + dot_nt(grad_conv, weight_ref[...])
    pre_ref[0:1, :] += jnp.sum(grad_normed * normed.astype(jnp.float32), axis=0, keepdims=True)

    normed_grad_ref[...] = grad_normed.astype(LOW)

    @pl.when(slot == pl.num_programs(0) - 1)
    def _():
        core = place_ref[8]
        taps_count = taps_ref.shape[0]
        extra_ref[...] = jnp.zeros_like(extra_ref)
        extra_ref[: taps_count + 1, :] = small_ref[: taps_count + 1, :width]
        extra_ref[5:6, :inner] = small_ref[5:6, :inner]
        extra_ref[5:6, inner:] = pre_ref[0:1, 2 * width :]
        extra_ref[6:7, :inner] = gain_grad_ref[0:1, :]
        extra_ref[6:7, inner : inner + LANES] = small_ref[5:6, width:]
        extra_ref[6:7, inner + LANES :] = small_ref[6:7, width:]
        extra_ref[7:8, :] = pre_ref[0:1, :width]
        extra_ref[8:9, :] = pre_ref[0:1, width : 2 * width]
        high, rest = parts_of(extra_ref[...], 2)
        for piece in (piece_0, piece_1, piece_2, piece_3):
            piece[8 * chunk // 4 : 8 * chunk // 4 + 16, :] = high
            piece[8 * chunk // 4 + 16 :, :] = rest
        for away, piece in enumerate((piece_0, piece_1, piece_2, piece_3)):
            for half in range(2):
                rows = pl.ds(pl.multiple_of(place_ref[2 * away + half], 16), chunk)
                local = slice(half * chunk, (half + 1) * chunk)
                whole = slice((2 * away + half) * chunk, (2 * away + half + 1) * chunk)
                b_sums = sums_ref[rows, inner : inner + states].astype(LOW)
                c_sums = sums_ref[rows, inner + states : width].astype(LOW)
                given_ref[whole, :] = jnp.where(core == 0, c_sums, b_sums)
                piece[local, :inner] = sums_ref[rows, :inner].astype(LOW)
                piece[local, inner : inner + states] = jnp.where(core == 0, b_sums, c_sums)
                piece[local, inner + states :] = sums_ref[rows, width:].astype(LOW)


def row_block(length, width):
    return pl.BlockSpec((length, width), lambda slot, place: (slot, 0))


def core_block(length, width, half):
    def index(slot, place):
        return (2 * (slot % half) + (place[8] ^ (slot // half)), 0)

    return pl.BlockSpec((length, width), index)


def near_block(length, width, half):
    return pl.BlockSpec((length, width), lambda slot, place: (jnp.minimum(slot, half - 1), 0))


def far_block(length, width, half):
    return pl.BlockSpec((length, width), lambda slot, place: (jnp.maximum(slot - half, 0), 0))


def whole_block(shape):
    return pl.BlockSpec(shape, lambda slot, place: (0,) * len(shape))


def run_slots(kernel, slots, place, cut, whole, outs, scratch, micros, waits=(), block=row_block):
    in_specs, arrays, places = [], [], []
    for array in cut:
        places.append(len(arrays))
        if isinstance(array, tuple):
            length = 2 * array[0].shape[0] // slots
            in_specs.append(near_block(length, array[0].shape[1], slots // 2))
            in_specs.append(far_block(length, array[1].shape[1], slots // 2))
            arrays.extend(array)
        else:
            in_specs.append(block(array.shape[0] // slots, array.shape[1]))
            arrays.append(array)
    in_specs += [whole_block(array.shape) for array in whole]
    arrays += whole
    given = len(arrays)

    def run(place_ref, *refs):
        cut_refs = [
            (refs[at], refs[at + 1]) if isinstance(array, tuple) else refs[at]
            for at, array in zip(places, cut)
        ]
        kernel(place_ref, *cut_refs, *refs[given - len(whole) : given], *refs[given + len(waits) :])

    return pl.pallas_call(
        run,
        grid_spec=pltpu.PrefetchScalarGridSpec(
            num_scalar_prefetch=1,
            grid=(slots,),
            in_specs=in_specs + [pl.BlockSpec(memory_space=pl.ANY)] * len(waits),
            out_specs=[spec for _, _, spec in outs],
            scratch_shapes=scratch,
        ),
        out_shape=[jax.ShapeDtypeStruct(shape, dtype) for shape, dtype, _ in outs],
        compiler_params=pltpu.CompilerParams(vmem_limit_bytes=44 << 20),
        cost_estimate=pl.CostEstimate(flops=int(micros * 1e9), bytes_accessed=1 << 20, transcendentals=0),
    )(place, *arrays, *waits)


def copies(kernel, scalars, value, others, count, waits=()):
    shape = value.shape
    return pl.pallas_call(
        kernel,
        grid_spec=pltpu.PrefetchScalarGridSpec(
            num_scalar_prefetch=len(scalars),
            grid=(count,),
            in_specs=[pl.BlockSpec(array.shape, lambda *_: (0, 0)) for array in (value, *others)]
            + [pl.BlockSpec(memory_space=pl.ANY)] * len(waits),
            out_specs=pl.BlockSpec(shape, lambda index, *_: (index, 0)),
        ),
        out_shape=jax.ShapeDtypeStruct((count * shape[0], shape[1]), LOW),
        compiler_params=pltpu.CompilerParams(vmem_limit_bytes=16 << 20),
        cost_estimate=pl.CostEstimate(flops=int(2e9), bytes_accessed=1 << 20, transcendentals=0),
    )(*scalars, value, *others, *waits)


def combine(terms, dtype, waits=()):
    shape = terms[0].shape
    steps = max(1, shape[0] // 384)

    def run(*refs):
        values = [ref[...].astype(jnp.float32) for ref in refs[: len(terms)]]
        if len(values) == 4:
            values = [values[0] + values[1], values[2] + values[3]]
        refs[-1][...] = sum(values[1:], values[0]).astype(dtype)

    block = pl.BlockSpec((shape[0] // steps, shape[1]), lambda index: (index, 0))
    return pl.pallas_call(
        run,
        grid=(steps,),
        in_specs=[block] * len(terms) + [pl.BlockSpec(memory_space=pl.ANY)] * len(waits),
        out_specs=block,
        out_shape=jax.ShapeDtypeStruct(shape, dtype),
        cost_estimate=pl.CostEstimate(flops=int(1e9), bytes_accessed=1 << 20, transcendentals=0),
    )(*terms, *waits)


def hold(values, waits):
    anywhere = pl.BlockSpec(memory_space=pl.ANY)
    return pl.pallas_call(
        lambda *refs: None,
        in_specs=[anywhere] * (len(values) + len(waits)),
        out_specs=[anywhere] * len(values),
        out_shape=[jax.ShapeDtypeStruct(value.shape, value.dtype) for value in values],
        input_output_aliases={index: index for index in range(len(values))},
    )(*values, *waits)


def small_rows(below):
    return below[:16].astype(jnp.float32) + below[16:].astype(jnp.float32)


def side_sums(left, right, ranks):
    rows, width = left[0].shape
    own = rows // ranks
    terms = (*left, *right)
    small_width = right[0].shape[1]

    def run(*refs):
        def total(these, read):
            values = [read(ref) for ref in these]
            return (values[0] + values[1]) + (values[2] + values[3])

        out_ref = refs[-1]
        high, rest = parts_of(total(refs[4:8], lambda ref: small_rows(ref[rows:, :])), 2)
        for rank in range(ranks):
            local = slice(rank * own, (rank + 1) * own)
            out_ref[rank, :own, :width] = total(refs[:4], lambda ref: ref[local, :].astype(jnp.float32)).astype(LOW)
            out_ref[rank, :own, width:] = total(refs[4:8], lambda ref: ref[local, :].astype(jnp.float32)).astype(LOW)
            out_ref[rank, own:, :small_width] = high
            out_ref[rank, own:, small_width : 2 * small_width] = rest
            out_ref[rank, own:, 2 * small_width :] = jnp.zeros_like(out_ref[rank, own:, 2 * small_width :])

    shape = (ranks, own + 16, width + small_width)
    return pl.pallas_call(
        run,
        out_shape=jax.ShapeDtypeStruct(shape, LOW),
        compiler_params=pltpu.CompilerParams(vmem_limit_bytes=24 << 20),
        cost_estimate=pl.CostEstimate(flops=int(3e9), bytes_accessed=1 << 20, transcendentals=0),
    )(*terms)


def owner_outputs(owned, rows, heads, states, sizes, waits):
    proj, inner_all, taps_shape, model = sizes
    ranks = owned.shape[0]
    inner = inner_all // ranks
    width = inner + 2 * states

    def blocks(ref, store):
        def lanes_of(value, rank):
            lane = lax.broadcasted_iota(jnp.int32, value.shape, 1)
            value = jnp.where(lane < heads, value, 0.0)
            return pltpu.roll(value, rank * heads, 1)

        in_ref, out_ref, taps_ref, bias_ref, gain_ref, pre_ref, head_ref = store
        taps_count = taps_shape[0]
        shared, b_sum, c_sum, step_sum, dt_sum, alog_sum, skip_sum = [0.0] * 7
        for rank in range(ranks):
            lanes = slice(rank * inner, (rank + 1) * inner)
            main = ref[rank, :rows, :].astype(jnp.float32)
            extra = ref[rank, rows:, :width].astype(jnp.float32) + ref[rank, rows:, width : 2 * width].astype(jnp.float32)
            in_ref[:, lanes] = main[:, :inner]
            out_ref[:, lanes] = main[:, inner : 2 * inner]
            in_ref[:, inner_all + rank * inner : inner_all + (rank + 1) * inner] = main[:, 2 * inner : 3 * inner]
            if rank % 2 == 0:
                b_sum = b_sum + main[:, 3 * inner : 3 * inner + states]
            else:
                c_sum = c_sum + main[:, 3 * inner : 3 * inner + states]
            step_sum = step_sum + lanes_of(main[:, 3 * inner + states :], rank)
            shared = shared + extra
            taps_ref[:, lanes] = extra[:taps_count, :inner]
            bias_ref[:, lanes] = extra[taps_count : taps_count + 1, :inner]
            gain_ref[:, lanes] = extra[6:7, :inner]
            dt_sum = dt_sum + lanes_of(extra[6:7, inner : inner + LANES], rank)
            alog_sum = alog_sum + lanes_of(extra[6:7, inner + LANES :], rank)
            skip_sum = skip_sum + lanes_of(lanes_sum(extra[:, :inner], heads)[5:6], rank)
        first_state = 2 * inner_all
        in_ref[:, first_state : first_state + states] = b_sum
        in_ref[:, first_state + states : first_state + 2 * states] = c_sum
        in_ref[:, first_state + 2 * states :] = step_sum[:, : proj - first_state - 2 * states]
        taps_ref[:, inner_all:] = shared[:taps_count, inner:]
        bias_ref[:, inner_all:] = shared[taps_count : taps_count + 1, inner:]
        pre_ref[:, :width] = shared[7:8]
        pre_ref[:, width : 2 * width] = shared[8:9]
        pre_ref[:, 2 * width :] = shared[5:6, inner : inner + model - 2 * width]
        head_ref[0:1, :] = dt_sum
        head_ref[1:2, :] = alog_sum
        head_ref[2:3, :] = skip_sum

    shapes = [(rows, proj), (rows, inner_all), taps_shape, (1, taps_shape[1]), (1, inner_all), (1, model), (8, LANES)]
    return pl.pallas_call(
        lambda ref, *refs: blocks(ref, refs[len(waits) :]),
        in_specs=[pl.BlockSpec(owned.shape, lambda: (0, 0, 0))] + [pl.BlockSpec(memory_space=pl.ANY)] * len(waits),
        out_shape=[jax.ShapeDtypeStruct(shape, jnp.float32) for shape in shapes],
        compiler_params=pltpu.CompilerParams(vmem_limit_bytes=24 << 20),
        cost_estimate=pl.CostEstimate(flops=int(3e9), bytes_accessed=1 << 20, transcendentals=0),
    )(owned, *waits)


def add_states(pieces, states, start):
    count = len(pieces)
    rows, width = states.shape[0] // count, states.shape[1]

    def run(*refs):
        for index in range(count):
            own = refs[index][...].astype(jnp.float32)
            other = refs[count][index * rows : (index + 1) * rows, :].astype(jnp.float32)
            refs[count + 1 + index][...] = (own + other).astype(LOW)

    block = pl.BlockSpec((rows, width), lambda _: (0, start // width))
    return pl.pallas_call(
        run,
        grid=(1,),
        in_specs=[block] * count + [pl.BlockSpec(states.shape, lambda _: (0, 0))],
        out_specs=[block] * count,
        out_shape=[jax.ShapeDtypeStruct(piece.shape, piece.dtype) for piece in pieces],
        input_output_aliases={index: index for index in range(count)},
        cost_estimate=pl.CostEstimate(flops=int(1e9), bytes_accessed=1 << 20, transcendentals=0),
    )(*pieces, states)


def columns_of(value, start, width, waits):
    return pl.pallas_call(
        copy_kernel,
        grid=(1,),
        in_specs=[
            pl.BlockSpec((value.shape[0], LANES * (width // LANES)), lambda _: (0, start // width))
        ]
        + [pl.BlockSpec(memory_space=pl.ANY)] * len(waits),
        out_specs=pl.BlockSpec((value.shape[0], width), lambda _: (0, 0)),
        out_shape=jax.ShapeDtypeStruct((value.shape[0], width), LOW),
        cost_estimate=pl.CostEstimate(flops=int(1e9), bytes_accessed=1 << 20, transcendentals=0),
    )(value, *waits)


def body(
    sizes,
    hidden_in,
    lengths,
    cotangent,
    pre_gain,
    in_weight,
    conv_weight,
    conv_bias,
    dt_bias,
    a_log,
    skip,
    inner_gain,
    out_weight,
):
    length, model = hidden_in.shape
    rows = in_weight.shape[0]
    inner_all = out_weight.shape[1]
    heads_all = dt_bias.shape[0]
    states = (conv_weight.shape[1] - inner_all) // 2
    ranks = sizes["xi"] * sizes["yi"] * sizes["c"]
    lines = sizes["xo"] * sizes["zo"]
    slots = ranks
    tokens = slots * length
    inner = inner_all // ranks
    heads = heads_all // ranks
    head_width = inner // heads
    core = lax.axis_index("c")
    rank = (lax.axis_index("xi") * sizes["yi"] + lax.axis_index("yi")) * sizes["c"] + core
    direct = sizes["xo"] == 1 and sizes["zo"] == 4
    piece_rows = model // 4
    chunk = piece_rows // 2
    spread = (sizes["xo"], sizes["zo"], sizes["xi"], sizes["yi"] * sizes["c"] * rows)
    natural = (sizes["xo"], sizes["xi"], sizes["zo"], sizes["yi"] * sizes["c"] * rows)
    if direct:
        planes = [lax.axis_index("zo") ^ away for away in range(4)]
        starts = [half * (model // 2) + plane * chunk for plane in planes for half in range(2)]
    else:
        starts = [chunk * index for index in range(8)]
    place = jnp.stack([jnp.asarray(value, jnp.int32) for value in (*starts, core)])

    def gather_rows(piece):
        if direct:
            return [piece] + [cross(piece, LINE, away, 4) for away in range(1, 4)]
        whole = lax.all_gather(piece, LINE, axis=0, tiled=True).reshape(*spread, -1)
        whole = whole.transpose(0, 2, 1, 3, 4).reshape(model, -1)
        return [whole[index * piece_rows : (index + 1) * piece_rows] for index in range(4)]

    def scatter_rows(pieces):
        whole = jnp.concatenate(pieces, axis=0).reshape(*natural, -1)
        whole = whole.transpose(0, 2, 1, 3, 4).reshape(model, -1)
        moved = lax.all_to_all(whole, LINE, split_axis=0, concat_axis=0, tiled=True)
        return jnp.sum(moved.reshape(lines, model // lines, -1).astype(jnp.float32), axis=0).astype(LOW)

    def exchange(value):
        return lax.all_to_all(value, PLANE, split_axis=0, concat_axis=0, tiled=True)

    def gather_tokens(value):
        return lax.all_gather(value, PLANE, axis=0, tiled=True)

    def scatter_far(value):
        return lax.psum_scatter(value, PLANE, scatter_dimension=0, tiled=True)

    def by_rank(columns):
        return columns.reshape(rows, ranks, -1).transpose(1, 0, 2)

    first_state = 2 * inner_all
    first_step = first_state + 2 * states
    state_columns = in_weight[:, first_state:first_step].reshape(rows, 2, states).transpose(1, 0, 2)
    packed = jnp.concatenate(
        [
            by_rank(in_weight[:, :inner_all]),
            by_rank(out_weight),
            by_rank(in_weight[:, inner_all:first_state]),
            jnp.tile(state_columns, (ranks // 2, 1, 1)),
            jnp.pad(by_rank(in_weight[:, first_step:]), ((0, 0), (0, 0), (0, LANES - heads))),
        ],
        axis=2,
    )
    plane_weights = exchange(packed).reshape(ranks * rows, -1)
    conv_pieces = gather_rows(plane_weights[:, 2 * inner :])
    other_states = swap(jnp.concatenate([piece[:, inner : inner + states] for piece in conv_pieces], axis=0))
    late_pieces = gather_rows(columns_of(plane_weights, 0, 2 * inner, conv_pieces[1:]))

    stream = hidden_in.astype(jnp.float32)
    scale = lax.rsqrt(jnp.mean(stream * stream, axis=-1, keepdims=True) + EPSILON)
    valid = (jnp.arange(length) < lengths[0])[:, None]
    own_upstream = jnp.where(valid, cotangent, jnp.zeros_like(cotangent))
    own_normed = copies(norm_kernel, (), hidden_in, (pre_gain[None],), 1, (plane_weights,))
    normed = gather_tokens(own_normed)
    upstream = gather_tokens(copies(mask_kernel, (lengths,), cotangent, (), 1, (own_normed,)))

    def of_rank(value, count):
        return lax.dynamic_slice_in_dim(value, rank * count, count, axis=-1)

    taps = jnp.concatenate(
        [of_rank(conv_weight[:, :inner_all], inner), conv_weight[:, inner_all:]], axis=1
    )
    bias = jnp.concatenate([of_rank(conv_bias[:inner_all], inner), conv_bias[inner_all:]])[None]
    dt_row = jnp.pad(of_rank(dt_bias, heads), (0, LANES - heads))[None]
    alog_row = jnp.pad(of_rank(a_log, heads), (0, LANES - heads))[None]
    skip_row = jnp.repeat(of_rank(skip, heads), head_width)[None]
    gain_row = of_rank(inner_gain, inner)[None]
    params = (taps, bias, dt_row, alog_row, skip_row)
    part_width = inner + 2 * states + LANES

    part, scanned, conv_weights = run_slots(
        functools.partial(conv_kernel, heads),
        slots,
        place,
        (normed,),
        (*conv_pieces, other_states, *params),
        [
            ((tokens, part_width), jnp.float32, row_block(length, part_width)),
            ((tokens, inner), jnp.float32, row_block(length, inner)),
            ((model, part_width), LOW, whole_block((model, part_width))),
        ],
        [],
        12,
    )
    gate, grad_mixed, branch, stats, gate_weights = run_slots(
        gate_kernel,
        slots,
        place,
        (normed, upstream, scanned),
        (*late_pieces, gain_row),
        [
            ((tokens, inner), jnp.float32, row_block(length, inner)),
            ((tokens, inner), jnp.float32, row_block(length, inner)),
            ((tokens, model), LOW, row_block(length, model)),
            ((2 * slots, length), jnp.float32, whole_block((2 * slots, length))),
            ((model, inner), LOW, whole_block((model, inner))),
        ],
        [pltpu.VMEM((model, inner), LOW)],
        14,
    )
    stats = stats + swap(stats)
    far = [cross(stats, ("xi", "yi"), away, 4) for away in (3, 1, 2)]
    stats = (stats + far[0]) + (far[1] + far[2])
    branch_own = scatter_far(branch)
    squares = lax.dynamic_index_in_dim(stats, rank, axis=0, keepdims=False)
    inner_scale = lax.rsqrt(squares / inner_all + EPSILON)[:, None]
    output = jnp.where(valid, stream + branch_own * inner_scale, 0.0).astype(LOW)

    piece_shape = (piece_rows, 2 * inner)
    grad_gate, grad_scanned, gain_grad, *early = run_slots(
        functools.partial(early_kernel, inner_all),
        slots,
        place,
        (normed, upstream, scanned, gate, grad_mixed),
        (stats, gain_row),
        [
            ((tokens, inner), LOW, row_block(length, inner)),
            ((tokens, inner), jnp.float32, row_block(length, inner)),
            ((8, inner), jnp.float32, whole_block((8, inner))),
        ]
        + [(piece_shape, LOW, whole_block(piece_shape))] * 4,
        [pltpu.VMEM((model, 2 * inner), jnp.float32)],
        16,
    )
    width = taps.shape[1]
    piece_shape = (piece_rows + 32, inner + states + LANES)
    held = run_slots(
        functools.partial(back_kernel, heads),
        slots,
        place,
        (part, grad_scanned, scanned, grad_gate, normed),
        (conv_weights, gate_weights, *params, gain_grad),
        [
            ((tokens, model), LOW, row_block(length, model)),
            ((model, states), LOW, whole_block((model, states))),
        ]
        + [(piece_shape, LOW, whole_block(piece_shape))] * 4,
        [
            pltpu.VMEM((model, part_width), jnp.float32),
            pltpu.VMEM((length, part_width), LOW),
            pltpu.VMEM((8, part_width), jnp.float32),
            pltpu.VMEM((8, model), jnp.float32),
            pltpu.VMEM((16, width), jnp.float32),
        ],
        40,
    )
    if direct:
        early_moved = [cross(early[away], LINE, away, 4) for away in (2, 3, 1)]
        held = hold(held, [*early_moved, branch_own])
    grad_normed, given, *pieces = held
    pieces = add_states(pieces, swap(given), inner)
    if direct:
        conv_moved = [cross(pieces[away], LINE, away, 4) for away in (1, 2, 3)]
    else:
        conv_moved = []
    grad_own = scatter_far(grad_normed) * pre_gain
    along = jnp.mean(grad_own * stream, axis=-1, keepdims=True)
    grad_stream = grad_own * scale - stream * (scale**3 * along)
    grad_hidden = (own_upstream.astype(jnp.float32) + grad_stream).astype(LOW)

    if direct:
        early_terms, conv_terms = [early[0], *early_moved], [pieces[0], *conv_moved]
        side = side_sums(early_terms, conv_terms, ranks)
    else:
        extra = small_rows(pieces[0][piece_rows:])
        high, rest = parts_of(lax.psum(extra, LINE), 2)
        side = jnp.concatenate([scatter_rows(early), scatter_rows([p[:piece_rows] for p in pieces])], axis=1)
        below = jnp.pad(jnp.concatenate([high, rest], axis=1), ((0, 0), (0, side.shape[1] - 2 * width)))
        below = jnp.broadcast_to(below[None], (ranks, *below.shape))
        side = jnp.pad(side.reshape(ranks, rows, -1), ((0, 0), (0, -rows % 16), (0, 0)))
        side = jnp.concatenate([side, below], axis=1)
    owned = exchange(side)
    sizes_out = (in_weight.shape[1], inner_all, conv_weight.shape, model)
    owned_in, owned_out, taps_grad, bias_grad, gain_grads, pre_grad, head_grads = owner_outputs(
        owned, rows + -rows % 16, heads, states, sizes_out, (grad_hidden, output)
    )
    return (
        output,
        grad_hidden,
        pre_grad[0] / pre_gain,
        owned_in[:rows],
        taps_grad,
        bias_grad[0],
        head_grads[0, :heads_all],
        head_grads[1, :heads_all],
        head_grads[2, :heads_all],
        gain_grads[0],
        owned_out[:rows],
    )


def solution(mesh):
    dp, fsdp = mesh.shape["dp"], mesh.shape["fsdp"]
    shape = (dp // 2, 2, fsdp // 4, 2, 2)
    fine = Mesh(mesh.devices.reshape(shape), EVERY)
    split, kept = P(EVERY, None), P()
    in_specs = (split, P(EVERY), split, kept, split, kept, kept, kept, kept, kept, kept, split)
    out_specs = (split, split, kept, split, kept, kept, kept, kept, kept, kept, split)
    return jax.shard_map(
        functools.partial(body, dict(zip(EVERY, shape))),
        mesh=fine,
        in_specs=in_specs,
        out_specs=out_specs,
        check_vma=False,
    )
```

```python
import functools

import jax
import jax.numpy as jnp
from jax import lax
from jax.experimental import pallas as pl
from jax.experimental.pallas import tpu as pltpu
from jax.sharding import Mesh
from jax.sharding import PartitionSpec as P

EPSILON = 1e-05
LANES = 128
LOW = jnp.bfloat16
LOG2E = 1.4426950408889634

PLANE = ("xi", "yi", "c")
LINE = ("xo", "zo")
EVERY = ("xo", "xi", "zo", "yi", "c")


def swap(value):
    return lax.ppermute(value, "c", [(0, 1), (1, 0)])


def cross(value, axes, distance, count):
    return lax.ppermute(value, axes, [(i, i ^ distance) for i in range(count)])


def shift_down(value, rows):
    if rows == 0:
        return value
    index = lax.broadcasted_iota(jnp.int32, value.shape, 0)
    return jnp.where(index >= rows, pltpu.roll(value, rows, 0), 0.0)


def shift_up(value, rows):
    if rows == 0:
        return value
    length = value.shape[0]
    index = lax.broadcasted_iota(jnp.int32, value.shape, 0)
    return jnp.where(index < length - rows, pltpu.roll(value, length - rows, 0), 0.0)


def softplus(value):
    return jnp.maximum(value, 0.0) + jnp.log1p(jnp.exp(-jnp.abs(value)))


def dot_low(left, right):
    return jnp.dot(left, right, preferred_element_type=jnp.float32)


def dot_nt(left, right):
    return lax.dot_general(left, right, (((1,), (1,)), ((), ())), preferred_element_type=jnp.float32)


def dot_tn(left, right):
    return lax.dot_general(left, right, (((0,), (0,)), ((), ())), preferred_element_type=jnp.float32)


def parts_of(value, count):
    terms = []
    for _ in range(count):
        terms.append(value.astype(LOW))
        value = value - terms[-1].astype(jnp.float32)
    return terms


def convolve(conv_input, taps, bias):
    kernel_taps = taps.shape[0]
    summed = bias
    for tap in range(kernel_taps):
        summed = summed + taps[tap : tap + 1] * shift_down(conv_input, kernel_taps - 1 - tap)
    return summed


def triangle(length, lower):
    row = lax.broadcasted_iota(jnp.int32, (length, length), 0)
    column = lax.broadcasted_iota(jnp.int32, (length, length), 1)
    return row >= column if lower else row <= column


def cumulate(mask, value, count):
    mask = mask.astype(LOW)
    return sum(dot_low(mask, term) for term in parts_of(value, count))


def pair_lanes(value, pair, first):
    return jnp.where(first, value[:, 2 * pair : 2 * pair + 1], value[:, 2 * pair + 1 : 2 * pair + 2])


def lanes_sum(value, head_count):
    inner = value.shape[1]
    lane = lax.broadcasted_iota(jnp.int32, (inner, LANES), 0)
    head = lax.broadcasted_iota(jnp.int32, (inner, LANES), 1)
    start = head * (inner // head_count)
    member = jnp.logical_and(lane >= start, lane < start + inner // head_count).astype(LOW)
    return sum(dot_low(term, member) for term in parts_of(value, 2))


def turned_columns(rows):
    blank = jnp.zeros((LANES - rows.shape[0], rows.shape[1]), rows.dtype)
    return jnp.concatenate([rows, blank], axis=0).T


def read(ref):
    if not isinstance(ref, tuple):
        return ref[...]
    near, far = ref
    return jnp.where(pl.program_id(0) < pl.num_programs(0) // 2, near[...], far[...])


def row_spread(row):
    return jnp.broadcast_to(row, (8, row.shape[1])).T[:, :1]


def scan_forward(heads, part, taps_ref, bias_ref, dt_ref, alog_ref, skip_ref, out_ref):
    inner = out_ref.shape[1]
    length = out_ref.shape[0]
    width = taps_ref.shape[1]
    states = (width - inner) // 2
    conv_low = jax.nn.silu(convolve(part[:, :width], taps_ref[...], bias_ref[...])).astype(LOW)
    step = softplus(part[:, width:] + dt_ref[...])
    lower = triangle(length, True)
    cumulative = cumulate(lower, step * (-jnp.exp(alog_ref[...]) * LOG2E), 3)
    across = cumulative.T
    scores = dot_nt(conv_low[:, inner + states :], conv_low[:, inner : inner + states])
    scores = jnp.where(lower, scores, 0.0)
    first = lax.broadcasted_iota(jnp.int32, (length, LANES), 1) < inner // heads
    for pair in range(heads // 2):
        lanes = slice(pair * LANES, (pair + 1) * LANES)
        values = conv_low[:, lanes].astype(jnp.float32)
        scaled = (values * pair_lanes(step, pair, first)).astype(LOW)
        sums = []
        for head in (2 * pair, 2 * pair + 1):
            spread = cumulative[:, head : head + 1] - across[head : head + 1, :]
            mixing = scores * jnp.exp2(jnp.minimum(spread, 0.0))
            sums.append(dot_low(mixing.astype(LOW), scaled))
        out_ref[:, lanes] = jnp.where(first, sums[0], sums[1]) + skip_ref[:, lanes] * values


def norm_kernel(hidden_ref, gain_ref, *refs):
    stream = hidden_ref[...].astype(jnp.float32)
    scale = lax.rsqrt(jnp.mean(stream * stream, axis=-1, keepdims=True) + EPSILON)
    refs[-1][...] = (stream * scale * gain_ref[...]).astype(LOW)


def mask_kernel(lengths_ref, cotangent_ref, *refs):
    row = lax.broadcasted_iota(jnp.int32, cotangent_ref.shape, 0)
    own = cotangent_ref[...].astype(jnp.float32)
    refs[-1][...] = jnp.where(row < lengths_ref[0], own, 0.0).astype(LOW)


def copy_kernel(value_ref, *refs):
    refs[-1][...] = value_ref[...]


def conv_kernel(
    heads,
    place_ref,
    normed_ref,
    piece_0,
    piece_1,
    piece_2,
    piece_3,
    other_ref,
    taps_ref,
    bias_ref,
    dt_ref,
    alog_ref,
    skip_ref,
    part_ref,
    scanned_ref,
    weight_ref,
):
    inner = scanned_ref.shape[1]
    states = other_ref.shape[1]
    chunk = weight_ref.shape[0] // 8

    @pl.when(pl.program_id(0) == 0)
    def _():
        core = place_ref[8]
        for away, piece in enumerate((piece_0, piece_1, piece_2, piece_3)):
            steps = turned_columns(piece[2 * chunk :, : 2 * chunk].astype(jnp.float32)).astype(LOW)
            for half in range(2):
                rows = pl.ds(pl.multiple_of(place_ref[2 * away + half], 16), chunk)
                local = slice(half * chunk, (half + 1) * chunk)
                own = piece[local, inner : inner + states]
                other = other_ref[(2 * away + half) * chunk : (2 * away + half + 1) * chunk, :]
                weight_ref[rows, :inner] = piece[local, :inner]
                weight_ref[rows, inner : inner + states] = jnp.where(core == 0, own, other)
                weight_ref[rows, inner + states : inner + 2 * states] = jnp.where(core == 0, other, own)
                weight_ref[rows, inner + 2 * states :] = steps[local]

    part = dot_low(read(normed_ref), weight_ref[...])
    part_ref[...] = part
    scan_forward(heads, part, taps_ref, bias_ref, dt_ref, alog_ref, skip_ref, scanned_ref)


def scan_backward(
    counts,
    beside,
    heads,
    part_ref,
    grad_ref,
    scanned_ref,
    taps_ref,
    bias_ref,
    dt_ref,
    alog_ref,
    skip_ref,
    out_ref,
    small_ref,
):
    inner = grad_ref.shape[1]
    length = grad_ref.shape[0]
    width = taps_ref.shape[1]
    states = (width - inner) // 2
    kernel_taps = taps_ref.shape[0]
    conv_input = part_ref[:, :width]
    summed = convolve(conv_input, taps_ref[...], bias_ref[...])
    gate = jax.nn.sigmoid(summed)
    conv_low = (summed * gate).astype(LOW)
    slope = gate * (1.0 + summed * (1.0 - gate))
    raw = part_ref[:, width:] + dt_ref[...]
    step = softplus(raw)
    decay = -jnp.exp(alog_ref[...])
    lower = triangle(length, True)
    cumulative = cumulate(lower, step * (decay * LOG2E), 3)
    across = cumulative.T
    b_rows = conv_low[:, inner : inner + states]
    c_rows = conv_low[:, inner + states :]
    scores = jnp.where(lower, dot_nt(c_rows, b_rows), 0.0)
    values = conv_low[:, :inner].astype(jnp.float32)
    half = inner // heads
    first = lax.broadcasted_iota(jnp.int32, (length, LANES), 1) < half
    steps = jnp.concatenate([pair_lanes(step, pair, first) for pair in range(heads // 2)], axis=1)
    scaled = (values * steps).astype(LOW)
    grad = grad_ref[...]
    grad_low = grad.astype(LOW)
    grad_across = grad.T.astype(LOW)
    upper_rows = lax.broadcasted_iota(jnp.int32, (LANES, length), 0) < half
    grad_scores = jnp.zeros((length, length), jnp.float32)
    moved = []
    for pair in range(heads // 2):
        lanes = slice(pair * LANES, (pair + 1) * LANES)
        sums = []
        for head in (2 * pair, 2 * pair + 1):
            spread = cumulative[:, head : head + 1] - across[head : head + 1, :]
            decays = jnp.exp2(jnp.minimum(spread, 0.0))
            mixing = (scores * decays).astype(LOW)
            own = first if head % 2 == 0 else jnp.logical_not(first)
            grad_own = jnp.where(own, grad[:, lanes], 0.0).astype(LOW)
            beside(head)
            grad_scores = grad_scores + dot_nt(grad_own, scaled[:, lanes]) * decays
            sums.append(dot_low(grad_across[lanes], mixing))
        moved.append(jnp.where(upper_rows, sums[0], sums[1]).T)
    grad_scaled = jnp.concatenate(moved, axis=1)
    within = scanned_ref[...] - skip_ref[...] * values
    grad_cumulative = lanes_sum(
        grad_low.astype(jnp.float32) * within - scaled.astype(jnp.float32) * grad_scaled, heads
    )
    grad_rate = cumulate(triangle(length, False), grad_cumulative, 3)
    grad_step = grad_rate * decay + lanes_sum(values * grad_scaled, heads)
    grad_raw = grad_step * jax.nn.sigmoid(raw)
    grad_values = steps * grad_scaled + skip_ref[...] * grad
    scores_low = jnp.where(lower, grad_scores, 0.0).astype(LOW)
    grad_c = dot_low(scores_low, b_rows)
    grad_b = dot_low(c_rows.T, scores_low).T
    grad_summed = jnp.concatenate([grad_values, grad_b, grad_c], axis=1) * slope
    grad_input = jnp.zeros_like(grad_summed)
    rows = []
    for tap in range(kernel_taps):
        away = kernel_taps - 1 - tap
        shifted = shift_up(grad_summed, away)
        grad_input = grad_input + taps_ref[tap : tap + 1, :] * shifted
        rows.append(jnp.sum(shifted * conv_input, axis=0, keepdims=True))
    rows.append(jnp.sum(grad_summed, axis=0, keepdims=True))
    out_ref[:, :width] = grad_input.astype(LOW)
    out_ref[:, width:] = grad_raw.astype(LOW)

    def counted(row):
        return jnp.where(counts, row, 0.0)

    for index, row in enumerate(rows):
        small_ref[index : index + 1, :width] += counted(row)
    small_ref[5:6, :inner] += counted(jnp.sum(grad * values, axis=0, keepdims=True))
    small_ref[5:6, width:] += counted(jnp.sum(grad_raw, axis=0, keepdims=True))
    small_ref[6:7, width:] += counted(jnp.sum(grad_rate * step, axis=0, keepdims=True) * decay)


def gate_kernel(
    place_ref,
    normed_ref,
    upstream_ref,
    scanned_ref,
    piece_0,
    piece_1,
    piece_2,
    piece_3,
    gain_ref,
    gate_ref,
    mixed_ref,
    branch_ref,
    stats_ref,
    gate_weight,
    out_weight,
):
    inner = gain_ref.shape[1]
    length = gate_ref.shape[0]
    chunk = piece_0.shape[0] // 2
    slot = pl.program_id(0)

    @pl.when(slot == 0)
    def _():
        for away, piece in enumerate((piece_0, piece_1, piece_2, piece_3)):
            for half in range(2):
                rows = pl.ds(pl.multiple_of(place_ref[2 * away + half], 16), chunk)
                local = slice(half * chunk, (half + 1) * chunk)
                gate_weight[rows, :] = piece[local, :inner]
                out_weight[rows, :] = piece[local, inner:]

    gate = dot_low(read(normed_ref), gate_weight[...])
    gated = scanned_ref[...] * jax.nn.silu(gate)
    gained = gated * gain_ref[...]
    grad_mixed = dot_low(read(upstream_ref), out_weight[...])
    gate_ref[...] = gate
    mixed_ref[...] = grad_mixed
    branch_ref[...] = dot_nt(gained.astype(LOW), out_weight[...]).astype(LOW)
    squares = jnp.sum(gated * gated, axis=1, keepdims=True)
    products = jnp.sum(grad_mixed * gained, axis=1, keepdims=True)
    lane = lax.broadcasted_iota(jnp.int32, (length, LANES), 1)
    turned = jnp.where(lane == 0, squares, products).T
    span = stats_ref.shape[1]
    for part in range(length // span):
        row = slot * (length // span) + part
        lanes = slice(part * span, (part + 1) * span)
        stats_ref[pl.ds(row, 1), :] = turned[0:1, lanes]
        stats_ref[pl.ds(stats_ref.shape[0] // 2 + row, 1), :] = turned[1:2, lanes]


def early_kernel(
    inner_all,
    place_ref,
    normed_ref,
    upstream_ref,
    scanned_ref,
    gate_ref,
    mixed_ref,
    stats_ref,
    gain_ref,
    grad_gate_ref,
    grad_scanned_ref,
    gain_grad_ref,
    piece_0,
    piece_1,
    piece_2,
    piece_3,
    sums_ref,
):
    slot = pl.program_id(0)
    inner = gain_ref.shape[1]
    chunk = piece_0.shape[0] // 2
    count = pl.num_programs(0)
    scales, slopes = [], []
    span = gate_ref.shape[0] // stats_ref.shape[1]
    for part in range(span):
        row = slot * span + part
        scale = lax.rsqrt(stats_ref[pl.ds(row, 1), :] / inner_all + EPSILON)
        slope = scale * scale * scale * stats_ref[pl.ds(stats_ref.shape[0] // 2 + row, 1), :] / inner_all
        scales.append(row_spread(scale))
        slopes.append(row_spread(slope))
    scale, slope = jnp.concatenate(scales, axis=0), jnp.concatenate(slopes, axis=0)
    gate = gate_ref[...]
    scanned = scanned_ref[...]
    sigmoid = jax.nn.sigmoid(gate)
    silu = gate * sigmoid
    gated = scanned * silu
    scaled = gated * scale
    mixed_low = (scaled * gain_ref[...]).astype(LOW)
    grad_mixed = mixed_ref[...]
    grad_gated = grad_mixed * gain_ref[...] * scale - gated * slope
    grad_gate = (grad_gated * scanned * (sigmoid * (1.0 + gate * (1.0 - sigmoid)))).astype(LOW)
    grad_gate_ref[...] = grad_gate
    grad_scanned_ref[...] = grad_gated * silu

    @pl.when(slot == 0)
    def _():
        sums_ref[...] = jnp.zeros_like(sums_ref)
        gain_grad_ref[...] = jnp.zeros_like(gain_grad_ref)

    gain_grad_ref[0:1, :] += jnp.sum(grad_mixed * scaled, axis=0, keepdims=True)
    sums_ref[:, :inner] += dot_tn(read(normed_ref), grad_gate)
    sums_ref[:, inner:] += dot_tn(read(upstream_ref), mixed_low)

    @pl.when(slot == count - 1)
    def _():
        for away, piece in enumerate((piece_0, piece_1, piece_2, piece_3)):
            for half in range(2):
                rows = pl.ds(pl.multiple_of(place_ref[2 * away + half], 16), chunk)
                piece[half * chunk : (half + 1) * chunk, :] = sums_ref[rows, :].astype(LOW)


def back_kernel(
    heads,
    place_ref,
    part_ref,
    grad_ref,
    scanned_ref,
    grad_gate_ref,
    normed_ref,
    weight_ref,
    gate_weight,
    taps_ref,
    bias_ref,
    dt_ref,
    alog_ref,
    skip_ref,
    gain_grad_ref,
    normed_grad_ref,
    given_ref,
    piece_0,
    piece_1,
    piece_2,
    piece_3,
    sums_ref,
    conv_ref,
    last_ref,
    small_ref,
    pre_ref,
    extra_ref,
):
    slot = pl.program_id(0)
    inner = grad_ref.shape[1]
    width = taps_ref.shape[1]
    states = (width - inner) // 2
    chunk = sums_ref.shape[0] // 8

    @pl.when(slot == 0)
    def _():
        small_ref[...] = jnp.zeros_like(small_ref)
        pre_ref[...] = jnp.zeros_like(pre_ref)
        sums_ref[...] = jnp.zeros_like(sums_ref)
        conv_ref[...] = jnp.zeros_like(conv_ref)

    last_ref[...] = conv_ref[...]
    block = normed_ref.shape[1] // heads

    def beside(index):
        columns = slice(index * block, (index + 1) * block)
        normed = normed_ref[:, columns]
        sums_ref[columns, :] += dot_tn(normed, last_ref[...])
        grad_normed = dot_nt(grad_gate_ref[...], gate_weight[columns, :])
        grad_normed = grad_normed + dot_nt(last_ref[...], weight_ref[columns, :])
        pre_sum = jnp.sum(grad_normed * normed.astype(jnp.float32), axis=0, keepdims=True)
        pre_ref[0:1, columns] += jnp.where(slot > 0, pre_sum, 0.0)
        normed_grad_ref[:, columns] = grad_normed.astype(LOW)

    scan_backward(
        slot < pl.num_programs(0) - 1,
        beside,
        heads,
        part_ref,
        grad_ref,
        scanned_ref,
        taps_ref,
        bias_ref,
        dt_ref,
        alog_ref,
        skip_ref,
        conv_ref,
        small_ref,
    )
    @pl.when(slot == pl.num_programs(0) - 1)
    def _():
        core = place_ref[8]
        count = taps_ref.shape[0] + 1
        wide = inner + states
        extra_ref[...] = jnp.zeros_like(extra_ref)
        extra_ref[:count, :] = small_ref[:count, :wide]
        extra_ref[5:6, :inner] = small_ref[5:6, :inner]
        extra_ref[5:6, inner:] = small_ref[6:7, width:]
        extra_ref[6:7, :inner] = gain_grad_ref[0:1, :]
        extra_ref[6:7, inner:] = small_ref[5:6, width:]
        for part in range(3):
            extra_ref[7 + part : 8 + part, :] = pre_ref[0:1, part * wide : (part + 1) * wide]
        for part in range(count - 1):
            extra_ref[10:11, part * states : (part + 1) * states] = small_ref[part : part + 1, wide:width]
        extra_ref[11:12, :states] = small_ref[count - 1 : count, wide:width]
        high, rest = parts_of(extra_ref[...], 2)
        for piece in (piece_0, piece_1, piece_2, piece_3):
            piece[2 * chunk + 16 : 2 * chunk + 32, :] = high
            piece[2 * chunk + 32 :, :] = rest
            piece[2 * chunk : 2 * chunk + 16, 2 * chunk :] = jnp.zeros((16, wide - 2 * chunk), LOW)
        for away, piece in enumerate((piece_0, piece_1, piece_2, piece_3)):
            for half in range(2):
                rows = pl.ds(pl.multiple_of(place_ref[2 * away + half], 16), chunk)
                local = slice(half * chunk, (half + 1) * chunk)
                whole = slice((2 * away + half) * chunk, (2 * away + half + 1) * chunk)
                step_rows = [] if half == 0 else step_rows
                b_sums = sums_ref[rows, inner : inner + states].astype(LOW)
                c_sums = sums_ref[rows, inner + states : width].astype(LOW)
                steps = sums_ref[rows, width:]
                given_ref[whole, :] = jnp.where(core == 0, c_sums, b_sums)
                piece[local, :inner] = sums_ref[rows, :inner].astype(LOW)
                piece[local, inner : inner + states] = jnp.where(core == 0, b_sums, c_sums)
                step_rows.append(steps)
            turned = jnp.concatenate(step_rows, axis=0).T[:16]
            piece[2 * chunk : 2 * chunk + 16, : 2 * chunk] = turned.astype(LOW)


def row_block(length, width):
    return pl.BlockSpec((length, width), lambda slot, place: (slot, 0))


def core_block(length, width, half):
    def index(slot, place):
        return (2 * (slot % half) + (place[8] ^ (slot // half)), 0)

    return pl.BlockSpec((length, width), index)


def early_block(slots):
    return lambda length, width: pl.BlockSpec(
        (length, width), lambda step, place: (jnp.minimum(step, slots - 1), 0)
    )


def late_block(length, width):
    return pl.BlockSpec((length, width), lambda step, place: (jnp.maximum(step - 1, 0), 0))


def near_block(length, width, half):
    return pl.BlockSpec((length, width), lambda slot, place: (jnp.minimum(slot, half - 1), 0))


def far_block(length, width, half):
    return pl.BlockSpec((length, width), lambda slot, place: (jnp.maximum(slot - half, 0), 0))


def whole_block(shape):
    return pl.BlockSpec(shape, lambda slot, place: (0,) * len(shape))


def run_slots(kernel, slots, place, cut, whole, outs, scratch, micros, waits=(), specs=None):
    in_specs, arrays, places = [], [], []
    for array in cut:
        places.append(len(arrays))
        if isinstance(array, tuple):
            length = 2 * array[0].shape[0] // slots
            in_specs.append(near_block(length, array[0].shape[1], slots // 2))
            in_specs.append(far_block(length, array[1].shape[1], slots // 2))
            arrays.extend(array)
        else:
            spec = row_block if specs is None else specs[len(places) - 1]
            in_specs.append(spec(array.shape[0] // slots, array.shape[1]))
            arrays.append(array)
    arrays = [pltpu.with_memory_space_constraint(array, pltpu.HBM) for array in arrays]
    in_specs += [whole_block(array.shape) for array in whole]
    arrays += whole
    given = len(arrays)

    def run(place_ref, *refs):
        cut_refs = [
            (refs[at], refs[at + 1]) if isinstance(array, tuple) else refs[at]
            for at, array in zip(places, cut)
        ]
        kernel(place_ref, *cut_refs, *refs[given - len(whole) : given], *refs[given + len(waits) :])

    return pl.pallas_call(
        run,
        grid_spec=pltpu.PrefetchScalarGridSpec(
            num_scalar_prefetch=1,
            grid=(slots if specs is None else slots + 1,),
            in_specs=in_specs + [pl.BlockSpec(memory_space=pl.ANY)] * len(waits),
            out_specs=[spec for _, _, spec in outs],
            scratch_shapes=scratch,
        ),
        out_shape=[pltpu.HBM(shape, dtype) for shape, dtype, _ in outs],
        compiler_params=pltpu.CompilerParams(vmem_limit_bytes=44 << 20),
        cost_estimate=pl.CostEstimate(flops=int(micros * 1e9), bytes_accessed=1 << 20, transcendentals=0),
    )(place, *arrays, *waits)


def copies(kernel, scalars, value, others, count, waits=()):
    shape = value.shape
    return pl.pallas_call(
        kernel,
        grid_spec=pltpu.PrefetchScalarGridSpec(
            num_scalar_prefetch=len(scalars),
            grid=(count,),
            in_specs=[pl.BlockSpec(array.shape, lambda *_: (0, 0)) for array in (value, *others)]
            + [pl.BlockSpec(memory_space=pl.ANY)] * len(waits),
            out_specs=pl.BlockSpec(shape, lambda index, *_: (index, 0)),
        ),
        out_shape=jax.ShapeDtypeStruct((count * shape[0], shape[1]), LOW),
        compiler_params=pltpu.CompilerParams(vmem_limit_bytes=16 << 20),
        cost_estimate=pl.CostEstimate(flops=int(2e9), bytes_accessed=1 << 20, transcendentals=0),
    )(*scalars, value, *others, *waits)


def combine(terms, dtype, waits=()):
    shape = terms[0].shape
    steps = max(1, shape[0] // 384)

    def run(*refs):
        values = [ref[...].astype(jnp.float32) for ref in refs[: len(terms)]]
        if len(values) == 4:
            values = [values[0] + values[1], values[2] + values[3]]
        refs[-1][...] = sum(values[1:], values[0]).astype(dtype)

    block = pl.BlockSpec((shape[0] // steps, shape[1]), lambda index: (index, 0))
    return pl.pallas_call(
        run,
        grid=(steps,),
        in_specs=[block] * len(terms) + [pl.BlockSpec(memory_space=pl.ANY)] * len(waits),
        out_specs=block,
        out_shape=jax.ShapeDtypeStruct(shape, dtype),
        cost_estimate=pl.CostEstimate(flops=int(1e9), bytes_accessed=1 << 20, transcendentals=0),
    )(*terms, *waits)


def hold(values, waits):
    anywhere = pl.BlockSpec(memory_space=pl.ANY)
    return pl.pallas_call(
        lambda *refs: None,
        in_specs=[anywhere] * (len(values) + len(waits)),
        out_specs=[anywhere] * len(values),
        out_shape=[jax.ShapeDtypeStruct(value.shape, value.dtype) for value in values],
        input_output_aliases={index: index for index in range(len(values))},
    )(*values, *waits)


def small_rows(below):
    return below[:16].astype(jnp.float32) + below[16:].astype(jnp.float32)


def side_sums(terms, ranks, small, waits):
    width = terms[0].shape[1]
    rows = terms[0].shape[0] - 48 if small else terms[0].shape[0]
    own = rows // ranks

    def run(*refs):
        def total(read):
            values = [read(ref) for ref in refs[:4]]
            return (values[0] + values[1]) + (values[2] + values[3])

        out_ref = refs[-1]
        if small:
            steps = turned_columns(total(lambda ref: ref[rows : rows + 16, :rows].astype(jnp.float32))).astype(LOW)
            high, rest = parts_of(total(lambda ref: small_rows(ref[rows + 16 :, :])), 2)
        for rank in range(ranks):
            local = slice(rank * own, (rank + 1) * own)
            out_ref[rank, :own, :width] = total(lambda ref: ref[local, :].astype(jnp.float32)).astype(LOW)
            if small:
                out_ref[rank, :own, width:] = steps[local]
                out_ref[rank, own : own + 16, :width] = high
                out_ref[rank, own + 16 :, :width] = rest
                out_ref[rank, own:, width:] = jnp.zeros((32, LANES), LOW)

    whole = pl.BlockSpec(terms[0].shape, lambda: (0, 0))
    shape = (ranks, own + 32, width + LANES) if small else (ranks, own, width)
    return pl.pallas_call(
        run,
        in_specs=[whole] * 4 + [pl.BlockSpec(memory_space=pl.ANY)] * len(waits),
        out_shape=jax.ShapeDtypeStruct(shape, LOW),
        compiler_params=pltpu.CompilerParams(vmem_limit_bytes=24 << 20),
        cost_estimate=pl.CostEstimate(flops=int(2e9), bytes_accessed=1 << 20, transcendentals=0),
    )(*terms, *waits)


def owner_outputs(early, owned, rows, heads, states, sizes, waits):
    proj, inner_all, taps_shape, model = sizes
    ranks = owned.shape[0]
    inner = inner_all // ranks

    def blocks(early_ref, ref, store):
        def lanes_of(value, rank):
            lane = lax.broadcasted_iota(jnp.int32, value.shape, 1)
            value = jnp.where(lane < heads, value, 0.0)
            return pltpu.roll(value, rank * heads, 1)

        in_ref, out_ref, taps_ref, bias_ref, gain_ref, pre_ref, head_ref = store
        taps_count = taps_shape[0]
        shared, b_sum, c_sum, step_sum, dt_sum, alog_sum, skip_sum = [0.0] * 7
        for rank in range(ranks):
            lanes = slice(rank * inner, (rank + 1) * inner)
            main = ref[rank, :rows, :].astype(jnp.float32)
            extra = small_rows(ref[rank, rows:, : inner + states])
            in_ref[:, lanes] = early_ref[rank, :, :inner].astype(jnp.float32)
            out_ref[:, lanes] = early_ref[rank, :, inner:].astype(jnp.float32)
            in_ref[:, inner_all + rank * inner : inner_all + (rank + 1) * inner] = main[:, :inner]
            if rank % 2 == 0:
                b_sum = b_sum + main[:, inner : inner + states]
            else:
                c_sum = c_sum + main[:, inner : inner + states]
            step_sum = step_sum + lanes_of(main[:, inner + states :], rank)
            shared = shared + extra
            taps_ref[:, lanes] = extra[:taps_count, :inner]
            bias_ref[:, lanes] = extra[taps_count : taps_count + 1, :inner]
            gain_ref[:, lanes] = extra[6:7, :inner]
            dt_sum = dt_sum + lanes_of(extra[6:7, inner:], rank)
            alog_sum = alog_sum + lanes_of(extra[5:6, inner:], rank)
            skip_sum = skip_sum + lanes_of(lanes_sum(extra[:, :inner], heads)[5:6], rank)
        first_state = 2 * inner_all
        in_ref[:, first_state : first_state + states] = b_sum
        in_ref[:, first_state + states : first_state + 2 * states] = c_sum
        in_ref[:, first_state + 2 * states :] = step_sum[:, : proj - first_state - 2 * states]
        taps_ref[:, inner_all : inner_all + states] = shared[:taps_count, inner:]
        bias_ref[:, inner_all : inner_all + states] = shared[taps_count : taps_count + 1, inner:]
        for tap in range(taps_count):
            taps_ref[tap : tap + 1, inner_all + states :] = shared[10:11, tap * states : (tap + 1) * states]
        bias_ref[:, inner_all + states :] = shared[11:12, :states]
        wide = inner + states
        for part in range(3):
            pre_ref[:, part * wide : (part + 1) * wide] = shared[7 + part : 8 + part]
        head_ref[0:1, :] = dt_sum
        head_ref[1:2, :] = alog_sum
        head_ref[2:3, :] = skip_sum

    shapes = [(rows, proj), (rows, inner_all), taps_shape, (1, taps_shape[1]), (1, inner_all), (1, model), (8, LANES)]
    return pl.pallas_call(
        lambda early_ref, ref, *refs: blocks(early_ref, ref, refs[len(waits) :]),
        in_specs=[pl.BlockSpec(array.shape, lambda: (0, 0, 0)) for array in (early, owned)]
        + [pl.BlockSpec(memory_space=pl.ANY)] * len(waits),
        out_shape=[jax.ShapeDtypeStruct(shape, jnp.float32) for shape in shapes],
        compiler_params=pltpu.CompilerParams(vmem_limit_bytes=24 << 20),
        cost_estimate=pl.CostEstimate(flops=int(3e9), bytes_accessed=1 << 20, transcendentals=0),
    )(early, owned, *waits)


def pack_steps(value, start, width):
    rows = value.shape[0]

    def run(value_ref, out_ref):
        out_ref[:rows, :] = value_ref[:, start : start + width]
        steps = value_ref[:, start + width : start + width + LANES].astype(jnp.float32)
        out_ref[rows:, :rows] = steps.T[:16].astype(LOW)
        out_ref[rows:, rows:] = jnp.zeros((16, width - rows), LOW)

    return pl.pallas_call(
        run,
        out_shape=jax.ShapeDtypeStruct((rows + 16, width), LOW),
        cost_estimate=pl.CostEstimate(flops=int(1e9), bytes_accessed=1 << 20, transcendentals=0),
    )(value)


def add_states(pieces, states, start):
    count = len(pieces)
    rows, width = states.shape[0] // count, states.shape[1]

    def run(*refs):
        for index in range(count):
            own = refs[index][...].astype(jnp.float32)
            other = refs[count][index * rows : (index + 1) * rows, :].astype(jnp.float32)
            refs[count + 1 + index][...] = (own + other).astype(LOW)

    block = pl.BlockSpec((rows, width), lambda _: (0, start // width))
    return pl.pallas_call(
        run,
        grid=(1,),
        in_specs=[block] * count + [pl.BlockSpec(states.shape, lambda _: (0, 0))],
        out_specs=[block] * count,
        out_shape=[jax.ShapeDtypeStruct(piece.shape, piece.dtype) for piece in pieces],
        input_output_aliases={index: index for index in range(count)},
        cost_estimate=pl.CostEstimate(flops=int(1e9), bytes_accessed=1 << 20, transcendentals=0),
    )(*pieces, states)


def columns_of(value, start, width, waits):
    return pl.pallas_call(
        copy_kernel,
        grid=(1,),
        in_specs=[
            pl.BlockSpec((value.shape[0], LANES * (width // LANES)), lambda _: (0, start // width))
        ]
        + [pl.BlockSpec(memory_space=pl.ANY)] * len(waits),
        out_specs=pl.BlockSpec((value.shape[0], width), lambda _: (0, 0)),
        out_shape=jax.ShapeDtypeStruct((value.shape[0], width), LOW),
        cost_estimate=pl.CostEstimate(flops=int(1e9), bytes_accessed=1 << 20, transcendentals=0),
    )(value, *waits)


def body(
    sizes,
    hidden_in,
    lengths,
    cotangent,
    pre_gain,
    in_weight,
    conv_weight,
    conv_bias,
    dt_bias,
    a_log,
    skip,
    inner_gain,
    out_weight,
):
    length, model = hidden_in.shape
    rows = in_weight.shape[0]
    inner_all = out_weight.shape[1]
    heads_all = dt_bias.shape[0]
    states = (conv_weight.shape[1] - inner_all) // 2
    ranks = sizes["xi"] * sizes["yi"] * sizes["c"]
    lines = sizes["xo"] * sizes["zo"]
    slots = ranks
    tokens = slots * length
    inner = inner_all // ranks
    heads = heads_all // ranks
    head_width = inner // heads
    core = lax.axis_index("c")
    rank = (lax.axis_index("xi") * sizes["yi"] + lax.axis_index("yi")) * sizes["c"] + core
    direct = sizes["xo"] == 1 and sizes["zo"] == 4
    piece_rows = model // 4
    chunk = piece_rows // 2
    spread = (sizes["xo"], sizes["zo"], sizes["xi"], sizes["yi"] * sizes["c"] * rows)
    natural = (sizes["xo"], sizes["xi"], sizes["zo"], sizes["yi"] * sizes["c"] * rows)
    if direct:
        planes = [lax.axis_index("zo") ^ away for away in range(4)]
        starts = [half * (model // 2) + plane * chunk for plane in planes for half in range(2)]
    else:
        starts = [chunk * index for index in range(8)]
    place = jnp.stack([jnp.asarray(value, jnp.int32) for value in (*starts, core)])

    def gather_rows(piece):
        if direct:
            return [piece] + [cross(piece, LINE, away, 4) for away in range(1, 4)]
        whole = lax.all_gather(piece, LINE, axis=0, tiled=True).reshape(*spread, -1)
        whole = whole.transpose(0, 2, 1, 3, 4).reshape(model, -1)
        return [whole[index * piece_rows : (index + 1) * piece_rows] for index in range(4)]

    def scatter_rows(pieces):
        whole = jnp.concatenate(pieces, axis=0).reshape(*natural, -1)
        whole = whole.transpose(0, 2, 1, 3, 4).reshape(model, -1)
        moved = lax.all_to_all(whole, LINE, split_axis=0, concat_axis=0, tiled=True)
        return jnp.sum(moved.reshape(lines, model // lines, -1).astype(jnp.float32), axis=0).astype(LOW)

    def exchange(value):
        return lax.all_to_all(value, PLANE, split_axis=0, concat_axis=0, tiled=True)

    def gather_tokens(value):
        return lax.all_gather(value, PLANE, axis=0, tiled=True)

    def scatter_far(value):
        return lax.psum_scatter(value, PLANE, scatter_dimension=0, tiled=True)

    def by_rank(columns):
        return columns.reshape(rows, ranks, -1).transpose(1, 0, 2)

    first_state = 2 * inner_all
    first_step = first_state + 2 * states
    state_columns = in_weight[:, first_state:first_step].reshape(rows, 2, states).transpose(1, 0, 2)
    packed = jnp.concatenate(
        [
            by_rank(in_weight[:, :inner_all]),
            by_rank(out_weight),
            by_rank(in_weight[:, inner_all:first_state]),
            jnp.tile(state_columns, (ranks // 2, 1, 1)),
            jnp.pad(by_rank(in_weight[:, first_step:]), ((0, 0), (0, 0), (0, LANES - heads))),
        ],
        axis=2,
    )
    plane_weights = exchange(packed).reshape(ranks * rows, -1)
    if direct:
        conv_pieces = gather_rows(pack_steps(plane_weights, 2 * inner, inner + states))
    else:
        conv_pieces = [pack_steps(piece, 0, inner + states) for piece in gather_rows(plane_weights[:, 2 * inner :])]
    other_states = swap(
        jnp.concatenate([piece[:piece_rows, inner : inner + states] for piece in conv_pieces], axis=0)
    )
    late_pieces = gather_rows(columns_of(plane_weights, 0, 2 * inner, conv_pieces[1:]))

    stream = hidden_in.astype(jnp.float32)
    scale = lax.rsqrt(jnp.mean(stream * stream, axis=-1, keepdims=True) + EPSILON)
    valid = (jnp.arange(length) < lengths[0])[:, None]
    own_upstream = jnp.where(valid, cotangent, jnp.zeros_like(cotangent))
    own_normed = copies(norm_kernel, (), hidden_in, (pre_gain[None],), 1, (plane_weights,))
    normed = gather_tokens(own_normed)
    upstream = gather_tokens(copies(mask_kernel, (lengths,), cotangent, (), 1, (own_normed,)))

    def of_rank(value, count):
        return lax.dynamic_slice_in_dim(value, rank * count, count, axis=-1)

    taps = jnp.concatenate(
        [of_rank(conv_weight[:, :inner_all], inner), conv_weight[:, inner_all:]], axis=1
    )
    bias = jnp.concatenate([of_rank(conv_bias[:inner_all], inner), conv_bias[inner_all:]])[None]
    dt_row = jnp.pad(of_rank(dt_bias, heads), (0, LANES - heads))[None]
    alog_row = jnp.pad(of_rank(a_log, heads), (0, LANES - heads))[None]
    skip_row = jnp.repeat(of_rank(skip, heads), head_width)[None]
    gain_row = of_rank(inner_gain, inner)[None]
    params = (taps, bias, dt_row, alog_row, skip_row)
    part_width = inner + 2 * states + LANES

    part, scanned, conv_weights = run_slots(
        functools.partial(conv_kernel, heads),
        slots,
        place,
        (normed,),
        (*conv_pieces, other_states, *params),
        [
            ((tokens, part_width), jnp.float32, row_block(length, part_width)),
            ((tokens, inner), jnp.float32, row_block(length, inner)),
            ((model, part_width), LOW, whole_block((model, part_width))),
        ],
        [],
        12,
    )
    gate, grad_mixed, branch, stats, gate_weights = run_slots(
        gate_kernel,
        slots // 2,
        place,
        (normed, upstream, scanned),
        (*late_pieces, gain_row),
        [
            ((tokens, inner), jnp.float32, row_block(2 * length, inner)),
            ((tokens, inner), jnp.float32, row_block(2 * length, inner)),
            ((tokens, model), LOW, row_block(2 * length, model)),
            ((2 * slots, length), jnp.float32, whole_block((2 * slots, length))),
            ((model, inner), LOW, whole_block((model, inner))),
        ],
        [pltpu.VMEM((model, inner), LOW)],
        14,
    )
    stats = stats + swap(stats)
    far = [cross(stats, ("xi", "yi"), away, 4) for away in (3, 1, 2)]
    stats = (stats + far[0]) + (far[1] + far[2])
    branch_own = scatter_far(branch)
    squares = lax.dynamic_index_in_dim(stats, rank, axis=0, keepdims=False)
    inner_scale = lax.rsqrt(squares / inner_all + EPSILON)[:, None]
    output = jnp.where(valid, stream + branch_own * inner_scale, 0.0).astype(LOW)

    piece_shape = (piece_rows, 2 * inner)
    grad_gate, grad_scanned, gain_grad, *early = run_slots(
        functools.partial(early_kernel, inner_all),
        slots // 2,
        place,
        (normed, upstream, scanned, gate, grad_mixed),
        (stats, gain_row),
        [
            ((tokens, inner), LOW, row_block(2 * length, inner)),
            ((tokens, inner), jnp.float32, row_block(2 * length, inner)),
            ((8, inner), jnp.float32, whole_block((8, inner))),
        ]
        + [(piece_shape, LOW, whole_block(piece_shape))] * 4,
        [pltpu.VMEM((model, 2 * inner), jnp.float32)],
        16,
    )
    width = taps.shape[1]
    piece_shape = (piece_rows + 48, inner + states)
    held = run_slots(
        functools.partial(back_kernel, heads),
        slots,
        place,
        (part, grad_scanned, scanned, grad_gate, normed),
        (conv_weights, gate_weights, *params, gain_grad),
        [
            ((tokens, model), LOW, late_block(length, model)),
            ((model, states), LOW, whole_block((model, states))),
        ]
        + [(piece_shape, LOW, whole_block(piece_shape))] * 4,
        [
            pltpu.VMEM((model, part_width), jnp.float32),
            pltpu.VMEM((length, part_width), LOW),
            pltpu.VMEM((length, part_width), LOW),
            pltpu.VMEM((8, part_width), jnp.float32),
            pltpu.VMEM((8, model), jnp.float32),
            pltpu.VMEM((16, inner + states), jnp.float32),
        ],
        30,
        specs=[early_block(slots)] * 3 + [late_block] * 2,
    )
    if direct:
        early_moved = [cross(early[away], LINE, away, 4) for away in (2, 3, 1)]
        held = hold(held, [*early_moved, branch_own])
    grad_normed, given, *pieces = held
    pieces = add_states(pieces, swap(given), inner)
    if direct:
        conv_moved = [cross(pieces[away], LINE, away, 4) for away in (1, 2, 3)]
    else:
        conv_moved = []
    grad_own = scatter_far(grad_normed) * pre_gain
    along = jnp.mean(grad_own * stream, axis=-1, keepdims=True)
    grad_stream = grad_own * scale - stream * (scale**3 * along)
    grad_hidden = (own_upstream.astype(jnp.float32) + grad_stream).astype(LOW)

    if direct:
        early_owned = exchange(side_sums([early[0], *early_moved], ranks, False, pieces[:1]))
        owned = exchange(side_sums([pieces[0], *conv_moved], ranks, True, (early_owned,)))
    else:
        below = jnp.concatenate(parts_of(lax.psum(small_rows(pieces[0][piece_rows + 16 :]), LINE), 2), axis=0)
        below = jnp.pad(jnp.broadcast_to(below[None], (ranks, *below.shape)), ((0, 0), (0, 0), (0, LANES)))

        def padded(value):
            return jnp.pad(value.reshape(ranks, rows, -1), ((0, 0), (0, -rows % 16), (0, 0)))

        def with_steps(piece):
            steps = piece[piece_rows : piece_rows + 16, :piece_rows].T
            return jnp.concatenate([piece[:piece_rows], jnp.pad(steps, ((0, 0), (0, LANES - 16)))], axis=1)

        early_owned = exchange(padded(scatter_rows(early)))
        conv = padded(scatter_rows([with_steps(piece) for piece in pieces]))
        owned = exchange(jnp.concatenate([conv, below], axis=1))
    sizes_out = (in_weight.shape[1], inner_all, conv_weight.shape, model)
    owned_in, owned_out, taps_grad, bias_grad, gain_grads, pre_grad, head_grads = owner_outputs(
        early_owned, owned, rows + -rows % 16, heads, states, sizes_out, (output,)
    )
    return (
        output,
        grad_hidden,
        pre_grad[0] / pre_gain,
        owned_in[:rows],
        taps_grad,
        bias_grad[0],
        head_grads[0, :heads_all],
        head_grads[1, :heads_all],
        head_grads[2, :heads_all],
        gain_grads[0],
        owned_out[:rows],
    )


def solution(mesh):
    dp, fsdp = mesh.shape["dp"], mesh.shape["fsdp"]
    shape = (dp // 2, 2, fsdp // 4, 2, 2)
    fine = Mesh(mesh.devices.reshape(shape), EVERY)
    split, kept = P(EVERY, None), P()
    in_specs = (split, P(EVERY), split, kept, split, kept, kept, kept, kept, kept, kept, split)
    out_specs = (split, split, kept, split, kept, kept, kept, kept, kept, kept, split)
    return jax.shard_map(
        functools.partial(body, dict(zip(EVERY, shape))),
        mesh=fine,
        in_specs=in_specs,
        out_specs=out_specs,
        check_vma=False,
    )
```

```python
import functools

import jax
import jax.numpy as jnp
from jax import lax
from jax.experimental import pallas as pl
from jax.experimental.pallas import tpu as pltpu
from jax.sharding import Mesh
from jax.sharding import PartitionSpec as P

EPSILON = 1e-05
LANES = 128
LOW = jnp.bfloat16
LOG2E = 1.4426950408889634

PLANE = ("xi", "yi", "c")
LINE = ("xo", "zo")
EVERY = ("xo", "xi", "zo", "yi", "c")


def swap(value):
    return lax.ppermute(value, "c", [(0, 1), (1, 0)])


def cross(value, axes, distance, count):
    return lax.ppermute(value, axes, [(i, i ^ distance) for i in range(count)])


def shift_down(value, rows):
    if rows == 0:
        return value
    index = lax.broadcasted_iota(jnp.int32, value.shape, 0)
    return jnp.where(index >= rows, pltpu.roll(value, rows, 0), 0.0)


def shift_up(value, rows):
    if rows == 0:
        return value
    length = value.shape[0]
    index = lax.broadcasted_iota(jnp.int32, value.shape, 0)
    return jnp.where(index < length - rows, pltpu.roll(value, length - rows, 0), 0.0)


def softplus(value):
    return jnp.maximum(value, 0.0) + jnp.log1p(jnp.exp(-jnp.abs(value)))


def dot_low(left, right):
    return jnp.dot(left, right, preferred_element_type=jnp.float32)


def dot_nt(left, right):
    return lax.dot_general(left, right, (((1,), (1,)), ((), ())), preferred_element_type=jnp.float32)


def dot_tn(left, right):
    return lax.dot_general(left, right, (((0,), (0,)), ((), ())), preferred_element_type=jnp.float32)


def parts_of(value, count):
    terms = []
    for _ in range(count):
        terms.append(value.astype(LOW))
        value = value - terms[-1].astype(jnp.float32)
    return terms


def convolve(conv_input, taps, bias):
    kernel_taps = taps.shape[0]
    summed = bias
    for tap in range(kernel_taps):
        summed = summed + taps[tap : tap + 1] * shift_down(conv_input, kernel_taps - 1 - tap)
    return summed


def triangle(length, lower):
    row = lax.broadcasted_iota(jnp.int32, (length, length), 0)
    column = lax.broadcasted_iota(jnp.int32, (length, length), 1)
    return row >= column if lower else row <= column


def cumulate(mask, value, count):
    mask = mask.astype(LOW)
    return sum(dot_low(mask, term) for term in parts_of(value, count))


def pair_lanes(value, pair, first):
    return jnp.where(first, value[:, 2 * pair : 2 * pair + 1], value[:, 2 * pair + 1 : 2 * pair + 2])


def lanes_sum(value, head_count):
    inner = value.shape[1]
    lane = lax.broadcasted_iota(jnp.int32, (inner, LANES), 0)
    head = lax.broadcasted_iota(jnp.int32, (inner, LANES), 1)
    start = head * (inner // head_count)
    member = jnp.logical_and(lane >= start, lane < start + inner // head_count).astype(LOW)
    return sum(dot_low(term, member) for term in parts_of(value, 2))


def turned_columns(rows):
    blank = jnp.zeros((LANES - rows.shape[0], rows.shape[1]), rows.dtype)
    return jnp.concatenate([rows, blank], axis=0).T


def read(ref):
    if not isinstance(ref, tuple):
        return ref[...]
    near, far = ref
    return jnp.where(pl.program_id(0) < pl.num_programs(0) // 2, near[...], far[...])


def row_spread(row):
    return jnp.broadcast_to(row, (8, row.shape[1])).T[:, :1]


def scan_forward(heads, part, taps_ref, bias_ref, dt_ref, alog_ref, skip_ref, out_ref):
    inner = out_ref.shape[1]
    length = out_ref.shape[0]
    width = taps_ref.shape[1]
    states = (width - inner) // 2
    conv_low = jax.nn.silu(convolve(part[:, :width], taps_ref[...], bias_ref[...])).astype(LOW)
    step = softplus(part[:, width:] + dt_ref[...])
    lower = triangle(length, True)
    cumulative = cumulate(lower, step * (-jnp.exp(alog_ref[...]) * LOG2E), 3)
    across = cumulative.T
    scores = dot_nt(conv_low[:, inner + states :], conv_low[:, inner : inner + states])
    scores = jnp.where(lower, scores, 0.0)
    first = lax.broadcasted_iota(jnp.int32, (length, LANES), 1) < inner // heads
    for pair in range(heads // 2):
        lanes = slice(pair * LANES, (pair + 1) * LANES)
        values = conv_low[:, lanes].astype(jnp.float32)
        scaled = (values * pair_lanes(step, pair, first)).astype(LOW)
        sums = []
        for head in (2 * pair, 2 * pair + 1):
            spread = cumulative[:, head : head + 1] - across[head : head + 1, :]
            mixing = scores * jnp.exp2(jnp.minimum(spread, 0.0))
            sums.append(dot_low(mixing.astype(LOW), scaled))
        out_ref[:, lanes] = jnp.where(first, sums[0], sums[1]) + skip_ref[:, lanes] * values


def norm_kernel(hidden_ref, gain_ref, *refs):
    stream = hidden_ref[...].astype(jnp.float32)
    scale = lax.rsqrt(jnp.mean(stream * stream, axis=-1, keepdims=True) + EPSILON)
    refs[-1][...] = (stream * scale * gain_ref[...]).astype(LOW)


def mask_kernel(lengths_ref, cotangent_ref, *refs):
    row = lax.broadcasted_iota(jnp.int32, cotangent_ref.shape, 0)
    own = cotangent_ref[...].astype(jnp.float32)
    refs[-1][...] = jnp.where(row < lengths_ref[0], own, 0.0).astype(LOW)


def copy_kernel(value_ref, *refs):
    refs[-1][...] = value_ref[...]


def conv_kernel(
    heads,
    place_ref,
    normed_ref,
    piece_0,
    piece_1,
    piece_2,
    piece_3,
    other_ref,
    taps_ref,
    bias_ref,
    dt_ref,
    alog_ref,
    skip_ref,
    part_ref,
    scanned_ref,
    weight_ref,
):
    inner = scanned_ref.shape[1]
    states = other_ref.shape[1]
    chunk = weight_ref.shape[0] // 8

    @pl.when(pl.program_id(0) == 0)
    def _():
        core = place_ref[8]
        for away, piece in enumerate((piece_0, piece_1, piece_2, piece_3)):
            steps = turned_columns(piece[2 * chunk :, : 2 * chunk].astype(jnp.float32)).astype(LOW)
            for half in range(2):
                rows = pl.ds(pl.multiple_of(place_ref[2 * away + half], 16), chunk)
                local = slice(half * chunk, (half + 1) * chunk)
                own = piece[local, inner : inner + states]
                other = other_ref[(2 * away + half) * chunk : (2 * away + half + 1) * chunk, :]
                weight_ref[rows, :inner] = piece[local, :inner]
                weight_ref[rows, inner : inner + states] = jnp.where(core == 0, own, other)
                weight_ref[rows, inner + states : inner + 2 * states] = jnp.where(core == 0, other, own)
                weight_ref[rows, inner + 2 * states :] = steps[local]

    part = dot_low(read(normed_ref), weight_ref[...])
    part_ref[...] = part
    scan_forward(heads, part, taps_ref, bias_ref, dt_ref, alog_ref, skip_ref, scanned_ref)


def scan_backward(
    counts,
    beside,
    heads,
    part_ref,
    grad_ref,
    scanned_ref,
    taps_ref,
    bias_ref,
    dt_ref,
    alog_ref,
    skip_ref,
    out_ref,
    small_ref,
):
    inner = grad_ref.shape[1]
    length = grad_ref.shape[0]
    width = taps_ref.shape[1]
    states = (width - inner) // 2
    kernel_taps = taps_ref.shape[0]
    conv_input = part_ref[:, :width]
    summed = convolve(conv_input, taps_ref[...], bias_ref[...])
    gate = jax.nn.sigmoid(summed)
    conv_low = (summed * gate).astype(LOW)
    slope = gate * (1.0 + summed * (1.0 - gate))
    raw = part_ref[:, width:] + dt_ref[...]
    step = softplus(raw)
    decay = -jnp.exp(alog_ref[...])
    lower = triangle(length, True)
    cumulative = cumulate(lower, step * (decay * LOG2E), 3)
    across = cumulative.T
    b_rows = conv_low[:, inner : inner + states]
    c_rows = conv_low[:, inner + states :]
    scores = jnp.where(lower, dot_nt(c_rows, b_rows), 0.0)
    values = conv_low[:, :inner].astype(jnp.float32)
    half = inner // heads
    first = lax.broadcasted_iota(jnp.int32, (length, LANES), 1) < half
    steps = jnp.concatenate([pair_lanes(step, pair, first) for pair in range(heads // 2)], axis=1)
    scaled = (values * steps).astype(LOW)
    grad = grad_ref[...]
    grad_low = grad.astype(LOW)
    grad_across = grad.T.astype(LOW)
    upper_rows = lax.broadcasted_iota(jnp.int32, (LANES, length), 0) < half
    grad_scores = jnp.zeros((length, length), jnp.float32)
    moved = []
    for pair in range(heads // 2):
        lanes = slice(pair * LANES, (pair + 1) * LANES)
        sums = []
        for head in (2 * pair, 2 * pair + 1):
            spread = cumulative[:, head : head + 1] - across[head : head + 1, :]
            decays = jnp.exp2(jnp.minimum(spread, 0.0))
            mixing = (scores * decays).astype(LOW)
            own = first if head % 2 == 0 else jnp.logical_not(first)
            grad_own = jnp.where(own, grad[:, lanes], 0.0).astype(LOW)
            beside(head)
            grad_scores = grad_scores + dot_nt(grad_own, scaled[:, lanes]) * decays
            sums.append(dot_low(grad_across[lanes], mixing))
        moved.append(jnp.where(upper_rows, sums[0], sums[1]).T)
    grad_scaled = jnp.concatenate(moved, axis=1)
    within = scanned_ref[...] - skip_ref[...] * values
    grad_cumulative = lanes_sum(
        grad_low.astype(jnp.float32) * within - scaled.astype(jnp.float32) * grad_scaled, heads
    )
    grad_rate = cumulate(triangle(length, False), grad_cumulative, 3)
    grad_step = grad_rate * decay + lanes_sum(values * grad_scaled, heads)
    grad_raw = grad_step * jax.nn.sigmoid(raw)
    grad_values = steps * grad_scaled + skip_ref[...] * grad
    scores_low = jnp.where(lower, grad_scores, 0.0).astype(LOW)
    grad_c = dot_low(scores_low, b_rows)
    grad_b = dot_low(c_rows.T, scores_low).T
    grad_summed = jnp.concatenate([grad_values, grad_b, grad_c], axis=1) * slope
    grad_input = jnp.zeros_like(grad_summed)
    rows = []
    for tap in range(kernel_taps):
        away = kernel_taps - 1 - tap
        shifted = shift_up(grad_summed, away)
        grad_input = grad_input + taps_ref[tap : tap + 1, :] * shifted
        rows.append(jnp.sum(shifted * conv_input, axis=0, keepdims=True))
    rows.append(jnp.sum(grad_summed, axis=0, keepdims=True))
    out_ref[:, :width] = grad_input.astype(LOW)
    out_ref[:, width:] = grad_raw.astype(LOW)

    def counted(row):
        return jnp.where(counts, row, 0.0)

    for index, row in enumerate(rows):
        small_ref[index : index + 1, :width] += counted(row)
    small_ref[5:6, :inner] += counted(jnp.sum(grad * values, axis=0, keepdims=True))
    small_ref[5:6, width:] += counted(jnp.sum(grad_raw, axis=0, keepdims=True))
    small_ref[6:7, width:] += counted(jnp.sum(grad_rate * step, axis=0, keepdims=True) * decay)


def gate_kernel(
    place_ref,
    normed_ref,
    upstream_ref,
    scanned_ref,
    piece_0,
    piece_1,
    piece_2,
    piece_3,
    gain_ref,
    gate_ref,
    mixed_ref,
    branch_ref,
    stats_ref,
    gate_weight,
    out_weight,
):
    inner = gain_ref.shape[1]
    length = gate_ref.shape[0]
    chunk = piece_0.shape[0] // 2
    slot = pl.program_id(0)

    @pl.when(slot == 0)
    def _():
        for away, piece in enumerate((piece_0, piece_1, piece_2, piece_3)):
            for half in range(2):
                rows = pl.ds(pl.multiple_of(place_ref[2 * away + half], 16), chunk)
                local = slice(half * chunk, (half + 1) * chunk)
                gate_weight[rows, :] = piece[local, :inner]
                out_weight[rows, :] = piece[local, inner:]

    gate = dot_low(read(normed_ref), gate_weight[...])
    gated = scanned_ref[...] * jax.nn.silu(gate)
    gained = gated * gain_ref[...]
    grad_mixed = dot_low(read(upstream_ref), out_weight[...])
    gate_ref[...] = gate
    mixed_ref[...] = grad_mixed
    branch_ref[...] = dot_nt(gained.astype(LOW), out_weight[...]).astype(LOW)
    squares = jnp.sum(gated * gated, axis=1, keepdims=True)
    products = jnp.sum(grad_mixed * gained, axis=1, keepdims=True)
    lane = lax.broadcasted_iota(jnp.int32, (length, LANES), 1)
    turned = jnp.where(lane == 0, squares, products).T
    span = stats_ref.shape[1]
    for part in range(length // span):
        row = slot * (length // span) + part
        lanes = slice(part * span, (part + 1) * span)
        stats_ref[pl.ds(row, 1), :] = turned[0:1, lanes]
        stats_ref[pl.ds(stats_ref.shape[0] // 2 + row, 1), :] = turned[1:2, lanes]


def early_kernel(
    inner_all,
    place_ref,
    normed_ref,
    upstream_ref,
    scanned_ref,
    gate_ref,
    mixed_ref,
    stats_ref,
    gain_ref,
    grad_gate_ref,
    grad_scanned_ref,
    gain_grad_ref,
    piece_0,
    piece_1,
    piece_2,
    piece_3,
    sums_ref,
):
    slot = pl.program_id(0)
    inner = gain_ref.shape[1]
    chunk = piece_0.shape[0] // 2
    count = pl.num_programs(0)
    scales, slopes = [], []
    span = gate_ref.shape[0] // stats_ref.shape[1]
    for part in range(span):
        row = slot * span + part
        scale = lax.rsqrt(stats_ref[pl.ds(row, 1), :] / inner_all + EPSILON)
        slope = scale * scale * scale * stats_ref[pl.ds(stats_ref.shape[0] // 2 + row, 1), :] / inner_all
        scales.append(row_spread(scale))
        slopes.append(row_spread(slope))
    scale, slope = jnp.concatenate(scales, axis=0), jnp.concatenate(slopes, axis=0)
    gate = gate_ref[...]
    scanned = scanned_ref[...]
    sigmoid = jax.nn.sigmoid(gate)
    silu = gate * sigmoid
    gated = scanned * silu
    scaled = gated * scale
    mixed_low = (scaled * gain_ref[...]).astype(LOW)
    grad_mixed = mixed_ref[...]
    grad_gated = grad_mixed * gain_ref[...] * scale - gated * slope
    grad_gate = (grad_gated * scanned * (sigmoid * (1.0 + gate * (1.0 - sigmoid)))).astype(LOW)
    grad_gate_ref[...] = grad_gate
    grad_scanned_ref[...] = grad_gated * silu

    @pl.when(slot == 0)
    def _():
        sums_ref[...] = jnp.zeros_like(sums_ref)
        gain_grad_ref[...] = jnp.zeros_like(gain_grad_ref)

    gain_grad_ref[0:1, :] += jnp.sum(grad_mixed * scaled, axis=0, keepdims=True)
    sums_ref[:, :inner] += dot_tn(read(normed_ref), grad_gate)
    sums_ref[:, inner:] += dot_tn(read(upstream_ref), mixed_low)

    @pl.when(slot == count - 1)
    def _():
        for away, piece in enumerate((piece_0, piece_1, piece_2, piece_3)):
            for half in range(2):
                rows = pl.ds(pl.multiple_of(place_ref[2 * away + half], 16), chunk)
                piece[half * chunk : (half + 1) * chunk, :] = sums_ref[rows, :].astype(LOW)


def back_kernel(
    heads,
    place_ref,
    part_ref,
    grad_ref,
    scanned_ref,
    grad_gate_ref,
    normed_ref,
    weight_ref,
    gate_weight,
    taps_ref,
    bias_ref,
    dt_ref,
    alog_ref,
    skip_ref,
    gain_grad_ref,
    normed_grad_ref,
    given_ref,
    piece_0,
    piece_1,
    piece_2,
    piece_3,
    sums_ref,
    conv_ref,
    last_ref,
    small_ref,
    pre_ref,
    extra_ref,
):
    slot = pl.program_id(0)
    inner = grad_ref.shape[1]
    width = taps_ref.shape[1]
    states = (width - inner) // 2
    chunk = sums_ref.shape[0] // 8

    @pl.when(slot == 0)
    def _():
        small_ref[...] = jnp.zeros_like(small_ref)
        pre_ref[...] = jnp.zeros_like(pre_ref)
        sums_ref[...] = jnp.zeros_like(sums_ref)
        conv_ref[...] = jnp.zeros_like(conv_ref)

    last_ref[...] = conv_ref[...]
    block = normed_ref.shape[1] // heads

    def beside(index):
        columns = slice(index * block, (index + 1) * block)
        normed = normed_ref[:, columns]
        sums_ref[columns, :] += dot_tn(normed, last_ref[...])
        grad_normed = dot_nt(grad_gate_ref[...], gate_weight[columns, :])
        grad_normed = grad_normed + dot_nt(last_ref[...], weight_ref[columns, :])
        pre_sum = jnp.sum(grad_normed * normed.astype(jnp.float32), axis=0, keepdims=True)
        pre_ref[0:1, columns] += jnp.where(slot > 0, pre_sum, 0.0)
        normed_grad_ref[:, columns] = grad_normed.astype(LOW)

    scan_backward(
        slot < pl.num_programs(0) - 1,
        beside,
        heads,
        part_ref,
        grad_ref,
        scanned_ref,
        taps_ref,
        bias_ref,
        dt_ref,
        alog_ref,
        skip_ref,
        conv_ref,
        small_ref,
    )
    @pl.when(slot == pl.num_programs(0) - 1)
    def _():
        core = place_ref[8]
        count = taps_ref.shape[0] + 1
        wide = inner + states
        extra_ref[...] = jnp.zeros_like(extra_ref)
        extra_ref[:count, :] = small_ref[:count, :wide]
        extra_ref[5:6, :inner] = small_ref[5:6, :inner]
        extra_ref[5:6, inner:] = small_ref[6:7, width:]
        extra_ref[6:7, :inner] = gain_grad_ref[0:1, :]
        extra_ref[6:7, inner:] = small_ref[5:6, width:]
        for part in range(3):
            extra_ref[7 + part : 8 + part, :] = pre_ref[0:1, part * wide : (part + 1) * wide]
        for part in range(count - 1):
            extra_ref[10:11, part * states : (part + 1) * states] = small_ref[part : part + 1, wide:width]
        extra_ref[11:12, :states] = small_ref[count - 1 : count, wide:width]
        high, rest = parts_of(extra_ref[...], 2)
        for piece in (piece_0, piece_1, piece_2, piece_3):
            piece[2 * chunk + 16 : 2 * chunk + 32, :] = high
            piece[2 * chunk + 32 :, :] = rest
            piece[2 * chunk : 2 * chunk + 16, 2 * chunk :] = jnp.zeros((16, wide - 2 * chunk), LOW)
        for away, piece in enumerate((piece_0, piece_1, piece_2, piece_3)):
            for half in range(2):
                rows = pl.ds(pl.multiple_of(place_ref[2 * away + half], 16), chunk)
                local = slice(half * chunk, (half + 1) * chunk)
                whole = slice((2 * away + half) * chunk, (2 * away + half + 1) * chunk)
                step_rows = [] if half == 0 else step_rows
                b_sums = sums_ref[rows, inner : inner + states].astype(LOW)
                c_sums = sums_ref[rows, inner + states : width].astype(LOW)
                steps = sums_ref[rows, width:]
                given_ref[whole, :] = jnp.where(core == 0, c_sums, b_sums)
                piece[local, :inner] = sums_ref[rows, :inner].astype(LOW)
                piece[local, inner : inner + states] = jnp.where(core == 0, b_sums, c_sums)
                step_rows.append(steps)
            turned = jnp.concatenate(step_rows, axis=0).T[:16]
            piece[2 * chunk : 2 * chunk + 16, : 2 * chunk] = turned.astype(LOW)


def row_block(length, width):
    return pl.BlockSpec((length, width), lambda slot, place: (slot, 0))


def core_block(length, width, half):
    def index(slot, place):
        return (2 * (slot % half) + (place[8] ^ (slot // half)), 0)

    return pl.BlockSpec((length, width), index)


def early_block(slots):
    return lambda length, width: pl.BlockSpec(
        (length, width), lambda step, place: (jnp.minimum(step, slots - 1), 0)
    )


def late_block(length, width):
    return pl.BlockSpec((length, width), lambda step, place: (jnp.maximum(step - 1, 0), 0))


def near_block(length, width, half):
    return pl.BlockSpec((length, width), lambda slot, place: (jnp.minimum(slot, half - 1), 0))


def far_block(length, width, half):
    return pl.BlockSpec((length, width), lambda slot, place: (jnp.maximum(slot - half, 0), 0))


def whole_block(shape):
    return pl.BlockSpec(shape, lambda slot, place: (0,) * len(shape))


def run_slots(kernel, slots, place, cut, whole, outs, scratch, micros, waits=(), specs=None):
    in_specs, arrays, places = [], [], []
    for array in cut:
        places.append(len(arrays))
        if isinstance(array, tuple):
            length = 2 * array[0].shape[0] // slots
            in_specs.append(near_block(length, array[0].shape[1], slots // 2))
            in_specs.append(far_block(length, array[1].shape[1], slots // 2))
            arrays.extend(array)
        else:
            spec = row_block if specs is None else specs[len(places) - 1]
            in_specs.append(spec(array.shape[0] // slots, array.shape[1]))
            arrays.append(array)
    arrays = [pltpu.with_memory_space_constraint(array, pltpu.HBM) for array in arrays]
    in_specs += [whole_block(array.shape) for array in whole]
    arrays += whole
    given = len(arrays)

    def run(place_ref, *refs):
        cut_refs = [
            (refs[at], refs[at + 1]) if isinstance(array, tuple) else refs[at]
            for at, array in zip(places, cut)
        ]
        kernel(place_ref, *cut_refs, *refs[given - len(whole) : given], *refs[given + len(waits) :])

    return pl.pallas_call(
        run,
        grid_spec=pltpu.PrefetchScalarGridSpec(
            num_scalar_prefetch=1,
            grid=(slots if specs is None else slots + 1,),
            in_specs=in_specs + [pl.BlockSpec(memory_space=pl.ANY)] * len(waits),
            out_specs=[spec for _, _, spec in outs],
            scratch_shapes=scratch,
        ),
        out_shape=[pltpu.HBM(shape, dtype) for shape, dtype, _ in outs],
        compiler_params=pltpu.CompilerParams(vmem_limit_bytes=44 << 20),
        cost_estimate=pl.CostEstimate(flops=int(micros * 1e9), bytes_accessed=1 << 20, transcendentals=0),
    )(place, *arrays, *waits)


def copies(kernel, scalars, value, others, count, waits=()):
    shape = value.shape
    return pl.pallas_call(
        kernel,
        grid_spec=pltpu.PrefetchScalarGridSpec(
            num_scalar_prefetch=len(scalars),
            grid=(count,),
            in_specs=[pl.BlockSpec(array.shape, lambda *_: (0, 0)) for array in (value, *others)]
            + [pl.BlockSpec(memory_space=pl.ANY)] * len(waits),
            out_specs=pl.BlockSpec(shape, lambda index, *_: (index, 0)),
        ),
        out_shape=jax.ShapeDtypeStruct((count * shape[0], shape[1]), LOW),
        compiler_params=pltpu.CompilerParams(vmem_limit_bytes=16 << 20),
        cost_estimate=pl.CostEstimate(flops=int(2e9), bytes_accessed=1 << 20, transcendentals=0),
    )(*scalars, value, *others, *waits)


def combine(terms, dtype, waits=()):
    shape = terms[0].shape
    steps = max(1, shape[0] // 384)

    def run(*refs):
        values = [ref[...].astype(jnp.float32) for ref in refs[: len(terms)]]
        if len(values) == 4:
            values = [values[0] + values[1], values[2] + values[3]]
        refs[-1][...] = sum(values[1:], values[0]).astype(dtype)

    block = pl.BlockSpec((shape[0] // steps, shape[1]), lambda index: (index, 0))
    return pl.pallas_call(
        run,
        grid=(steps,),
        in_specs=[block] * len(terms) + [pl.BlockSpec(memory_space=pl.ANY)] * len(waits),
        out_specs=block,
        out_shape=jax.ShapeDtypeStruct(shape, dtype),
        cost_estimate=pl.CostEstimate(flops=int(1e9), bytes_accessed=1 << 20, transcendentals=0),
    )(*terms, *waits)


def hold(values, waits):
    anywhere = pl.BlockSpec(memory_space=pl.ANY)
    return pl.pallas_call(
        lambda *refs: None,
        in_specs=[anywhere] * (len(values) + len(waits)),
        out_specs=[anywhere] * len(values),
        out_shape=[jax.ShapeDtypeStruct(value.shape, value.dtype) for value in values],
        input_output_aliases={index: index for index in range(len(values))},
    )(*values, *waits)


def small_rows(below):
    return below[:16].astype(jnp.float32) + below[16:].astype(jnp.float32)


def side_sums(terms, ranks, small, waits):
    width = terms[0].shape[1]
    rows = terms[0].shape[0] - 48 if small else terms[0].shape[0]
    own = rows // ranks

    def run(*refs):
        def total(read):
            values = [read(ref) for ref in refs[:4]]
            return (values[0] + values[1]) + (values[2] + values[3])

        out_ref = refs[-1]
        if small:
            steps = turned_columns(total(lambda ref: ref[rows : rows + 16, :rows].astype(jnp.float32))).astype(LOW)
            high, rest = parts_of(total(lambda ref: small_rows(ref[rows + 16 :, :])), 2)
        for rank in range(ranks):
            local = slice(rank * own, (rank + 1) * own)
            out_ref[rank, :own, :width] = total(lambda ref: ref[local, :].astype(jnp.float32)).astype(LOW)
            if small:
                out_ref[rank, :own, width:] = steps[local]
                out_ref[rank, own : own + 16, :width] = high
                out_ref[rank, own + 16 :, :width] = rest
                out_ref[rank, own:, width:] = jnp.zeros((32, LANES), LOW)

    whole = pl.BlockSpec(terms[0].shape, lambda: (0, 0))
    shape = (ranks, own + 32, width + LANES) if small else (ranks, own, width)
    return pl.pallas_call(
        run,
        in_specs=[whole] * 4 + [pl.BlockSpec(memory_space=pl.ANY)] * len(waits),
        out_shape=jax.ShapeDtypeStruct(shape, LOW),
        compiler_params=pltpu.CompilerParams(vmem_limit_bytes=24 << 20),
        cost_estimate=pl.CostEstimate(flops=int(2e9), bytes_accessed=1 << 20, transcendentals=0),
    )(*terms, *waits)


def owner_outputs(early, owned, rows, heads, states, sizes, waits):
    proj, inner_all, taps_shape, model = sizes
    ranks = owned.shape[0]
    inner = inner_all // ranks

    def blocks(early_ref, ref, store):
        def lanes_of(value, rank):
            lane = lax.broadcasted_iota(jnp.int32, value.shape, 1)
            value = jnp.where(lane < heads, value, 0.0)
            return pltpu.roll(value, rank * heads, 1)

        in_ref, out_ref, taps_ref, bias_ref, gain_ref, pre_ref, head_ref = store
        taps_count = taps_shape[0]
        shared, b_sum, c_sum, step_sum, dt_sum, alog_sum, skip_sum = [0.0] * 7
        for rank in range(ranks):
            lanes = slice(rank * inner, (rank + 1) * inner)
            main = ref[rank, :rows, :].astype(jnp.float32)
            extra = small_rows(ref[rank, rows:, : inner + states])
            in_ref[:, lanes] = early_ref[rank, :, :inner].astype(jnp.float32)
            out_ref[:, lanes] = early_ref[rank, :, inner:].astype(jnp.float32)
            in_ref[:, inner_all + rank * inner : inner_all + (rank + 1) * inner] = main[:, :inner]
            if rank % 2 == 0:
                b_sum = b_sum + main[:, inner : inner + states]
            else:
                c_sum = c_sum + main[:, inner : inner + states]
            step_sum = step_sum + lanes_of(main[:, inner + states :], rank)
            shared = shared + extra
            taps_ref[:, lanes] = extra[:taps_count, :inner]
            bias_ref[:, lanes] = extra[taps_count : taps_count + 1, :inner]
            gain_ref[:, lanes] = extra[6:7, :inner]
            dt_sum = dt_sum + lanes_of(extra[6:7, inner:], rank)
            alog_sum = alog_sum + lanes_of(extra[5:6, inner:], rank)
            skip_sum = skip_sum + lanes_of(lanes_sum(extra[:, :inner], heads)[5:6], rank)
        first_state = 2 * inner_all
        in_ref[:, first_state : first_state + states] = b_sum
        in_ref[:, first_state + states : first_state + 2 * states] = c_sum
        in_ref[:, first_state + 2 * states :] = step_sum[:, : proj - first_state - 2 * states]
        taps_ref[:, inner_all : inner_all + states] = shared[:taps_count, inner:]
        bias_ref[:, inner_all : inner_all + states] = shared[taps_count : taps_count + 1, inner:]
        for tap in range(taps_count):
            taps_ref[tap : tap + 1, inner_all + states :] = shared[10:11, tap * states : (tap + 1) * states]
        bias_ref[:, inner_all + states :] = shared[11:12, :states]
        wide = inner + states
        for part in range(3):
            pre_ref[:, part * wide : (part + 1) * wide] = shared[7 + part : 8 + part]
        head_ref[0:1, :] = dt_sum
        head_ref[1:2, :] = alog_sum
        head_ref[2:3, :] = skip_sum

    shapes = [(rows, proj), (rows, inner_all), taps_shape, (1, taps_shape[1]), (1, inner_all), (1, model), (8, LANES)]
    return pl.pallas_call(
        lambda early_ref, ref, *refs: blocks(early_ref, ref, refs[len(waits) :]),
        in_specs=[pl.BlockSpec(array.shape, lambda: (0, 0, 0)) for array in (early, owned)]
        + [pl.BlockSpec(memory_space=pl.ANY)] * len(waits),
        out_shape=[jax.ShapeDtypeStruct(shape, jnp.float32) for shape in shapes],
        compiler_params=pltpu.CompilerParams(vmem_limit_bytes=24 << 20),
        cost_estimate=pl.CostEstimate(flops=int(3e9), bytes_accessed=1 << 20, transcendentals=0),
    )(early, owned, *waits)


def pack_weights(in_weight, out_weight, ranks, heads):
    rows, inner_all = out_weight.shape
    inner = inner_all // ranks
    first_step = in_weight.shape[1] - ranks * heads
    states = (first_step - 2 * inner_all) // 2

    def run(in_ref, weight_ref, conv_ref, late_ref):
        steps = in_ref[:, first_step:].astype(jnp.float32)
        steps = jnp.concatenate([steps, jnp.zeros((rows, LANES - steps.shape[1]), jnp.float32)], axis=1)
        lane = lax.broadcasted_iota(jnp.int32, (rows, LANES), 1)
        for rank in range(ranks):
            own = slice(rank * inner, (rank + 1) * inner)
            late_ref[rank, :, :inner] = in_ref[:, own]
            late_ref[rank, :, inner:] = weight_ref[:, own]
            conv_ref[rank, :, :inner] = in_ref[:, inner_all + rank * inner : inner_all + (rank + 1) * inner]
            state = 2 * inner_all + (rank % 2) * states
            conv_ref[rank, :, inner : inner + states] = in_ref[:, state : state + states]
            moved = pltpu.roll(steps, (LANES - rank * heads) % LANES, 1)
            conv_ref[rank, :, inner + states :] = jnp.where(lane < heads, moved, 0.0).astype(LOW)

    return pl.pallas_call(
        run,
        out_shape=[
            jax.ShapeDtypeStruct((ranks, rows, inner + states + LANES), LOW),
            jax.ShapeDtypeStruct((ranks, rows, 2 * inner), LOW),
        ],
        cost_estimate=pl.CostEstimate(flops=int(1e9), bytes_accessed=1 << 20, transcendentals=0),
    )(in_weight, out_weight)


def pack_steps(value, start, width):
    rows = value.shape[0]

    def run(value_ref, out_ref):
        out_ref[:rows, :] = value_ref[:, start : start + width]
        steps = value_ref[:, start + width : start + width + LANES].astype(jnp.float32)
        out_ref[rows:, :rows] = steps.T[:16].astype(LOW)
        out_ref[rows:, rows:] = jnp.zeros((16, width - rows), LOW)

    return pl.pallas_call(
        run,
        out_shape=jax.ShapeDtypeStruct((rows + 16, width), LOW),
        cost_estimate=pl.CostEstimate(flops=int(1e9), bytes_accessed=1 << 20, transcendentals=0),
    )(value)


def add_states(pieces, states, start):
    count = len(pieces)
    rows, width = states.shape[0] // count, states.shape[1]

    def run(*refs):
        for index in range(count):
            own = refs[index][...].astype(jnp.float32)
            other = refs[count][index * rows : (index + 1) * rows, :].astype(jnp.float32)
            refs[count + 1 + index][...] = (own + other).astype(LOW)

    block = pl.BlockSpec((rows, width), lambda _: (0, start // width))
    return pl.pallas_call(
        run,
        grid=(1,),
        in_specs=[block] * count + [pl.BlockSpec(states.shape, lambda _: (0, 0))],
        out_specs=[block] * count,
        out_shape=[jax.ShapeDtypeStruct(piece.shape, piece.dtype) for piece in pieces],
        input_output_aliases={index: index for index in range(count)},
        cost_estimate=pl.CostEstimate(flops=int(1e9), bytes_accessed=1 << 20, transcendentals=0),
    )(*pieces, states)


def columns_of(value, start, width, waits):
    return pl.pallas_call(
        copy_kernel,
        grid=(1,),
        in_specs=[
            pl.BlockSpec((value.shape[0], LANES * (width // LANES)), lambda _: (0, start // width))
        ]
        + [pl.BlockSpec(memory_space=pl.ANY)] * len(waits),
        out_specs=pl.BlockSpec((value.shape[0], width), lambda _: (0, 0)),
        out_shape=jax.ShapeDtypeStruct((value.shape[0], width), LOW),
        cost_estimate=pl.CostEstimate(flops=int(1e9), bytes_accessed=1 << 20, transcendentals=0),
    )(value, *waits)


def body(
    sizes,
    hidden_in,
    lengths,
    cotangent,
    pre_gain,
    in_weight,
    conv_weight,
    conv_bias,
    dt_bias,
    a_log,
    skip,
    inner_gain,
    out_weight,
):
    length, model = hidden_in.shape
    rows = in_weight.shape[0]
    inner_all = out_weight.shape[1]
    heads_all = dt_bias.shape[0]
    states = (conv_weight.shape[1] - inner_all) // 2
    ranks = sizes["xi"] * sizes["yi"] * sizes["c"]
    lines = sizes["xo"] * sizes["zo"]
    slots = ranks
    tokens = slots * length
    inner = inner_all // ranks
    heads = heads_all // ranks
    head_width = inner // heads
    core = lax.axis_index("c")
    rank = (lax.axis_index("xi") * sizes["yi"] + lax.axis_index("yi")) * sizes["c"] + core
    direct = sizes["xo"] == 1 and sizes["zo"] == 4
    piece_rows = model // 4
    chunk = piece_rows // 2
    spread = (sizes["xo"], sizes["zo"], sizes["xi"], sizes["yi"] * sizes["c"] * rows)
    natural = (sizes["xo"], sizes["xi"], sizes["zo"], sizes["yi"] * sizes["c"] * rows)
    if direct:
        planes = [lax.axis_index("zo") ^ away for away in range(4)]
        starts = [half * (model // 2) + plane * chunk for plane in planes for half in range(2)]
    else:
        starts = [chunk * index for index in range(8)]
    place = jnp.stack([jnp.asarray(value, jnp.int32) for value in (*starts, core)])

    def gather_rows(piece):
        if direct:
            return [piece] + [cross(piece, LINE, away, 4) for away in range(1, 4)]
        whole = lax.all_gather(piece, LINE, axis=0, tiled=True).reshape(*spread, -1)
        whole = whole.transpose(0, 2, 1, 3, 4).reshape(model, -1)
        return [whole[index * piece_rows : (index + 1) * piece_rows] for index in range(4)]

    def scatter_rows(pieces):
        whole = jnp.concatenate(pieces, axis=0).reshape(*natural, -1)
        whole = whole.transpose(0, 2, 1, 3, 4).reshape(model, -1)
        moved = lax.all_to_all(whole, LINE, split_axis=0, concat_axis=0, tiled=True)
        return jnp.sum(moved.reshape(lines, model // lines, -1).astype(jnp.float32), axis=0).astype(LOW)

    def exchange(value):
        return lax.all_to_all(value, PLANE, split_axis=0, concat_axis=0, tiled=True)

    def gather_tokens(value):
        return lax.all_gather(value, PLANE, axis=0, tiled=True)

    def scatter_far(value):
        return lax.psum_scatter(value, PLANE, scatter_dimension=0, tiled=True)

    packed_conv, packed_late = pack_weights(in_weight, out_weight, ranks, heads)
    conv_plane = exchange(packed_conv).reshape(ranks * rows, -1)
    (late_packed,) = hold([packed_late], [conv_plane])
    late_plane = exchange(late_packed).reshape(ranks * rows, -1)
    if direct:
        conv_pieces = gather_rows(pack_steps(conv_plane, 0, inner + states))
    else:
        conv_pieces = [pack_steps(piece, 0, inner + states) for piece in gather_rows(conv_plane)]
    other_states = swap(
        jnp.concatenate([piece[:piece_rows, inner : inner + states] for piece in conv_pieces], axis=0)
    )
    (late_columns,) = hold([late_plane], conv_pieces[1:2])
    late_pieces = gather_rows(late_columns)

    stream = hidden_in.astype(jnp.float32)
    scale = lax.rsqrt(jnp.mean(stream * stream, axis=-1, keepdims=True) + EPSILON)
    valid = (jnp.arange(length) < lengths[0])[:, None]
    own_upstream = jnp.where(valid, cotangent, jnp.zeros_like(cotangent))
    own_normed = copies(norm_kernel, (), hidden_in, (pre_gain[None],), 1, (conv_plane,))
    normed = gather_tokens(own_normed)
    upstream = gather_tokens(copies(mask_kernel, (lengths,), cotangent, (), 1, (own_normed,)))

    def of_rank(value, count):
        return lax.dynamic_slice_in_dim(value, rank * count, count, axis=-1)

    taps = jnp.concatenate(
        [of_rank(conv_weight[:, :inner_all], inner), conv_weight[:, inner_all:]], axis=1
    )
    bias = jnp.concatenate([of_rank(conv_bias[:inner_all], inner), conv_bias[inner_all:]])[None]
    dt_row = jnp.pad(of_rank(dt_bias, heads), (0, LANES - heads))[None]
    alog_row = jnp.pad(of_rank(a_log, heads), (0, LANES - heads))[None]
    skip_row = jnp.repeat(of_rank(skip, heads), head_width)[None]
    gain_row = of_rank(inner_gain, inner)[None]
    params = (taps, bias, dt_row, alog_row, skip_row)
    part_width = inner + 2 * states + LANES

    part, scanned, conv_weights = run_slots(
        functools.partial(conv_kernel, heads),
        slots,
        place,
        (normed,),
        (*conv_pieces, other_states, *params),
        [
            ((tokens, part_width), jnp.float32, row_block(length, part_width)),
            ((tokens, inner), jnp.float32, row_block(length, inner)),
            ((model, part_width), LOW, whole_block((model, part_width))),
        ],
        [],
        12,
    )
    gate, grad_mixed, branch, stats, gate_weights = run_slots(
        gate_kernel,
        slots // 2,
        place,
        (normed, upstream, scanned),
        (*late_pieces, gain_row),
        [
            ((tokens, inner), jnp.float32, row_block(2 * length, inner)),
            ((tokens, inner), jnp.float32, row_block(2 * length, inner)),
            ((tokens, model), LOW, row_block(2 * length, model)),
            ((2 * slots, length), jnp.float32, whole_block((2 * slots, length))),
            ((model, inner), LOW, whole_block((model, inner))),
        ],
        [pltpu.VMEM((model, inner), LOW)],
        14,
    )
    stats = stats + swap(stats)
    far = [cross(stats, ("xi", "yi"), away, 4) for away in (3, 1, 2)]
    stats = (stats + far[0]) + (far[1] + far[2])
    branch_own = scatter_far(branch)
    squares = lax.dynamic_index_in_dim(stats, rank, axis=0, keepdims=False)
    inner_scale = lax.rsqrt(squares / inner_all + EPSILON)[:, None]
    output = jnp.where(valid, stream + branch_own * inner_scale, 0.0).astype(LOW)

    piece_shape = (piece_rows, 2 * inner)
    grad_gate, grad_scanned, gain_grad, *early = run_slots(
        functools.partial(early_kernel, inner_all),
        slots // 2,
        place,
        (normed, upstream, scanned, gate, grad_mixed),
        (stats, gain_row),
        [
            ((tokens, inner), LOW, row_block(2 * length, inner)),
            ((tokens, inner), jnp.float32, row_block(2 * length, inner)),
            ((8, inner), jnp.float32, whole_block((8, inner))),
        ]
        + [(piece_shape, LOW, whole_block(piece_shape))] * 4,
        [pltpu.VMEM((model, 2 * inner), jnp.float32)],
        16,
    )
    width = taps.shape[1]
    piece_shape = (piece_rows + 48, inner + states)
    held = run_slots(
        functools.partial(back_kernel, heads),
        slots,
        place,
        (part, grad_scanned, scanned, grad_gate, normed),
        (conv_weights, gate_weights, *params, gain_grad),
        [
            ((tokens, model), LOW, late_block(length, model)),
            ((model, states), LOW, whole_block((model, states))),
        ]
        + [(piece_shape, LOW, whole_block(piece_shape))] * 4,
        [
            pltpu.VMEM((model, part_width), jnp.float32),
            pltpu.VMEM((length, part_width), LOW),
            pltpu.VMEM((length, part_width), LOW),
            pltpu.VMEM((8, part_width), jnp.float32),
            pltpu.VMEM((8, model), jnp.float32),
            pltpu.VMEM((16, inner + states), jnp.float32),
        ],
        30,
        specs=[early_block(slots)] * 3 + [late_block] * 2,
    )
    if direct:
        early_moved = [cross(early[away], LINE, away, 4) for away in (2, 3, 1)]
        held = hold(held, [*early_moved, branch_own])
    grad_normed, given, *pieces = held
    pieces = add_states(pieces, swap(given), inner)
    if direct:
        conv_moved = [cross(pieces[away], LINE, away, 4) for away in (1, 2, 3)]
    else:
        conv_moved = []
    grad_own = scatter_far(grad_normed) * pre_gain
    along = jnp.mean(grad_own * stream, axis=-1, keepdims=True)
    grad_stream = grad_own * scale - stream * (scale**3 * along)
    grad_hidden = (own_upstream.astype(jnp.float32) + grad_stream).astype(LOW)

    if direct:
        early_owned = exchange(side_sums([early[0], *early_moved], ranks, False, pieces[:1]))
        owned = exchange(side_sums([pieces[0], *conv_moved], ranks, True, (early_owned,)))
    else:
        below = jnp.concatenate(parts_of(lax.psum(small_rows(pieces[0][piece_rows + 16 :]), LINE), 2), axis=0)
        below = jnp.pad(jnp.broadcast_to(below[None], (ranks, *below.shape)), ((0, 0), (0, 0), (0, LANES)))

        def padded(value):
            return jnp.pad(value.reshape(ranks, rows, -1), ((0, 0), (0, -rows % 16), (0, 0)))

        def with_steps(piece):
            steps = piece[piece_rows : piece_rows + 16, :piece_rows].T
            return jnp.concatenate([piece[:piece_rows], jnp.pad(steps, ((0, 0), (0, LANES - 16)))], axis=1)

        early_owned = exchange(padded(scatter_rows(early)))
        conv = padded(scatter_rows([with_steps(piece) for piece in pieces]))
        owned = exchange(jnp.concatenate([conv, below], axis=1))
    sizes_out = (in_weight.shape[1], inner_all, conv_weight.shape, model)
    owned_in, owned_out, taps_grad, bias_grad, gain_grads, pre_grad, head_grads = owner_outputs(
        early_owned, owned, rows + -rows % 16, heads, states, sizes_out, (output,)
    )
    return (
        output,
        grad_hidden,
        pre_grad[0] / pre_gain,
        owned_in[:rows],
        taps_grad,
        bias_grad[0],
        head_grads[0, :heads_all],
        head_grads[1, :heads_all],
        head_grads[2, :heads_all],
        gain_grads[0],
        owned_out[:rows],
    )


def solution(mesh):
    dp, fsdp = mesh.shape["dp"], mesh.shape["fsdp"]
    shape = (dp // 2, 2, fsdp // 4, 2, 2)
    fine = Mesh(mesh.devices.reshape(shape), EVERY)
    split, kept = P(EVERY, None), P()
    in_specs = (split, P(EVERY), split, kept, split, kept, kept, kept, kept, kept, kept, split)
    out_specs = (split, split, kept, split, kept, kept, kept, kept, kept, kept, split)
    return jax.shard_map(
        functools.partial(body, dict(zip(EVERY, shape))),
        mesh=fine,
        in_specs=in_specs,
        out_specs=out_specs,
        check_vma=False,
    )
```

```python
import functools

import jax
import jax.numpy as jnp
from jax import lax
from jax.experimental import pallas as pl
from jax.experimental.pallas import tpu as pltpu
from jax.sharding import Mesh
from jax.sharding import PartitionSpec as P

EPSILON = 1e-05
LANES = 128
LOW = jnp.bfloat16
LOG2E = 1.4426950408889634

PLANE = ("xi", "yi", "c")
LINE = ("xo", "zo")
EVERY = ("xo", "xi", "zo", "yi", "c")


def swap(value):
    return lax.ppermute(value, "c", [(0, 1), (1, 0)])


def cross(value, axes, distance, count):
    return lax.ppermute(value, axes, [(i, i ^ distance) for i in range(count)])


def shift_down(value, rows):
    if rows == 0:
        return value
    index = lax.broadcasted_iota(jnp.int32, value.shape, 0)
    return jnp.where(index >= rows, pltpu.roll(value, rows, 0), 0.0)


def shift_up(value, rows):
    if rows == 0:
        return value
    length = value.shape[0]
    index = lax.broadcasted_iota(jnp.int32, value.shape, 0)
    return jnp.where(index < length - rows, pltpu.roll(value, length - rows, 0), 0.0)


def softplus(value):
    return jnp.maximum(value, 0.0) + jnp.log1p(jnp.exp(-jnp.abs(value)))


def dot_low(left, right):
    return jnp.dot(left, right, preferred_element_type=jnp.float32)


def dot_nt(left, right):
    return lax.dot_general(left, right, (((1,), (1,)), ((), ())), preferred_element_type=jnp.float32)


def dot_tn(left, right):
    return lax.dot_general(left, right, (((0,), (0,)), ((), ())), preferred_element_type=jnp.float32)


def parts_of(value, count):
    terms = []
    for _ in range(count):
        terms.append(value.astype(LOW))
        value = value - terms[-1].astype(jnp.float32)
    return terms


def convolve(conv_input, taps, bias):
    kernel_taps = taps.shape[0]
    summed = bias
    for tap in range(kernel_taps):
        summed = summed + taps[tap : tap + 1] * shift_down(conv_input, kernel_taps - 1 - tap)
    return summed


def triangle(length, lower):
    row = lax.broadcasted_iota(jnp.int32, (length, length), 0)
    column = lax.broadcasted_iota(jnp.int32, (length, length), 1)
    return row >= column if lower else row <= column


def cumulate(mask, value, count):
    mask = mask.astype(LOW)
    return sum(dot_low(mask, term) for term in parts_of(value, count))


def pair_lanes(value, pair, first):
    return jnp.where(first, value[:, 2 * pair : 2 * pair + 1], value[:, 2 * pair + 1 : 2 * pair + 2])


def lanes_sum(value, head_count):
    inner = value.shape[1]
    lane = lax.broadcasted_iota(jnp.int32, (inner, LANES), 0)
    head = lax.broadcasted_iota(jnp.int32, (inner, LANES), 1)
    start = head * (inner // head_count)
    member = jnp.logical_and(lane >= start, lane < start + inner // head_count).astype(LOW)
    return sum(dot_low(term, member) for term in parts_of(value, 2))


def turned_columns(rows):
    blank = jnp.zeros((LANES - rows.shape[0], rows.shape[1]), rows.dtype)
    return jnp.concatenate([rows, blank], axis=0).T


def read(ref):
    if not isinstance(ref, tuple):
        return ref[...]
    near, far = ref
    return jnp.where(pl.program_id(0) < pl.num_programs(0) // 2, near[...], far[...])


def row_spread(row):
    return jnp.broadcast_to(row, (8, row.shape[1])).T[:, :1]


def scan_forward(heads, part, taps_ref, bias_ref, dt_ref, alog_ref, skip_ref, out_ref):
    inner = out_ref.shape[1]
    length = out_ref.shape[0]
    width = taps_ref.shape[1]
    states = (width - inner) // 2
    conv_low = jax.nn.silu(convolve(part[:, :width], taps_ref[...], bias_ref[...])).astype(LOW)
    step = softplus(part[:, width:] + dt_ref[...])
    lower = triangle(length, True)
    cumulative = cumulate(lower, step * (-jnp.exp(alog_ref[...]) * LOG2E), 3)
    across = cumulative.T
    scores = dot_nt(conv_low[:, inner + states :], conv_low[:, inner : inner + states])
    scores = jnp.where(lower, scores, 0.0)
    first = lax.broadcasted_iota(jnp.int32, (length, LANES), 1) < inner // heads
    for pair in range(heads // 2):
        lanes = slice(pair * LANES, (pair + 1) * LANES)
        values = conv_low[:, lanes].astype(jnp.float32)
        scaled = (values * pair_lanes(step, pair, first)).astype(LOW)
        sums = []
        for head in (2 * pair, 2 * pair + 1):
            spread = cumulative[:, head : head + 1] - across[head : head + 1, :]
            mixing = scores * jnp.exp2(jnp.minimum(spread, 0.0))
            sums.append(dot_low(mixing.astype(LOW), scaled))
        out_ref[:, lanes] = jnp.where(first, sums[0], sums[1]) + skip_ref[:, lanes] * values


def norm_kernel(hidden_ref, gain_ref, *refs):
    stream = hidden_ref[...].astype(jnp.float32)
    scale = lax.rsqrt(jnp.mean(stream * stream, axis=-1, keepdims=True) + EPSILON)
    refs[-1][...] = (stream * scale * gain_ref[...]).astype(LOW)


def mask_kernel(lengths_ref, cotangent_ref, *refs):
    row = lax.broadcasted_iota(jnp.int32, cotangent_ref.shape, 0)
    own = cotangent_ref[...].astype(jnp.float32)
    refs[-1][...] = jnp.where(row < lengths_ref[0], own, 0.0).astype(LOW)


def hidden_kernel(grad_ref, hidden_ref, upstream_ref, gain_ref, out_ref):
    stream = hidden_ref[...].astype(jnp.float32)
    scale = lax.rsqrt(jnp.mean(stream * stream, axis=-1, keepdims=True) + EPSILON)
    grad = grad_ref[...].astype(jnp.float32) * gain_ref[...]
    along = jnp.mean(grad * stream, axis=-1, keepdims=True)
    grad_stream = grad * scale - stream * (scale * scale * scale * along)
    out_ref[...] = (upstream_ref[...].astype(jnp.float32) + grad_stream).astype(LOW)


def hidden_gradient(grad, hidden, upstream, gain):
    length, width = hidden.shape
    block = pl.BlockSpec((length // 2, width), lambda index: (index, 0))
    return pl.pallas_call(
        hidden_kernel,
        grid=(2,),
        in_specs=[block] * 3 + [pl.BlockSpec(gain.shape, lambda index: (0, 0))],
        out_specs=block,
        out_shape=jax.ShapeDtypeStruct((length, width), LOW),
        cost_estimate=pl.CostEstimate(flops=int(2e9), bytes_accessed=1 << 20, transcendentals=0),
    )(grad, hidden, upstream, gain)


def copy_kernel(value_ref, *refs):
    refs[-1][...] = value_ref[...]


def conv_kernel(
    heads,
    place_ref,
    normed_ref,
    piece_0,
    piece_1,
    piece_2,
    piece_3,
    other_ref,
    taps_ref,
    bias_ref,
    dt_ref,
    alog_ref,
    skip_ref,
    part_ref,
    scanned_ref,
    weight_ref,
):
    inner = scanned_ref.shape[1]
    states = other_ref.shape[1]
    chunk = weight_ref.shape[0] // 8

    @pl.when(pl.program_id(0) == 0)
    def _():
        core = place_ref[8]
        for away, piece in enumerate((piece_0, piece_1, piece_2, piece_3)):
            steps = turned_columns(piece[2 * chunk :, : 2 * chunk].astype(jnp.float32)).astype(LOW)
            for half in range(2):
                rows = pl.ds(pl.multiple_of(place_ref[2 * away + half], 16), chunk)
                local = slice(half * chunk, (half + 1) * chunk)
                own = piece[local, inner : inner + states]
                other = other_ref[(2 * away + half) * chunk : (2 * away + half + 1) * chunk, :]
                weight_ref[rows, :inner] = piece[local, :inner]
                weight_ref[rows, inner : inner + states] = jnp.where(core == 0, own, other)
                weight_ref[rows, inner + states : inner + 2 * states] = jnp.where(core == 0, other, own)
                weight_ref[rows, inner + 2 * states :] = steps[local]

    part = dot_low(read(normed_ref), weight_ref[...])
    part_ref[...] = part
    scan_forward(heads, part, taps_ref, bias_ref, dt_ref, alog_ref, skip_ref, scanned_ref)


def scan_backward(
    counts,
    beside,
    heads,
    part_ref,
    grad_ref,
    scanned_ref,
    taps_ref,
    bias_ref,
    dt_ref,
    alog_ref,
    skip_ref,
    out_ref,
    small_ref,
):
    inner = grad_ref.shape[1]
    length = grad_ref.shape[0]
    width = taps_ref.shape[1]
    states = (width - inner) // 2
    kernel_taps = taps_ref.shape[0]
    conv_input = part_ref[:, :width]
    summed = convolve(conv_input, taps_ref[...], bias_ref[...])
    gate = jax.nn.sigmoid(summed)
    conv_low = (summed * gate).astype(LOW)
    slope = gate * (1.0 + summed * (1.0 - gate))
    raw = part_ref[:, width:] + dt_ref[...]
    step = softplus(raw)
    decay = -jnp.exp(alog_ref[...])
    lower = triangle(length, True)
    cumulative = cumulate(lower, step * (decay * LOG2E), 3)
    across = cumulative.T
    b_rows = conv_low[:, inner : inner + states]
    c_rows = conv_low[:, inner + states :]
    scores = jnp.where(lower, dot_nt(c_rows, b_rows), 0.0)
    values = conv_low[:, :inner].astype(jnp.float32)
    half = inner // heads
    first = lax.broadcasted_iota(jnp.int32, (length, LANES), 1) < half
    steps = jnp.concatenate([pair_lanes(step, pair, first) for pair in range(heads // 2)], axis=1)
    scaled = (values * steps).astype(LOW)
    grad = grad_ref[...]
    grad_low = grad.astype(LOW)
    grad_across = grad.T.astype(LOW)
    upper_rows = lax.broadcasted_iota(jnp.int32, (LANES, length), 0) < half
    grad_scores = jnp.zeros((length, length), jnp.float32)
    moved = []
    for pair in range(heads // 2):
        lanes = slice(pair * LANES, (pair + 1) * LANES)
        sums = []
        for head in (2 * pair, 2 * pair + 1):
            spread = cumulative[:, head : head + 1] - across[head : head + 1, :]
            decays = jnp.exp2(jnp.minimum(spread, 0.0))
            mixing = (scores * decays).astype(LOW)
            own = first if head % 2 == 0 else jnp.logical_not(first)
            grad_own = jnp.where(own, grad[:, lanes], 0.0).astype(LOW)
            beside(head)
            grad_scores = grad_scores + dot_nt(grad_own, scaled[:, lanes]) * decays
            sums.append(dot_low(grad_across[lanes], mixing))
        moved.append(jnp.where(upper_rows, sums[0], sums[1]).T)
    grad_scaled = jnp.concatenate(moved, axis=1)
    within = scanned_ref[...] - skip_ref[...] * values
    grad_cumulative = lanes_sum(
        grad_low.astype(jnp.float32) * within - scaled.astype(jnp.float32) * grad_scaled, heads
    )
    grad_rate = cumulate(triangle(length, False), grad_cumulative, 3)
    grad_step = grad_rate * decay + lanes_sum(values * grad_scaled, heads)
    grad_raw = grad_step * jax.nn.sigmoid(raw)
    grad_values = steps * grad_scaled + skip_ref[...] * grad
    scores_low = jnp.where(lower, grad_scores, 0.0).astype(LOW)
    grad_c = dot_low(scores_low, b_rows)
    grad_b = dot_low(c_rows.T, scores_low).T
    grad_summed = jnp.concatenate([grad_values, grad_b, grad_c], axis=1) * slope
    grad_input = jnp.zeros_like(grad_summed)
    rows = []
    for tap in range(kernel_taps):
        away = kernel_taps - 1 - tap
        shifted = shift_up(grad_summed, away)
        grad_input = grad_input + taps_ref[tap : tap + 1, :] * shifted
        rows.append(jnp.sum(shifted * conv_input, axis=0, keepdims=True))
    rows.append(jnp.sum(grad_summed, axis=0, keepdims=True))
    out_ref[:, :width] = grad_input.astype(LOW)
    out_ref[:, width:] = grad_raw.astype(LOW)

    def counted(row):
        return jnp.where(counts, row, 0.0)

    for index, row in enumerate(rows):
        small_ref[index : index + 1, :width] += counted(row)
    small_ref[5:6, :inner] += counted(jnp.sum(grad * values, axis=0, keepdims=True))
    small_ref[5:6, width:] += counted(jnp.sum(grad_raw, axis=0, keepdims=True))
    small_ref[6:7, width:] += counted(jnp.sum(grad_rate * step, axis=0, keepdims=True) * decay)


def gate_kernel(
    place_ref,
    normed_ref,
    upstream_ref,
    scanned_ref,
    piece_0,
    piece_1,
    piece_2,
    piece_3,
    gain_ref,
    gate_ref,
    mixed_ref,
    branch_ref,
    stats_ref,
    gate_weight,
    out_weight,
):
    inner = gain_ref.shape[1]
    length = gate_ref.shape[0]
    chunk = piece_0.shape[0] // 2
    slot = pl.program_id(0)

    @pl.when(slot == 0)
    def _():
        for away, piece in enumerate((piece_0, piece_1, piece_2, piece_3)):
            for half in range(2):
                rows = pl.ds(pl.multiple_of(place_ref[2 * away + half], 16), chunk)
                local = slice(half * chunk, (half + 1) * chunk)
                gate_weight[rows, :] = piece[local, :inner]
                out_weight[rows, :] = piece[local, inner:]

    gate = dot_low(read(normed_ref), gate_weight[...])
    gated = scanned_ref[...] * jax.nn.silu(gate)
    gained = gated * gain_ref[...]
    grad_mixed = dot_low(read(upstream_ref), out_weight[...])
    gate_ref[...] = gate
    mixed_ref[...] = grad_mixed
    branch_ref[...] = dot_nt(gained.astype(LOW), out_weight[...]).astype(LOW)
    squares = jnp.sum(gated * gated, axis=1, keepdims=True)
    products = jnp.sum(grad_mixed * gained, axis=1, keepdims=True)
    lane = lax.broadcasted_iota(jnp.int32, (length, LANES), 1)
    turned = jnp.where(lane == 0, squares, products).T
    span = stats_ref.shape[1]
    for part in range(length // span):
        row = slot * (length // span) + part
        lanes = slice(part * span, (part + 1) * span)
        stats_ref[pl.ds(row, 1), :] = turned[0:1, lanes]
        stats_ref[pl.ds(stats_ref.shape[0] // 2 + row, 1), :] = turned[1:2, lanes]


def early_kernel(
    inner_all,
    place_ref,
    normed_ref,
    upstream_ref,
    scanned_ref,
    gate_ref,
    mixed_ref,
    stats_ref,
    gain_ref,
    grad_gate_ref,
    grad_scanned_ref,
    gain_grad_ref,
    piece_0,
    piece_1,
    piece_2,
    piece_3,
    sums_ref,
):
    slot = pl.program_id(0)
    inner = gain_ref.shape[1]
    chunk = piece_0.shape[0] // 2
    count = pl.num_programs(0)
    scales, slopes = [], []
    span = gate_ref.shape[0] // stats_ref.shape[1]
    for part in range(span):
        row = slot * span + part
        scale = lax.rsqrt(stats_ref[pl.ds(row, 1), :] / inner_all + EPSILON)
        slope = scale * scale * scale * stats_ref[pl.ds(stats_ref.shape[0] // 2 + row, 1), :] / inner_all
        scales.append(row_spread(scale))
        slopes.append(row_spread(slope))
    scale, slope = jnp.concatenate(scales, axis=0), jnp.concatenate(slopes, axis=0)
    gate = gate_ref[...]
    scanned = scanned_ref[...]
    sigmoid = jax.nn.sigmoid(gate)
    silu = gate * sigmoid
    gated = scanned * silu
    scaled = gated * scale
    mixed_low = (scaled * gain_ref[...]).astype(LOW)
    grad_mixed = mixed_ref[...]
    grad_gated = grad_mixed * gain_ref[...] * scale - gated * slope
    grad_gate = (grad_gated * scanned * (sigmoid * (1.0 + gate * (1.0 - sigmoid)))).astype(LOW)
    grad_gate_ref[...] = grad_gate
    grad_scanned_ref[...] = grad_gated * silu

    @pl.when(slot == 0)
    def _():
        sums_ref[...] = jnp.zeros_like(sums_ref)
        gain_grad_ref[...] = jnp.zeros_like(gain_grad_ref)

    gain_grad_ref[0:1, :] += jnp.sum(grad_mixed * scaled, axis=0, keepdims=True)
    sums_ref[:, :inner] += dot_tn(read(normed_ref), grad_gate)
    sums_ref[:, inner:] += dot_tn(read(upstream_ref), mixed_low)

    @pl.when(slot == count - 1)
    def _():
        for away, piece in enumerate((piece_0, piece_1, piece_2, piece_3)):
            for half in range(2):
                rows = pl.ds(pl.multiple_of(place_ref[2 * away + half], 16), chunk)
                piece[half * chunk : (half + 1) * chunk, :] = sums_ref[rows, :].astype(LOW)


def back_kernel(
    heads,
    place_ref,
    part_ref,
    grad_ref,
    scanned_ref,
    grad_gate_ref,
    normed_ref,
    weight_ref,
    gate_weight,
    taps_ref,
    bias_ref,
    dt_ref,
    alog_ref,
    skip_ref,
    gain_grad_ref,
    normed_grad_ref,
    given_ref,
    piece_0,
    piece_1,
    piece_2,
    piece_3,
    sums_ref,
    conv_ref,
    last_ref,
    small_ref,
    pre_ref,
    extra_ref,
):
    slot = pl.program_id(0)
    inner = grad_ref.shape[1]
    width = taps_ref.shape[1]
    states = (width - inner) // 2
    chunk = sums_ref.shape[0] // 8

    @pl.when(slot == 0)
    def _():
        small_ref[...] = jnp.zeros_like(small_ref)
        pre_ref[...] = jnp.zeros_like(pre_ref)
        sums_ref[...] = jnp.zeros_like(sums_ref)
        conv_ref[...] = jnp.zeros_like(conv_ref)

    last_ref[...] = conv_ref[...]
    block = normed_ref.shape[1] // heads

    def beside(index):
        columns = slice(index * block, (index + 1) * block)
        normed = normed_ref[:, columns]
        sums_ref[columns, :] += dot_tn(normed, last_ref[...])
        grad_normed = dot_nt(grad_gate_ref[...], gate_weight[columns, :])
        grad_normed = grad_normed + dot_nt(last_ref[...], weight_ref[columns, :])
        pre_sum = jnp.sum(grad_normed * normed.astype(jnp.float32), axis=0, keepdims=True)
        pre_ref[0:1, columns] += jnp.where(slot > 0, pre_sum, 0.0)
        normed_grad_ref[:, columns] = grad_normed.astype(LOW)

    scan_backward(
        slot < pl.num_programs(0) - 1,
        beside,
        heads,
        part_ref,
        grad_ref,
        scanned_ref,
        taps_ref,
        bias_ref,
        dt_ref,
        alog_ref,
        skip_ref,
        conv_ref,
        small_ref,
    )
    @pl.when(slot == pl.num_programs(0) - 1)
    def _():
        core = place_ref[8]
        count = taps_ref.shape[0] + 1
        wide = inner + states
        extra_ref[...] = jnp.zeros_like(extra_ref)
        extra_ref[:count, :] = small_ref[:count, :wide]
        extra_ref[5:6, :inner] = small_ref[5:6, :inner]
        extra_ref[5:6, inner:] = small_ref[6:7, width:]
        extra_ref[6:7, :inner] = gain_grad_ref[0:1, :]
        extra_ref[6:7, inner:] = small_ref[5:6, width:]
        for part in range(3):
            extra_ref[7 + part : 8 + part, :] = pre_ref[0:1, part * wide : (part + 1) * wide]
        for part in range(count - 1):
            extra_ref[10:11, part * states : (part + 1) * states] = small_ref[part : part + 1, wide:width]
        extra_ref[11:12, :states] = small_ref[count - 1 : count, wide:width]
        high, rest = parts_of(extra_ref[...], 2)
        for piece in (piece_0, piece_1, piece_2, piece_3):
            piece[2 * chunk + 16 : 2 * chunk + 32, :] = high
            piece[2 * chunk + 32 :, :] = rest
            piece[2 * chunk : 2 * chunk + 16, 2 * chunk :] = jnp.zeros((16, wide - 2 * chunk), LOW)
        for away, piece in enumerate((piece_0, piece_1, piece_2, piece_3)):
            for half in range(2):
                rows = pl.ds(pl.multiple_of(place_ref[2 * away + half], 16), chunk)
                local = slice(half * chunk, (half + 1) * chunk)
                whole = slice((2 * away + half) * chunk, (2 * away + half + 1) * chunk)
                step_rows = [] if half == 0 else step_rows
                b_sums = sums_ref[rows, inner : inner + states].astype(LOW)
                c_sums = sums_ref[rows, inner + states : width].astype(LOW)
                steps = sums_ref[rows, width:]
                given_ref[whole, :] = jnp.where(core == 0, c_sums, b_sums)
                piece[local, :inner] = sums_ref[rows, :inner].astype(LOW)
                piece[local, inner : inner + states] = jnp.where(core == 0, b_sums, c_sums)
                step_rows.append(steps)
            turned = jnp.concatenate(step_rows, axis=0).T[:16]
            piece[2 * chunk : 2 * chunk + 16, : 2 * chunk] = turned.astype(LOW)


def row_block(length, width):
    return pl.BlockSpec((length, width), lambda slot, place: (slot, 0))


def core_block(length, width, half):
    def index(slot, place):
        return (2 * (slot % half) + (place[8] ^ (slot // half)), 0)

    return pl.BlockSpec((length, width), index)


def early_block(slots):
    return lambda length, width: pl.BlockSpec(
        (length, width), lambda step, place: (jnp.minimum(step, slots - 1), 0)
    )


def late_block(length, width):
    return pl.BlockSpec((length, width), lambda step, place: (jnp.maximum(step - 1, 0), 0))


def near_block(length, width, half):
    return pl.BlockSpec((length, width), lambda slot, place: (jnp.minimum(slot, half - 1), 0))


def far_block(length, width, half):
    return pl.BlockSpec((length, width), lambda slot, place: (jnp.maximum(slot - half, 0), 0))


def whole_block(shape):
    return pl.BlockSpec(shape, lambda slot, place: (0,) * len(shape))


def run_slots(kernel, slots, place, cut, whole, outs, scratch, micros, waits=(), specs=None):
    in_specs, arrays, places = [], [], []
    for array in cut:
        places.append(len(arrays))
        if isinstance(array, tuple):
            length = 2 * array[0].shape[0] // slots
            in_specs.append(near_block(length, array[0].shape[1], slots // 2))
            in_specs.append(far_block(length, array[1].shape[1], slots // 2))
            arrays.extend(array)
        else:
            spec = row_block if specs is None else specs[len(places) - 1]
            in_specs.append(spec(array.shape[0] // slots, array.shape[1]))
            arrays.append(array)
    arrays = [pltpu.with_memory_space_constraint(array, pltpu.HBM) for array in arrays]
    in_specs += [whole_block(array.shape) for array in whole]
    arrays += whole
    given = len(arrays)

    def run(place_ref, *refs):
        cut_refs = [
            (refs[at], refs[at + 1]) if isinstance(array, tuple) else refs[at]
            for at, array in zip(places, cut)
        ]
        kernel(place_ref, *cut_refs, *refs[given - len(whole) : given], *refs[given + len(waits) :])

    return pl.pallas_call(
        run,
        grid_spec=pltpu.PrefetchScalarGridSpec(
            num_scalar_prefetch=1,
            grid=(slots if specs is None else slots + 1,),
            in_specs=in_specs + [pl.BlockSpec(memory_space=pl.ANY)] * len(waits),
            out_specs=[spec for _, _, spec in outs],
            scratch_shapes=scratch,
        ),
        out_shape=[pltpu.HBM(shape, dtype) for shape, dtype, _ in outs],
        compiler_params=pltpu.CompilerParams(vmem_limit_bytes=44 << 20),
        cost_estimate=pl.CostEstimate(flops=int(micros * 1e9), bytes_accessed=1 << 20, transcendentals=0),
    )(place, *arrays, *waits)


def copies(kernel, scalars, value, others, count, waits=()):
    shape = value.shape
    return pl.pallas_call(
        kernel,
        grid_spec=pltpu.PrefetchScalarGridSpec(
            num_scalar_prefetch=len(scalars),
            grid=(count,),
            in_specs=[pl.BlockSpec(array.shape, lambda *_: (0, 0)) for array in (value, *others)]
            + [pl.BlockSpec(memory_space=pl.ANY)] * len(waits),
            out_specs=pl.BlockSpec(shape, lambda index, *_: (index, 0)),
        ),
        out_shape=jax.ShapeDtypeStruct((count * shape[0], shape[1]), LOW),
        compiler_params=pltpu.CompilerParams(vmem_limit_bytes=16 << 20),
        cost_estimate=pl.CostEstimate(flops=int(2e9), bytes_accessed=1 << 20, transcendentals=0),
    )(*scalars, value, *others, *waits)


def combine(terms, dtype, waits=()):
    shape = terms[0].shape
    steps = max(1, shape[0] // 384)

    def run(*refs):
        values = [ref[...].astype(jnp.float32) for ref in refs[: len(terms)]]
        if len(values) == 4:
            values = [values[0] + values[1], values[2] + values[3]]
        refs[-1][...] = sum(values[1:], values[0]).astype(dtype)

    block = pl.BlockSpec((shape[0] // steps, shape[1]), lambda index: (index, 0))
    return pl.pallas_call(
        run,
        grid=(steps,),
        in_specs=[block] * len(terms) + [pl.BlockSpec(memory_space=pl.ANY)] * len(waits),
        out_specs=block,
        out_shape=jax.ShapeDtypeStruct(shape, dtype),
        cost_estimate=pl.CostEstimate(flops=int(1e9), bytes_accessed=1 << 20, transcendentals=0),
    )(*terms, *waits)


def hold(values, waits):
    anywhere = pl.BlockSpec(memory_space=pl.ANY)
    return pl.pallas_call(
        lambda *refs: None,
        in_specs=[anywhere] * (len(values) + len(waits)),
        out_specs=[anywhere] * len(values),
        out_shape=[jax.ShapeDtypeStruct(value.shape, value.dtype) for value in values],
        input_output_aliases={index: index for index in range(len(values))},
    )(*values, *waits)


def small_rows(below):
    return below[:16].astype(jnp.float32) + below[16:].astype(jnp.float32)


def side_sums(terms, ranks, small, waits):
    width = terms[0].shape[1]
    rows = terms[0].shape[0] - 48 if small else terms[0].shape[0]
    own = rows // ranks

    def run(*refs):
        def total(read):
            values = [read(ref) for ref in refs[:4]]
            return (values[0] + values[1]) + (values[2] + values[3])

        out_ref = refs[-1]
        if small:
            steps = turned_columns(total(lambda ref: ref[rows : rows + 16, :rows].astype(jnp.float32))).astype(LOW)
            high, rest = parts_of(total(lambda ref: small_rows(ref[rows + 16 :, :])), 2)
        for rank in range(ranks):
            local = slice(rank * own, (rank + 1) * own)
            out_ref[rank, :own, :width] = total(lambda ref: ref[local, :].astype(jnp.float32)).astype(LOW)
            if small:
                out_ref[rank, :own, width:] = steps[local]
                out_ref[rank, own : own + 16, :width] = high
                out_ref[rank, own + 16 :, :width] = rest
                out_ref[rank, own:, width:] = jnp.zeros((32, LANES), LOW)

    whole = pl.BlockSpec(terms[0].shape, lambda: (0, 0))
    shape = (ranks, own + 32, width + LANES) if small else (ranks, own, width)
    return pl.pallas_call(
        run,
        in_specs=[whole] * 4 + [pl.BlockSpec(memory_space=pl.ANY)] * len(waits),
        out_shape=jax.ShapeDtypeStruct(shape, LOW),
        compiler_params=pltpu.CompilerParams(vmem_limit_bytes=24 << 20),
        cost_estimate=pl.CostEstimate(flops=int(2e9), bytes_accessed=1 << 20, transcendentals=0),
    )(*terms, *waits)


def owner_outputs(early, owned, gain, rows, heads, states, sizes, waits):
    proj, inner_all, taps_shape, model = sizes
    ranks = owned.shape[0]
    inner = inner_all // ranks

    def blocks(early_ref, ref, divisor_ref, store):
        def lanes_of(value, rank):
            lane = lax.broadcasted_iota(jnp.int32, value.shape, 1)
            value = jnp.where(lane < heads, value, 0.0)
            return pltpu.roll(value, rank * heads, 1)

        in_ref, out_ref, taps_ref, bias_ref, gain_ref, pre_ref, head_ref = store
        taps_count = taps_shape[0]
        shared, b_sum, c_sum, step_sum, dt_sum, alog_sum, skip_sum = [0.0] * 7
        for rank in range(ranks):
            lanes = slice(rank * inner, (rank + 1) * inner)
            main = ref[rank, :rows, :].astype(jnp.float32)
            extra = small_rows(ref[rank, rows:, : inner + states])
            in_ref[:, lanes] = early_ref[rank, :, :inner].astype(jnp.float32)
            out_ref[:, lanes] = early_ref[rank, :, inner:].astype(jnp.float32)
            in_ref[:, inner_all + rank * inner : inner_all + (rank + 1) * inner] = main[:, :inner]
            if rank % 2 == 0:
                b_sum = b_sum + main[:, inner : inner + states]
            else:
                c_sum = c_sum + main[:, inner : inner + states]
            step_sum = step_sum + lanes_of(main[:, inner + states :], rank)
            shared = shared + extra
            taps_ref[:, lanes] = extra[:taps_count, :inner]
            bias_ref[:, lanes] = extra[taps_count : taps_count + 1, :inner]
            gain_ref[:, lanes] = extra[6:7, :inner]
            dt_sum = dt_sum + lanes_of(extra[6:7, inner:], rank)
            alog_sum = alog_sum + lanes_of(extra[5:6, inner:], rank)
            skip_sum = skip_sum + lanes_of(lanes_sum(extra[:, :inner], heads)[5:6], rank)
        first_state = 2 * inner_all
        in_ref[:, first_state : first_state + states] = b_sum
        in_ref[:, first_state + states : first_state + 2 * states] = c_sum
        in_ref[:, first_state + 2 * states :] = step_sum[:, : proj - first_state - 2 * states]
        taps_ref[:, inner_all : inner_all + states] = shared[:taps_count, inner:]
        bias_ref[:, inner_all : inner_all + states] = shared[taps_count : taps_count + 1, inner:]
        for tap in range(taps_count):
            taps_ref[tap : tap + 1, inner_all + states :] = shared[10:11, tap * states : (tap + 1) * states]
        bias_ref[:, inner_all + states :] = shared[11:12, :states]
        wide = inner + states
        for part in range(3):
            lanes = slice(part * wide, (part + 1) * wide)
            pre_ref[:, lanes] = shared[7 + part : 8 + part] / divisor_ref[:, lanes]
        head_ref[0:1, :] = dt_sum
        head_ref[1:2, :] = alog_sum
        head_ref[2:3, :] = skip_sum

    shapes = [(rows, proj), (rows, inner_all), taps_shape, (1, taps_shape[1]), (1, inner_all), (1, model), (8, LANES)]
    return pl.pallas_call(
        lambda early_ref, ref, divisor_ref, *refs: blocks(early_ref, ref, divisor_ref, refs[len(waits) :]),
        in_specs=[pl.BlockSpec(array.shape, lambda: (0, 0, 0)) for array in (early, owned)]
        + [pl.BlockSpec(gain.shape, lambda: (0, 0))]
        + [pl.BlockSpec(memory_space=pl.ANY)] * len(waits),
        out_shape=[jax.ShapeDtypeStruct(shape, jnp.float32) for shape in shapes],
        compiler_params=pltpu.CompilerParams(vmem_limit_bytes=24 << 20),
        cost_estimate=pl.CostEstimate(flops=int(3e9), bytes_accessed=1 << 20, transcendentals=0),
    )(early, owned, gain, *waits)


def pack_weights(in_weight, out_weight, ranks, heads):
    rows, inner_all = out_weight.shape
    inner = inner_all // ranks
    first_step = in_weight.shape[1] - ranks * heads
    states = (first_step - 2 * inner_all) // 2

    def run(in_ref, weight_ref, conv_ref, late_ref):
        steps = in_ref[:, first_step:].astype(jnp.float32)
        steps = jnp.concatenate([steps, jnp.zeros((rows, LANES - steps.shape[1]), jnp.float32)], axis=1)
        lane = lax.broadcasted_iota(jnp.int32, (rows, LANES), 1)
        for rank in range(ranks):
            own = slice(rank * inner, (rank + 1) * inner)
            late_ref[rank, :, :inner] = in_ref[:, own]
            late_ref[rank, :, inner:] = weight_ref[:, own]
            conv_ref[rank, :, :inner] = in_ref[:, inner_all + rank * inner : inner_all + (rank + 1) * inner]
            state = 2 * inner_all + (rank % 2) * states
            conv_ref[rank, :, inner : inner + states] = in_ref[:, state : state + states]
            moved = pltpu.roll(steps, (LANES - rank * heads) % LANES, 1)
            conv_ref[rank, :, inner + states :] = jnp.where(lane < heads, moved, 0.0).astype(LOW)

    return pl.pallas_call(
        run,
        out_shape=[
            jax.ShapeDtypeStruct((ranks, rows, inner + states + LANES), LOW),
            jax.ShapeDtypeStruct((ranks, rows, 2 * inner), LOW),
        ],
        cost_estimate=pl.CostEstimate(flops=int(1e9), bytes_accessed=1 << 20, transcendentals=0),
    )(in_weight, out_weight)


def pack_steps(value, start, width):
    rows = value.shape[0]

    def run(value_ref, out_ref):
        out_ref[:rows, :] = value_ref[:, start : start + width]
        steps = value_ref[:, start + width : start + width + LANES].astype(jnp.float32)
        out_ref[rows:, :rows] = steps.T[:16].astype(LOW)
        out_ref[rows:, rows:] = jnp.zeros((16, width - rows), LOW)

    return pl.pallas_call(
        run,
        out_shape=jax.ShapeDtypeStruct((rows + 16, width), LOW),
        cost_estimate=pl.CostEstimate(flops=int(1e9), bytes_accessed=1 << 20, transcendentals=0),
    )(value)


def add_states(pieces, states, start):
    count = len(pieces)
    rows, width = states.shape[0] // count, states.shape[1]

    def run(*refs):
        for index in range(count):
            own = refs[index][...].astype(jnp.float32)
            other = refs[count][index * rows : (index + 1) * rows, :].astype(jnp.float32)
            refs[count + 1 + index][...] = (own + other).astype(LOW)

    block = pl.BlockSpec((rows, width), lambda _: (0, start // width))
    return pl.pallas_call(
        run,
        grid=(1,),
        in_specs=[block] * count + [pl.BlockSpec(states.shape, lambda _: (0, 0))],
        out_specs=[block] * count,
        out_shape=[jax.ShapeDtypeStruct(piece.shape, piece.dtype) for piece in pieces],
        input_output_aliases={index: index for index in range(count)},
        cost_estimate=pl.CostEstimate(flops=int(1e9), bytes_accessed=1 << 20, transcendentals=0),
    )(*pieces, states)


def columns_of(value, start, width, waits):
    return pl.pallas_call(
        copy_kernel,
        grid=(1,),
        in_specs=[
            pl.BlockSpec((value.shape[0], LANES * (width // LANES)), lambda _: (0, start // width))
        ]
        + [pl.BlockSpec(memory_space=pl.ANY)] * len(waits),
        out_specs=pl.BlockSpec((value.shape[0], width), lambda _: (0, 0)),
        out_shape=jax.ShapeDtypeStruct((value.shape[0], width), LOW),
        cost_estimate=pl.CostEstimate(flops=int(1e9), bytes_accessed=1 << 20, transcendentals=0),
    )(value, *waits)


def body(
    sizes,
    hidden_in,
    lengths,
    cotangent,
    pre_gain,
    in_weight,
    conv_weight,
    conv_bias,
    dt_bias,
    a_log,
    skip,
    inner_gain,
    out_weight,
):
    length, model = hidden_in.shape
    rows = in_weight.shape[0]
    inner_all = out_weight.shape[1]
    heads_all = dt_bias.shape[0]
    states = (conv_weight.shape[1] - inner_all) // 2
    ranks = sizes["xi"] * sizes["yi"] * sizes["c"]
    lines = sizes["xo"] * sizes["zo"]
    slots = ranks
    tokens = slots * length
    inner = inner_all // ranks
    heads = heads_all // ranks
    head_width = inner // heads
    core = lax.axis_index("c")
    rank = (lax.axis_index("xi") * sizes["yi"] + lax.axis_index("yi")) * sizes["c"] + core
    direct = sizes["xo"] == 1 and sizes["zo"] == 4
    piece_rows = model // 4
    chunk = piece_rows // 2
    spread = (sizes["xo"], sizes["zo"], sizes["xi"], sizes["yi"] * sizes["c"] * rows)
    natural = (sizes["xo"], sizes["xi"], sizes["zo"], sizes["yi"] * sizes["c"] * rows)
    if direct:
        planes = [lax.axis_index("zo") ^ away for away in range(4)]
        starts = [half * (model // 2) + plane * chunk for plane in planes for half in range(2)]
    else:
        starts = [chunk * index for index in range(8)]
    place = jnp.stack([jnp.asarray(value, jnp.int32) for value in (*starts, core)])

    def gather_rows(piece):
        if direct:
            return [piece] + [cross(piece, LINE, away, 4) for away in range(1, 4)]
        whole = lax.all_gather(piece, LINE, axis=0, tiled=True).reshape(*spread, -1)
        whole = whole.transpose(0, 2, 1, 3, 4).reshape(model, -1)
        return [whole[index * piece_rows : (index + 1) * piece_rows] for index in range(4)]

    def scatter_rows(pieces):
        whole = jnp.concatenate(pieces, axis=0).reshape(*natural, -1)
        whole = whole.transpose(0, 2, 1, 3, 4).reshape(model, -1)
        moved = lax.all_to_all(whole, LINE, split_axis=0, concat_axis=0, tiled=True)
        return jnp.sum(moved.reshape(lines, model // lines, -1).astype(jnp.float32), axis=0).astype(LOW)

    def exchange(value):
        return lax.all_to_all(value, PLANE, split_axis=0, concat_axis=0, tiled=True)

    def gather_tokens(value):
        return lax.all_gather(value, PLANE, axis=0, tiled=True)

    def scatter_far(value):
        return lax.psum_scatter(value, PLANE, scatter_dimension=0, tiled=True)

    packed_conv, packed_late = pack_weights(in_weight, out_weight, ranks, heads)
    conv_plane = exchange(packed_conv).reshape(ranks * rows, -1)
    (late_packed,) = hold([packed_late], [conv_plane])
    late_plane = exchange(late_packed).reshape(ranks * rows, -1)
    if direct:
        conv_pieces = gather_rows(pack_steps(conv_plane, 0, inner + states))
    else:
        conv_pieces = [pack_steps(piece, 0, inner + states) for piece in gather_rows(conv_plane)]
    other_states = swap(
        jnp.concatenate([piece[:piece_rows, inner : inner + states] for piece in conv_pieces], axis=0)
    )
    (late_columns,) = hold([late_plane], conv_pieces[1:2])
    late_pieces = gather_rows(late_columns)

    stream = hidden_in.astype(jnp.float32)
    valid = (jnp.arange(length) < lengths[0])[:, None]
    own_normed = copies(norm_kernel, (), hidden_in, (pre_gain[None],), 1, (conv_plane,))
    normed = gather_tokens(own_normed)
    own_masked = copies(mask_kernel, (lengths,), cotangent, (), 1, (own_normed,))
    upstream = gather_tokens(own_masked)

    def of_rank(value, count):
        return lax.dynamic_slice_in_dim(value, rank * count, count, axis=-1)

    taps = jnp.concatenate(
        [of_rank(conv_weight[:, :inner_all], inner), conv_weight[:, inner_all:]], axis=1
    )
    bias = jnp.concatenate([of_rank(conv_bias[:inner_all], inner), conv_bias[inner_all:]])[None]
    dt_row = jnp.pad(of_rank(dt_bias, heads), (0, LANES - heads))[None]
    alog_row = jnp.pad(of_rank(a_log, heads), (0, LANES - heads))[None]
    skip_row = jnp.repeat(of_rank(skip, heads), head_width)[None]
    gain_row = of_rank(inner_gain, inner)[None]
    params = (taps, bias, dt_row, alog_row, skip_row)
    part_width = inner + 2 * states + LANES

    part, scanned, conv_weights = run_slots(
        functools.partial(conv_kernel, heads),
        slots,
        place,
        (normed,),
        (*conv_pieces, other_states, *params),
        [
            ((tokens, part_width), jnp.float32, row_block(length, part_width)),
            ((tokens, inner), jnp.float32, row_block(length, inner)),
            ((model, part_width), LOW, whole_block((model, part_width))),
        ],
        [],
        12,
    )
    gate, grad_mixed, branch, stats, gate_weights = run_slots(
        gate_kernel,
        slots // 2,
        place,
        (normed, upstream, scanned),
        (*late_pieces, gain_row),
        [
            ((tokens, inner), jnp.float32, row_block(2 * length, inner)),
            ((tokens, inner), jnp.float32, row_block(2 * length, inner)),
            ((tokens, model), LOW, row_block(2 * length, model)),
            ((2 * slots, length), jnp.float32, whole_block((2 * slots, length))),
            ((model, inner), LOW, whole_block((model, inner))),
        ],
        [pltpu.VMEM((model, inner), LOW)],
        14,
    )
    stats = stats + swap(stats)
    far = [cross(stats, ("xi", "yi"), away, 4) for away in (3, 1, 2)]
    stats = (stats + far[0]) + (far[1] + far[2])
    branch_own = scatter_far(branch)
    squares = lax.dynamic_index_in_dim(stats, rank, axis=0, keepdims=False)
    inner_scale = lax.rsqrt(squares / inner_all + EPSILON)[:, None]
    output = jnp.where(valid, stream + branch_own * inner_scale, 0.0).astype(LOW)

    piece_shape = (piece_rows, 2 * inner)
    grad_gate, grad_scanned, gain_grad, *early = run_slots(
        functools.partial(early_kernel, inner_all),
        slots // 2,
        place,
        (normed, upstream, scanned, gate, grad_mixed),
        (stats, gain_row),
        [
            ((tokens, inner), LOW, row_block(2 * length, inner)),
            ((tokens, inner), jnp.float32, row_block(2 * length, inner)),
            ((8, inner), jnp.float32, whole_block((8, inner))),
        ]
        + [(piece_shape, LOW, whole_block(piece_shape))] * 4,
        [pltpu.VMEM((model, 2 * inner), jnp.float32)],
        16,
    )
    width = taps.shape[1]
    piece_shape = (piece_rows + 48, inner + states)
    held = run_slots(
        functools.partial(back_kernel, heads),
        slots,
        place,
        (part, grad_scanned, scanned, grad_gate, normed),
        (conv_weights, gate_weights, *params, gain_grad),
        [
            ((tokens, model), LOW, late_block(length, model)),
            ((model, states), LOW, whole_block((model, states))),
        ]
        + [(piece_shape, LOW, whole_block(piece_shape))] * 4,
        [
            pltpu.VMEM((model, part_width), jnp.float32),
            pltpu.VMEM((length, part_width), LOW),
            pltpu.VMEM((length, part_width), LOW),
            pltpu.VMEM((8, part_width), jnp.float32),
            pltpu.VMEM((8, model), jnp.float32),
            pltpu.VMEM((16, inner + states), jnp.float32),
        ],
        30,
        specs=[early_block(slots)] * 3 + [late_block] * 2,
    )
    if direct:
        early_moved = [cross(early[away], LINE, away, 4) for away in (2, 3, 1)]
        held = hold(held, [*early_moved, branch_own])
    grad_normed, given, *pieces = held
    pieces = add_states(pieces, swap(given), inner)
    if direct:
        conv_moved = [cross(pieces[away], LINE, away, 4) for away in (1, 2, 3)]
    else:
        conv_moved = []
    grad_hidden = hidden_gradient(scatter_far(grad_normed), hidden_in, own_masked, pre_gain[None])

    if direct:
        early_owned = exchange(side_sums([early[0], *early_moved], ranks, False, pieces[:1]))
        owned = exchange(side_sums([pieces[0], *conv_moved], ranks, True, (early_owned,)))
    else:
        below = jnp.concatenate(parts_of(lax.psum(small_rows(pieces[0][piece_rows + 16 :]), LINE), 2), axis=0)
        below = jnp.pad(jnp.broadcast_to(below[None], (ranks, *below.shape)), ((0, 0), (0, 0), (0, LANES)))

        def padded(value):
            return jnp.pad(value.reshape(ranks, rows, -1), ((0, 0), (0, -rows % 16), (0, 0)))

        def with_steps(piece):
            steps = piece[piece_rows : piece_rows + 16, :piece_rows].T
            return jnp.concatenate([piece[:piece_rows], jnp.pad(steps, ((0, 0), (0, LANES - 16)))], axis=1)

        early_owned = exchange(padded(scatter_rows(early)))
        conv = padded(scatter_rows([with_steps(piece) for piece in pieces]))
        owned = exchange(jnp.concatenate([conv, below], axis=1))
    sizes_out = (in_weight.shape[1], inner_all, conv_weight.shape, model)
    owned_in, owned_out, taps_grad, bias_grad, gain_grads, pre_grad, head_grads = owner_outputs(
        early_owned, owned, pre_gain[None], rows + -rows % 16, heads, states, sizes_out, (output,)
    )
    return (
        output,
        grad_hidden,
        pre_grad[0],
        owned_in[:rows],
        taps_grad,
        bias_grad[0],
        head_grads[0, :heads_all],
        head_grads[1, :heads_all],
        head_grads[2, :heads_all],
        gain_grads[0],
        owned_out[:rows],
    )


def solution(mesh):
    dp, fsdp = mesh.shape["dp"], mesh.shape["fsdp"]
    shape = (dp // 2, 2, fsdp // 4, 2, 2)
    fine = Mesh(mesh.devices.reshape(shape), EVERY)
    split, kept = P(EVERY, None), P()
    in_specs = (split, P(EVERY), split, kept, split, kept, kept, kept, kept, kept, kept, split)
    out_specs = (split, split, kept, split, kept, kept, kept, kept, kept, kept, split)
    return jax.shard_map(
        functools.partial(body, dict(zip(EVERY, shape))),
        mesh=fine,
        in_specs=in_specs,
        out_specs=out_specs,
        check_vma=False,
    )
```
